32 devices in a mesh: dp: 8 (over y, x, core), tensor: 4 (over z).
Axes of the slice: x: 2, y: 2, z: 4, core: 2. Of those that a mesh axis runs over, the one named last changes fastest.
Arguments:
- block_input: bfloat16 [8192, 768], P(('dp', 'tensor')), may hold values from -6 to 6
- w_qkv: bfloat16 [2, 768, 3, 768], P(None, None, None, 'tensor'), may hold values from -0.3125 to 0.3125
- qv_bias: float32 [2, 2, 768], P(None, None, 'tensor'), may hold values from -4 to 4
- w_out: bfloat16 [2, 768, 768], P(None, 'tensor'), may hold values from -0.875 to 0.875
- out_bias: float32 [2, 2, 768], replicated, may hold values from -4 to 4
- w_up: bfloat16 [2, 768, 3072], P(None, None, 'tensor'), may hold values from -0.21875 to 0.21875
- up_bias: float32 [2, 3072], P(None, 'tensor'), may hold values from -4 to 4
- w_down: bfloat16 [2, 3072, 768], P(None, 'tensor'), may hold values from -0.109375 to 0.109375
- norm_gain: float32 [2, 2, 768], replicated, may hold values from 0.1 to 1.9
- norm_shift: float32 [2, 2, 768], replicated, may hold values from -4 to 4
- segment_ids: int32 [16, 512], P('dp'), may hold values from 0 to 3, never falling along the last dimension, each value on 1 to 256 neighbouring positions
- slot_counts: int32 [16], P('dp'), may hold values from 256 to 512
- cotangent: bfloat16 [8192, 768], P(('dp', 'tensor')), may hold values from -6 to 6
Outputs:
- mixed: bfloat16 [8192, 768], P(('dp', 'tensor'))
- input_grad: float32 [8192, 768], P(('dp', 'tensor'))
- grad_qkv: float32 [2, 768, 3, 768], P(None, None, None, 'tensor')
- grad_qv_bias: float32 [2, 2, 768], P(None, None, 'tensor')
- grad_out: float32 [2, 768, 768], P(None, 'tensor')
- grad_out_bias: float32 [2, 2, 768], replicated
- grad_up: float32 [2, 768, 3072], P(None, None, 'tensor')
- grad_up_bias: float32 [2, 3072], P(None, 'tensor')
- grad_down: float32 [2, 3072, 768], P(None, 'tensor')
- grad_gain: float32 [2, 2, 768], replicated
- grad_shift: float32 [2, 2, 768], replicated
The draws below stay inside these ranges and needn't reach their ends.
All inputs are finite; a program needn't handle non-finite values.
Results may differ from the reference program's by a relative error of at most 0.04.
The reference program's roundings to bfloat16 on the way count: a program that leaves them out, or rounds other values in their place, can miss the bound.
Values may be sent and summed in bfloat16 or wider, within the bound.
No kernel may reach another device: no remote copies, remote signals or barrier semaphores. Data moves between devices by JAX's collectives and lax.ppermute only.
A program may use at most 128 MiB of HBM per device.

```python
import math
import jax
import jax.numpy as jnp
import numpy as np
from jax import lax

D = 768
HEADS = 12
HEAD_DIM = 64
FF = 3072
LAYERS = 2
SEQ = 512
SEQS = 16
TOKENS = 8192


def place_ends(drawn, stream_key, least, high):
    place = [jax.random.randint(jax.random.fold_in(stream_key, axis), (), 0, length) for axis, length in enumerate(drawn.shape)]
    longest = drawn.shape.index(max(drawn.shape))
    next_to = place[:longest] + [(place[longest] + 1) % drawn.shape[longest]] + place[longest + 1:]
    return drawn.at[tuple(place)].set(least).at[tuple(next_to)].set(high)


def shard_levels(rng, shape, split, smallest, largest):
    def one(dim, shards_of):
        draws = jax.random.uniform(jax.random.fold_in(jax.random.fold_in(rng, 6), dim), (shards_of,), jnp.float32, smallest / len(split), largest / len(split))
        return jnp.repeat(jnp.exp(draws), shape[dim] // shards_of).reshape((-1,) + (1,) * (len(shape) - dim - 1))

    level = one(*split[0])
    for cut in split[1:]:
        level = level * one(*cut)
    return level


def profile(amount, total, most, skew):
    portions = [(1 << 20) // math.isqrt(standing ** skew) + 1 for standing in range(2, amount + 1)]
    surplus, counts = total - most - (amount - 1), [1] * (amount - 1)
    while surplus > 0:
        movable = [i for i in range(amount - 1) if counts[i] < most]
        mass, budget = sum([portions[i] for i in movable]), surplus
        for i in movable:
            addition = min(most - counts[i], max(1, budget * portions[i] // mass), surplus)
            counts[i] = counts[i] + addition
            surplus = surplus - addition
    return np.array([most] + counts)


def uneven_parts(key, number_of, total, limit, lean):
    if number_of == 2:
        one = jax.random.randint(key, (), max(1, total - limit), min(limit, total - 1) + 1)
        return jnp.stack([one, total - one])
    sizes = jnp.asarray(profile(number_of, total, limit, lean), jnp.int32)
    pairs = (number_of - 1) // 2
    source_of, receiver = sizes[1:1 + 2 * pairs:2], sizes[2:2 + 2 * pairs:2]
    margin = jnp.minimum(source_of - 1, limit - receiver)
    shifted = jax.random.randint(jax.random.fold_in(key, 1), (pairs,), 0, 1 << 20) % (margin + 1)
    sizes = sizes.at[1:1 + 2 * pairs:2].set(source_of - shifted).at[2:2 + 2 * pairs:2].set(receiver + shifted)
    return sizes[jax.random.permutation(jax.random.fold_in(key, 2), number_of)]


def normal_values(key, shape, width, limit, shards=(), dtype=jnp.bfloat16):
    loudness = shard_levels(key, shape, shards, -0.22, 0.18) if shards else 1.0
    array = jax.random.normal(key, shape, jnp.float32) * width * loudness
    return jnp.minimum(jnp.maximum(array, -limit), limit).astype(dtype)


def setup_inputs(seed: int = 0) -> dict:
    arg_keys = jax.random.split(jax.random.key(seed), 14)
    block_input = normal_values(arg_keys[0], (TOKENS, D), 1.0, 6.0, ((0, 32),))
    w_qkv = normal_values(arg_keys[1], (LAYERS, D, 3, D), (D // 2) ** -0.5, 0.3125, ((3, 4),))
    qv_bias = normal_values(arg_keys[2], (LAYERS, 2, D), 0.3, 4.0, ((2, 4),), jnp.float32)
    w_out = normal_values(arg_keys[3], (LAYERS, D, D), (D // 16) ** -0.5, 0.875, ((1, 4),))
    out_bias = normal_values(arg_keys[4], (LAYERS, 2, D), 0.3, 4.0, (), jnp.float32)
    w_up = normal_values(arg_keys[5], (LAYERS, D, FF), D ** -0.5, 0.21875, ((2, 4),))
    up_bias = normal_values(arg_keys[6], (LAYERS, FF), 0.3, 4.0, ((1, 4),), jnp.float32)
    w_down = normal_values(arg_keys[7], (LAYERS, FF, D), FF ** -0.5, 0.109375, ((1, 4),))
    norm_gain = jnp.clip(1.0 + 0.18 * jax.random.normal(arg_keys[8], (LAYERS, 2, D), jnp.float32), 0.1, 1.9)
    norm_shift = normal_values(arg_keys[9], (LAYERS, 2, D), 0.3, 4.0, (), jnp.float32)
    segment_ids = jax.vmap(lambda own: jnp.searchsorted(jnp.cumsum(uneven_parts(own, 4, SEQ, SEQ // 2, 0)), jnp.arange(SEQ), side="right"))(jax.random.split(arg_keys[10], SEQS)).reshape((SEQS, SEQ)).astype(jnp.int32)
    slot_counts = place_ends(jax.random.randint(arg_keys[11], (SEQS,), SEQ // 2, SEQ + 1), jax.random.fold_in(arg_keys[11], 1), SEQ // 2, SEQ).astype(jnp.int32)
    cotangent = normal_values(arg_keys[12], (TOKENS, D), 1.0, 6.0, ((0, 32),))
    return dict(block_input=block_input, w_qkv=w_qkv, qv_bias=qv_bias, w_out=w_out, out_bias=out_bias, w_up=w_up, up_bias=up_bias, w_down=w_down, norm_gain=norm_gain, norm_shift=norm_shift, segment_ids=segment_ids, slot_counts=slot_counts, cotangent=cotangent)


epsilon = 1e-06
masked_fill = -1e+30
highest = lax.Precision.HIGHEST

@jax.custom_vjp
def low(v):
    return lax.optimization_barrier(v.astype(jnp.bfloat16)).astype(jnp.float32)

@jax.custom_vjp
def low_back(v):
    return v

def low_keep(v):
    return (low(v), None)

def low_pass(kept, grad):
    return (grad,)

def back_keep(v):
    return (v, None)

def back_low(kept, grad):
    return (low(grad),)
low.defvjp(low_keep, low_pass)
low_back.defvjp(back_keep, back_low)

def allowed(segments, slot_count):
    places = lax.broadcasted_iota(jnp.int32, (segments.shape[0],), 0)
    filled = places < slot_count
    same = segments[:, None] == segments[None, :]
    return same & (filled[None, :] | jnp.logical_not(filled)[:, None])

def layer_norm(summed, gain, shift):
    center = summed - lax.optimization_barrier(jnp.mean(summed, -1, keepdims=True))
    recip = lax.rsqrt(lax.optimization_barrier(jnp.mean(center * center, -1, keepdims=True)) + epsilon)
    return center * recip * gain + shift

def one_sequence(queries, key_rows, value_rows, segments, slot_count):
    visible = allowed(segments, slot_count)
    raw_scores = jnp.einsum('qhd,khd->hqk', queries, key_rows, precision=highest) * (1.0 / math.sqrt(HEAD_DIM))
    scores = low_back(raw_scores)
    weights = low(jax.nn.softmax(jnp.where(visible[None], scores, masked_fill), axis=-1))
    return jnp.einsum('hqk,khd->qhd', weights, value_rows, precision=highest)

def forward(rows, w_qkv, qv_bias, w_out, out_bias, w_up, up_bias, w_down, norm_gain, norm_shift, segments, slot_counts):
    group = segments.shape[0]
    checked = jax.checkpoint(one_sequence)

    def mapped(packed):
        return checked(packed[0], packed[1], packed[2], packed[3], packed[4])
    state = rows
    for depth in range(LAYERS):
        entered = low(state)
        projected = jnp.dot(entered, w_qkv[depth].reshape(D, 3 * D), precision=highest).reshape(-1, 3, D)
        queries = low(low_back(projected[:, 0] + qv_bias[depth, 0]))
        key_rows = low(low_back(projected[:, 1]))
        value_rows = low(low_back(projected[:, 2] + qv_bias[depth, 1]))
        shaped = (group, SEQ, HEADS, HEAD_DIM)
        attended = lax.map(mapped, (queries.reshape(shaped), key_rows.reshape(shaped), value_rows.reshape(shaped), segments, slot_counts))
        attended = low(low_back(attended.reshape(-1, D)))
        branch = low_back(jnp.dot(attended, w_out[depth], precision=highest))
        middle = layer_norm(state + branch + out_bias[depth, 0], norm_gain[depth, 0], norm_shift[depth, 0])
        hidden_in = low(middle)
        upward = low_back(jnp.dot(hidden_in, w_up[depth], precision=highest) + up_bias[depth])
        activated = low(jax.nn.gelu(upward, approximate=False))
        downward = low_back(jnp.dot(activated, w_down[depth], precision=highest))
        state = layer_norm(middle + downward + out_bias[depth, 1], norm_gain[depth, 1], norm_shift[depth, 1])
    return state

def reference(block_input, w_qkv, qv_bias, w_out, out_bias, w_up, up_bias, w_down, norm_gain, norm_shift, segment_ids, slot_counts, cotangent):
    params = tuple((entry.astype(jnp.float32) for entry in (w_qkv, qv_bias, w_out, out_bias, w_up, up_bias, w_down, norm_gain, norm_shift)))
    group = 8
    step_count = SEQS // group
    inputs = block_input.astype(jnp.float32).reshape(step_count, group * SEQ, D)
    cotans = cotangent.astype(jnp.float32).reshape(step_count, group * SEQ, D)
    segment_groups = segment_ids.reshape(step_count, group, SEQ)
    count_groups = slot_counts.reshape(step_count, group)

    def step(summed, packed):
        rows, cotan_rows, segments, slot_group = packed

        def closed(rows_in, *weights):
            return forward(rows_in, *weights, segments, slot_group)
        result, pull = jax.vjp(closed, rows, *params)
        pulled = pull(cotan_rows)
        summed = tuple((total_sum + fresh for total_sum, fresh in zip(summed, pulled[1:])))
        return (summed, (result.astype(jnp.bfloat16), pulled[0]))
    zeros = tuple((jnp.zeros_like(entry) for entry in params))
    summed, (results, input_grads) = lax.scan(step, zeros, (inputs, cotans, segment_groups, count_groups))
    mixed = results.reshape(TOKENS, D)
    input_grad = input_grads.reshape(TOKENS, D)
    return (mixed, input_grad, summed[0], summed[1], summed[2], summed[3], summed[4], summed[5], summed[6], summed[7], summed[8])
```

```python
from functools import partial
import math

import jax
import jax.numpy as jnp
from jax import lax
from jax.sharding import PartitionSpec as P

HEAD_DIM = 64
epsilon = 1e-06
masked_fill = -1e30
bf16 = jnp.bfloat16
f32 = jnp.float32


def dot_nn(left, right):
    return lax.dot_general(left, right, (((1,), (0,)), ((), ())), preferred_element_type=f32)


def dot_nt(left, right):
    return lax.dot_general(left, right, (((1,), (1,)), ((), ())), preferred_element_type=f32)


def dot_tn(left, right):
    return lax.dot_general(left, right, (((0,), (0,)), ((), ())), preferred_element_type=f32)


def norm_forward(summed, gain, shift):
    center = summed - jnp.mean(summed, -1, keepdims=True)
    recip = lax.rsqrt(jnp.mean(center * center, -1, keepdims=True) + epsilon)
    normed = center * recip
    return normed * gain + shift, normed, recip


def norm_backward(grad_rows, normed, recip, gain):
    scaled = grad_rows * gain
    first_mean = jnp.mean(scaled, -1, keepdims=True)
    second_mean = jnp.mean(scaled * normed, -1, keepdims=True)
    grad_in = recip * (scaled - first_mean - normed * second_mean)
    return grad_in, jnp.sum(grad_rows * normed, 0), jnp.sum(grad_rows, 0)


def allowed(segments, slot_count):
    places = lax.broadcasted_iota(jnp.int32, (segments.shape[0],), 0)
    filled = places < slot_count
    same = segments[:, None] == segments[None, :]
    return same & (filled[None, :] | jnp.logical_not(filled)[:, None])


def attend(queries, key_rows, value_rows, visible, scale):
    scores = jnp.einsum("qhd,khd->hqk", queries, key_rows, preferred_element_type=f32) * scale
    scores = jnp.where(visible[None], scores, masked_fill)
    row_max = jnp.max(scores, -1, keepdims=True)
    exponent = jnp.exp(scores - row_max)
    denom = jnp.sum(exponent, -1, keepdims=True)
    weights = (exponent / denom).astype(bf16)
    result = jnp.einsum("hqk,khd->qhd", weights, value_rows, preferred_element_type=f32)
    return result.astype(bf16), row_max + jnp.log(denom)


def attend_back(queries, key_rows, value_rows, visible, log_total, grad_result, scale):
    scores = jnp.einsum("qhd,khd->hqk", queries, key_rows, preferred_element_type=f32) * scale
    scores = jnp.where(visible[None], scores, masked_fill)
    weights = jnp.exp(scores - log_total)
    weights_low = weights.astype(bf16)
    grad_values = jnp.einsum("hqk,qhd->khd", weights_low, grad_result, preferred_element_type=f32)
    grad_weights = jnp.einsum("qhd,khd->hqk", grad_result, value_rows, preferred_element_type=f32)
    grad_scores = weights * (grad_weights - jnp.sum(weights * grad_weights, -1, keepdims=True))
    low = grad_scores.astype(bf16)
    grad_queries = jnp.einsum("hqk,khd->qhd", low, key_rows, preferred_element_type=f32) * scale
    grad_keys = jnp.einsum("hqk,qhd->khd", low, queries, preferred_element_type=f32) * scale
    return grad_queries, grad_keys, grad_values


def local(
    block_input,
    w_qkv,
    qv_bias,
    w_out,
    out_bias,
    w_up,
    up_bias,
    w_down,
    norm_gain,
    norm_shift,
    segment_ids,
    slot_counts,
    cotangent,
):
    layers, width, _, cols = w_qkv.shape
    hidden = w_up.shape[2]
    seq_len = segment_ids.shape[1]
    n_dp, n_t = lax.axis_size("dp"), lax.axis_size("tensor")
    dp, z = lax.axis_index("dp"), lax.axis_index("tensor")
    core, place = dp & 1, (dp >> 1) & 3
    first = core == 0
    scale = 1.0 / math.sqrt(HEAD_DIM)
    half = cols // 2
    heads = n_t // 2 * cols // HEAD_DIM
    part = hidden // 8

    def flip(v, bit):
        return lax.ppermute(v, "dp", [(i, i ^ (1 << bit)) for i in range(n_dp)])

    def across(v):
        return flip(v, 0)

    def rotate(v, by):
        return lax.ppermute(v, "tensor", [(i, (i + by) % n_t) for i in range(n_t)])

    def swap(v):
        pairs = []
        for i in range(n_dp):
            for k in range(n_t):
                if (i & 1) != (k & 1):
                    pairs.append((i * n_t + k, (i ^ 1) * n_t + (k ^ 1)))
        moved = lax.ppermute(v, ("dp", "tensor"), pairs)
        return jnp.where(core == (z & 1), v, moved)

    def in_core_order(mine, theirs, axis):
        return jnp.where(
            first,
            jnp.concatenate([mine, theirs], axis),
            jnp.concatenate([theirs, mine], axis),
        )

    def add_low(a, b):
        return (a.astype(f32) + b.astype(f32)).astype(bf16)

    def whole_rows(v):
        own = swap(v)
        return in_core_order(own, across(own), 0)

    x_low = whole_rows(block_input)
    seg_theirs, count_theirs = across(segment_ids), across(slot_counts)
    seg_sel = jnp.where(core == (z & 1), segment_ids, seg_theirs)
    count_sel = jnp.where(core == (z & 1), slot_counts, count_theirs)
    segments = lax.dynamic_index_in_dim(seg_sel, z >> 1, 0, False)
    slot_count = lax.dynamic_index_in_dim(count_sel, z >> 1, 0, False)
    visible = allowed(segments, slot_count)

    def gather_pieces(piece, split):
        rel = jnp.stack([rotate(piece, k) for k in range(1, n_t)])
        a, b = rel[:, :split], rel[:, split:]
        xa = flip(a, 1)
        yb = flip(b, 2)
        ya = flip(jnp.stack([a, xa]), 2)
        xb = flip(jnp.stack([b, yb]), 1)
        return (
            jnp.stack([a, xa, ya[0], ya[1]], 1),
            jnp.stack([b, xb[0], yb, xb[1]], 1),
        )

    attn_w, up_w, down_w = [], [], []
    for l in range(layers):
        own_attn = jnp.concatenate(
            [jnp.transpose(w_qkv[l], (1, 2, 0)), w_out[l][None]], 0
        )
        piece = lax.dynamic_index_in_dim(own_attn, place, 0, False)
        piece = lax.dynamic_slice_in_dim(piece, core * half, half, 0)
        a, b = gather_pieces(piece, half // 2)
        got = jnp.concatenate([a, b], 2)
        got = in_core_order(got, across(got), 2)
        order = jnp.arange(4) ^ place
        got = jnp.take(got, order, axis=1)
        attn_w.append(jnp.concatenate([own_attn[None], got], 0))

        order_ff = (jnp.arange(4) ^ place) * 2 + core
        own_up = w_up[l].T.reshape(8, part, width)
        own_down = w_down[l].reshape(8, part, width)
        own_up = jnp.take(own_up, order_ff, axis=0)
        own_down = jnp.take(own_down, order_ff, axis=0)
        a, b = gather_pieces(jnp.concatenate([own_up[0], own_down[0]], 0), part)
        up_w.append(jnp.concatenate([own_up[None], a], 0).reshape(-1, width))
        down_w.append(jnp.concatenate([own_down[None], b], 0).reshape(-1, width))

    small = jnp.concatenate([up_bias.reshape(-1), qv_bias.reshape(-1)])
    small = lax.all_gather(small, "tensor", axis=0)
    rel_quarter = (z - jnp.arange(n_t)) % n_t
    small = jnp.take(small, rel_quarter, axis=0)
    up_bias_all = small[:, : layers * hidden].reshape(n_t, layers, 8, part)
    up_bias_all = jnp.take(up_bias_all, (jnp.arange(4) ^ place) * 2 + core, axis=2)
    up_bias_all = jnp.transpose(up_bias_all, (1, 0, 2, 3)).reshape(layers, -1)
    qv_all = small[:, layers * hidden :].reshape(n_t, layers, 2, cols)
    qv_mine = lax.dynamic_slice_in_dim(qv_all, core * (n_t // 2), n_t // 2, 0)
    qv_mine = jnp.transpose(qv_mine, (1, 2, 0, 3)).reshape(layers, 2, -1)

    def my_heads(w):
        return lax.dynamic_slice_in_dim(w, core * (n_t // 2), n_t // 2, 0)

    def their_heads(w):
        return lax.dynamic_slice_in_dim(w, (1 - core) * (n_t // 2), n_t // 2, 0)

    state = x_low.astype(f32)
    saved = []
    for l in range(layers):
        mine = my_heads(attn_w[l])
        w3 = jnp.transpose(mine[:, :3], (1, 0, 2, 3)).reshape(-1, width)
        w_o = mine[:, 3].reshape(-1, width)
        w_o_theirs = their_heads(attn_w[l])[:, 3].reshape(-1, width)
        xr = state.astype(bf16)
        bias = jnp.concatenate([qv_mine[l, 0], jnp.zeros_like(qv_mine[l, 0]), qv_mine[l, 1]])
        qkv = (dot_nt(xr, w3) + bias).astype(bf16).reshape(seq_len, 3, heads, HEAD_DIM)
        o, lse = attend(qkv[:, 0], qkv[:, 1], qkv[:, 2], visible, scale)
        o = o.reshape(seq_len, -1)
        o_theirs = across(o)
        branch = dot_nn(o, w_o) + dot_nn(o_theirs, w_o_theirs)
        h, n1, r1 = norm_forward(state + branch + out_bias[l, 0], norm_gain[l, 0], norm_shift[l, 0])
        hr = h.astype(bf16)
        u = dot_nt(hr, up_w[l]) + up_bias_all[l]
        g = jax.nn.gelu(u, approximate=False).astype(bf16)
        f_part = dot_nn(g, down_w[l])
        f = f_part + across(f_part.astype(bf16)).astype(f32)
        new, n2, r2 = norm_forward(h + f + out_bias[l, 1], norm_gain[l, 1], norm_shift[l, 1])
        saved.append((xr, w3, w_o, qkv, o, lse, n1, r1, hr, u, g, n2, r2))
        state = new
    out_rows = lax.dynamic_slice_in_dim(state.astype(bf16), core * (seq_len // 2), seq_len // 2, 0)
    mixed = swap(out_rows)

    def reduce_pieces(a, b):
        ra = flip(a[:, 2:], 2)
        rb = flip(b[:, 1::2], 1)
        a = add_low(a[:, :2], ra)
        b = add_low(b[:, 0::2], rb)
        a1 = flip(a[:, 1], 1)
        b1 = flip(b[:, 1], 2)
        both = jnp.concatenate([add_low(a[:, 0], a1), add_low(b[:, 0], b1)], 1)
        total = both[0].astype(f32)
        for k in range(1, n_t):
            total = total + rotate(both[k], n_t - k).astype(f32)
        total = total.astype(bf16)
        bit = 3
        while (1 << bit) < n_dp:
            total = add_low(total, flip(total, bit))
            bit += 1
        rows = a.shape[2]
        a, b = total[:rows], total[rows:]
        xa = flip(a, 1)
        yb = flip(b, 2)
        ya = flip(jnp.stack([a, xa]), 2)
        xb = flip(jnp.stack([b, yb]), 1)
        return jnp.stack([a, xa, ya[0], ya[1]]), jnp.stack([b, xb[0], yb, xb[1]])

    order = jnp.arange(4) ^ place
    grads = []
    dy = whole_rows(cotangent).astype(f32)
    for l in reversed(range(layers)):
        xr, w3, w_o, qkv, o, lse, n1, r1, hr, u, g, n2, r2 = saved[l]
        dz2, gain2, shift2 = norm_backward(dy, n2, r2, norm_gain[l, 1])
        dzr2 = dz2.astype(bf16)
        dg = dot_nt(dzr2, down_w[l])
        _, pull = jax.vjp(partial(jax.nn.gelu, approximate=False), u)
        du = pull(dg)[0].astype(bf16)
        dh_part = dot_nn(du, up_w[l])
        dh = dz2 + dh_part + across(dh_part.astype(bf16)).astype(f32)
        g_down = dot_tn(g, dzr2).astype(bf16).reshape(n_t, 4, part, width)
        g_up = dot_tn(du, hr).astype(bf16).reshape(n_t, 4, part, width)
        g_up_bias = jnp.sum(du, 0, dtype=f32).reshape(n_t, 4, part)
        g_up, g_down = reduce_pieces(g_up, g_down)
        ff = jnp.stack([g_up, g_down])
        ff = in_core_order(ff[:, :, None], across(ff)[:, :, None], 2)
        ff = jnp.take(ff, order, axis=1).reshape(2, hidden, width).astype(f32)

        dz1, gain1, shift1 = norm_backward(dh, n1, r1, norm_gain[l, 0])
        dzr1 = dz1.astype(bf16)
        do = dot_nt(dzr1, w_o).astype(bf16).reshape(seq_len, heads, HEAD_DIM)
        d3 = attend_back(qkv[:, 0], qkv[:, 1], qkv[:, 2], visible, lse, do, scale)
        d3 = jnp.stack(d3, 1).astype(bf16).reshape(seq_len, -1)
        dx_part = dot_nn(d3, w3)
        dy = dz1 + dx_part + across(dx_part.astype(bf16)).astype(f32)
        g3 = dot_tn(d3, xr).astype(bf16).reshape(3, n_t // 2, 2, half, width)
        g_o = dot_tn(o, dzr1).astype(bf16).reshape(1, n_t // 2, 2, half, width)
        g_attn = jnp.transpose(jnp.concatenate([g3, g_o], 0), (2, 1, 0, 3, 4))
        keep = lax.dynamic_index_in_dim(g_attn, core, 0, False)
        give = lax.dynamic_index_in_dim(g_attn, 1 - core, 0, False)
        both = in_core_order(keep, across(give), 0)
        both = jnp.take(both, order, axis=1)
        a, b = reduce_pieces(both[:, :, : half // 2], both[:, :, half // 2 :])
        at = jnp.concatenate([a, b], 1)
        at = in_core_order(at, across(at), 1)
        at = jnp.take(at, order, axis=0).astype(f32)

        col = jnp.sum(d3, 0, dtype=f32).reshape(3, n_t // 2, cols)
        g_qv = jnp.stack([col[0], col[2]])
        grads.append((ff, at, g_up_bias, g_qv, gain1, gain2, shift1, shift2, jnp.sum(dz1, 0), jnp.sum(dz2, 0)))

    grads = grads[::-1]
    out_half = lax.dynamic_slice_in_dim(dy, core * (seq_len // 2), seq_len // 2, 0)
    input_grad = swap(out_half)

    once = jnp.where(first, 1.0, 0.0).astype(f32)
    norm_rows = jnp.stack([jnp.stack(g[4:]) for g in grads]) * once
    abs_quarter = (z - jnp.arange(n_t)) % n_t
    ub = jnp.stack([g[2] for g in grads])
    ub = jnp.take(jnp.take(ub, abs_quarter, axis=1), order, axis=2)
    zero = jnp.zeros_like(ub)
    ub = in_core_order(jnp.where(first, ub, ub)[:, :, :, None], zero[:, :, :, None], 3)
    qv = jnp.stack([g[3] for g in grads])
    qv = in_core_order(qv, jnp.zeros_like(qv), 2)
    qv = jnp.take(qv, abs_quarter, axis=2)
    flat = jnp.concatenate([norm_rows.reshape(-1), ub.reshape(-1), qv.reshape(-1)])
    flat = flat.reshape(-1, 128)
    bit = 0
    while (1 << bit) < n_dp:
        flat = flat + flip(flat, bit)
        bit += 1
    bit = 0
    while (1 << bit) < n_t:
        flat = flat + lax.ppermute(flat, "tensor", [(i, i ^ (1 << bit)) for i in range(n_t)])
        bit += 1
    flat = flat.reshape(-1)
    n0 = norm_rows.size
    norm_rows = flat[:n0].reshape(layers, 6, width)
    ub = flat[n0 : n0 + ub.size].reshape(layers, n_t, hidden)
    qv = flat[n0 + ub.size :].reshape(layers, 2, n_t, cols)
    grad_up_bias = lax.dynamic_index_in_dim(ub, z, 1, False)
    grad_qv_bias = lax.dynamic_index_in_dim(qv, z, 2, False)
    return (
        mixed,
        input_grad,
        jnp.stack([jnp.transpose(g[1][:3], (2, 0, 1)) for g in grads]),
        grad_qv_bias,
        jnp.stack([g[1][3] for g in grads]),
        norm_rows[:, 4:6],
        jnp.stack([g[0][0].T for g in grads]),
        grad_up_bias,
        jnp.stack([g[0][1] for g in grads]),
        norm_rows[:, 0:2],
        norm_rows[:, 2:4],
    )


def solution(mesh):
    placed = (
        P(("dp", "tensor"), None),
        P(None, None, None, "tensor"),
        P(None, None, "tensor"),
        P(None, "tensor", None),
        P(),
        P(None, None, "tensor"),
        P(None, "tensor"),
        P(None, "tensor", None),
        P(),
        P(),
        P("dp", None),
        P("dp"),
        P(("dp", "tensor"), None),
    )
    return jax.shard_map(
        local,
        mesh=mesh,
        in_specs=placed,
        out_specs=(
            P(("dp", "tensor"), None),
            P(("dp", "tensor"), None),
            P(None, None, None, "tensor"),
            P(None, None, "tensor"),
            P(None, "tensor", None),
            P(),
            P(None, None, "tensor"),
            P(None, "tensor"),
            P(None, "tensor", None),
            P(),
            P(),
        ),
        check_vma=False,
    )
```

```python
import functools
import math

import jax
import jax.numpy as jnp
from jax import lax
from jax.experimental import pallas as pl
from jax.experimental.pallas import tpu as pltpu
from jax.sharding import PartitionSpec as P

HEAD_DIM = 64
epsilon = 1e-06
masked_fill = -1e30
bf16 = jnp.bfloat16
f32 = jnp.float32
ANY = pl.BlockSpec(memory_space=pl.ANY)
SMEM = pl.BlockSpec(memory_space=pltpu.SMEM)
VMEM = pl.BlockSpec(memory_space=pltpu.VMEM)
ROOM = 56 * 1024 * 1024
SLOTS = 2


def dot_nn(left, right):
    return lax.dot_general(left, right, (((1,), (0,)), ((), ())), preferred_element_type=f32)


def dot_nt(left, right):
    return lax.dot_general(left, right, (((1,), (1,)), ((), ())), preferred_element_type=f32)


def dot_tn(left, right):
    return lax.dot_general(left, right, (((0,), (0,)), ((), ())), preferred_element_type=f32)


def norm_forward(summed, gain, shift):
    center = summed - jnp.mean(summed, -1, keepdims=True)
    recip = lax.rsqrt(jnp.mean(center * center, -1, keepdims=True) + epsilon)
    normed = center * recip
    return normed * gain + shift, normed, recip


def norm_backward(grad_rows, normed, recip, gain):
    scaled = grad_rows * gain
    first_mean = jnp.mean(scaled, -1, keepdims=True)
    second_mean = jnp.mean(scaled * normed, -1, keepdims=True)
    return recip * (scaled - first_mean - normed * second_mean)


def shape(dims, dtype):
    return jax.ShapeDtypeStruct(dims, dtype)


def params(**more):
    return pltpu.CompilerParams(vmem_limit_bytes=ROOM, **more)


def cost(us):
    return pl.CostEstimate(flops=int(us * 1.1e9), bytes_accessed=int(us * 3.6e6), transcendentals=0)


def lane_half(rows, which):
    lane = lax.broadcasted_iota(jnp.int32, (rows, 2 * HEAD_DIM), 1)
    return (lane < HEAD_DIM) if which == 0 else (lane >= HEAD_DIM)


def fetch_attn(scal, layer, own_qkv, own_out, a_refs, b_refs, w, sems):
    core, place = scal[0], scal[1]
    cols = own_out.shape[1]

    def b_copy(j):
        return pltpu.make_async_copy(b_refs[j].at[pl.ds(0, cols)], w.at[j ^ place, pl.ds(cols, cols)], sems.at[j])

    def a_copy(j):
        return pltpu.make_async_copy(a_refs[j].at[pl.ds(0, cols)], w.at[j ^ place, pl.ds(0, cols)], sems.at[4 + j])

    def own_copy(j):
        own = own_qkv.at[layer, j] if j < 3 else own_out.at[layer]
        return pltpu.make_async_copy(own, w.at[j, pl.ds(0, cols)], sems.at[4 + j])

    for j in range(4):
        b_copy(j).start()

    @pl.when(core == 0)
    def _():
        for j in range(4):
            own_copy(j).start()

    @pl.when(core != 0)
    def _():
        for j in range(4):
            a_copy(j).start()

    def wait():
        for j in range(4):
            b_copy(j).wait()
            own_copy(j).wait()

    return wait


def fetch_ff(scal, layer, own_up, own_down, moved, wu, wd, sems):
    core, place = scal[0], scal[1]
    n_t, width, half = wu.shape
    part, rows = width // 4, half // 4
    own, x, y, diag_up, diag_down = moved
    ups = [own.at[0], x.at[0], y.at[0], diag_up]
    downs = [own.at[1], x.at[1], y.at[1], diag_down]
    others = pl.ds(1, n_t - 1)
    copies = [
        pltpu.make_async_copy(own_up.at[layer, :, pl.ds(pl.multiple_of(core * half, half), half)], wu.at[0], sems.at[0]),
        pltpu.make_async_copy(own_down.at[layer, pl.ds(pl.multiple_of(core * half, half), half)], wd.at[0], sems.at[1]),
    ]
    for j in range(4):
        at = pl.ds(pl.multiple_of((j ^ place) * part, part), part)
        copies.append(pltpu.make_async_copy(ups[j], wu.at[others, at], sems.at[2 + 3 * j]))
        at = pl.ds(pl.multiple_of((j ^ place) * rows, rows), rows)
        for n in range(2):
            copies.append(
                pltpu.make_async_copy(
                    downs[j].at[:, pl.ds(n * rows, rows)],
                    wd.at[others, at, pl.ds(n * half, half)],
                    sems.at[3 + 3 * j + n],
                )
            )
    for c in copies:
        c.start()
    for c in copies:
        c.wait()


BIAS_ROWS = 16


def split_rows(v):
    parts = []
    for _ in range(3):
        low = v.astype(bf16)
        parts.append(low)
        v = v - low.astype(f32)
    n = sum(p.shape[0] for p in parts)
    return jnp.concatenate(parts + [jnp.zeros((BIAS_ROWS - n, v.shape[1]), bf16)], 0)


def pack_bias_kernel(scal, up_bias, qv_bias, out_up, out_qv):
    half = out_up.shape[2]
    for l in range(out_up.shape[0]):
        row = jnp.where(scal[0] == 0, up_bias[l : l + 1, :half], up_bias[l : l + 1, half:])
        out_up[l] = split_rows(row)
    out_qv[...] = split_rows(qv_bias[...])


def pack_bias(scal, up_bias, qv_bias):
    layers, hidden = up_bias.shape
    return pl.pallas_call(
        pack_bias_kernel,
        out_shape=[
            shape((layers, BIAS_ROWS, hidden // 2), bf16),
            shape((BIAS_ROWS, qv_bias.shape[1]), bf16),
        ],
        in_specs=[SMEM, VMEM, VMEM],
        out_specs=[VMEM, VMEM],
        compiler_params=params(),
        cost_estimate=cost(1),
        name="pack_bias",
    )(scal, up_bias, qv_bias)


def attn_fwd_kernel(layer, *refs):
    refs = list(refs)
    scal = refs.pop(0)
    first = layer == 0
    if first:
        x_mine, x_theirs = refs[:2]
        refs = refs[2:]
    else:
        h_in, f_mine, f_theirs, ob, gain, shift = refs[:6]
        refs = refs[6:]
    seg_row, seg_col = refs[:2]
    own_bias, a_bias, b_bias, own_qkv, own_out = refs[2:7]
    a_refs, b_refs = refs[7:11], refs[11:15]
    refs = refs[15:]
    state, xr = refs[:2]
    refs = refs[2:]
    if not first:
        normed, recip = refs[:2]
        refs = refs[2:]
    qkv, lse_t, o, a_low, w, mask, lse, packed, sems = refs
    cols = own_out.shape[1]
    bias_copies = [
        pltpu.make_async_copy(ref.at[pl.ds(cols, BIAS_ROWS)], packed.at[n], sems.at[8 + n])
        for n, ref in enumerate((a_bias, b_bias))
    ]
    for c in bias_copies:
        c.start()
    wait = fetch_attn(scal, layer, own_qkv, own_out, a_refs, b_refs, w, sems)
    core, slots = scal[0], scal[2]
    seq = xr.shape[0]
    half = seq // 2
    if first:
        mine = x_mine[...]
        theirs = x_theirs[...]
        at = pl.ds(pl.multiple_of(core * half, half), half)
        xr[at] = mine
        state[at] = mine.astype(f32)
        at = pl.ds(pl.multiple_of((1 - core) * half, half), half)
        xr[at] = theirs
        state[at] = theirs.astype(f32)
    else:
        @pl.loop(0, seq // 128)
        def _(i):
            at = pl.ds(pl.multiple_of(i * 128, 128), 128)
            z = h_in[at] + (f_mine[at].astype(f32) + f_theirs[at].astype(f32)) + ob[layer - 1, 1:2]
            new, n, r = norm_forward(z, gain[layer - 1, 1:2], shift[layer - 1, 1:2])
            state[at] = new
            xr[at] = new.astype(bf16)
            normed[at] = n
            recip[at] = r

    qi = lax.broadcasted_iota(jnp.int32, (seq, seq), 0)
    ki = lax.broadcasted_iota(jnp.int32, (seq, seq), 1)
    visible = (seg_col[...] == seg_row[...]) & ((ki < slots) | (qi >= slots))
    mask[...] = jnp.where(visible, 0.0, masked_fill)
    for c in bias_copies:
        c.wait()
    a_row, b_row = (jnp.sum(packed[n, 0:3].astype(f32), 0, keepdims=True) for n in range(2))
    a_row = jnp.where(core == 0, own_bias[...], a_row)
    qb = []
    for i in range(2):
        base = (2 * layer + i) * cols
        qb.append(jnp.concatenate([a_row[:, base : base + cols], b_row[:, base : base + cols]], 1))
    wait()
    rows = 256
    for t in range(3):
        for i in range(seq // rows):
            at = pl.ds(i * rows, rows)
            acc = dot_nt(xr[at], w[t])
            if t != 1:
                acc = acc + qb[t // 2]
            qkv[t, at] = acc.astype(bf16)
    pairs = qkv.shape[2] // 128
    tile = 128
    lane = lax.broadcasted_iota(jnp.int32, (tile, 128), 1)

    @pl.loop(0, seq // tile)
    def _(i):
        at = pl.ds(pl.multiple_of(i * tile, tile), tile)
        bias = mask[at]
        keep = jnp.zeros((tile, 128), f32)
        for g in range(pairs):
            cs = pl.ds(g * 128, 128)
            q2 = qkv[0, at, cs] * jnp.asarray(1.0 / math.sqrt(HEAD_DIM), bf16)
            k2 = qkv[1, :, cs]
            v2 = qkv[2, :, cs]
            acc = None
            for hh in range(2):
                qm = jnp.where(lane_half(tile, hh), q2, jnp.zeros_like(q2))
                s = dot_nt(qm, k2) + bias
                top = jnp.max(s, -1, keepdims=True)
                e = jnp.exp(s - top)
                d = jnp.sum(e, -1, keepdims=True)
                pr = (e * (1.0 / d)).astype(bf16)
                keep = jnp.where(lane == 2 * g + hh, top + jnp.log(d), keep)
                vm = jnp.where(lane_half(seq, hh), v2, jnp.zeros_like(v2))
                got = dot_nn(pr, vm)
                acc = got if acc is None else acc + got
            o[at, cs] = acc.astype(bf16)
        lse[at] = keep

    lse_t[...] = jnp.transpose(lse[...])[0:8]
    for i in range(seq // rows):
        at = pl.ds(i * rows, rows)
        a_low[at] = dot_nn(o[at], w[3]).astype(bf16)


def attn_fwd(layer, scal, rows_in, seg_row, seg_col, bias, own_qkv, own_out, a_refs, b_refs):
    first = layer == 0
    seq, width, cols = seg_row.shape[1], own_out.shape[2], own_out.shape[1]
    wide = SLOTS * cols
    outs = [shape((seq, width), f32), shape((seq, width), bf16)]
    if not first:
        outs += [shape((seq, width), f32), shape((seq, 1), f32)]
    outs += [
        shape((3, seq, wide), bf16),
        shape((8, seq), f32),
        shape((seq, wide), bf16),
        shape((seq, width), bf16),
    ]
    got = pl.pallas_call(
        functools.partial(attn_fwd_kernel, layer),
        out_shape=outs,
        in_specs=[SMEM] + [VMEM] * (len(rows_in) + 3) + [ANY] * 12,
        out_specs=[VMEM] * len(outs),
        scratch_shapes=[
            pltpu.VMEM((4, wide, width), bf16),
            pltpu.VMEM((seq, seq), f32),
            pltpu.VMEM((seq, 128), f32),
            pltpu.VMEM((2, BIAS_ROWS, width), bf16),
            pltpu.SemaphoreType.DMA((10,)),
        ],
        compiler_params=params(),
        cost_estimate=cost(12),
        name="attn_fwd",
    )(scal, *rows_in, seg_row, seg_col, *bias, own_qkv, own_out, *a_refs, *b_refs)
    if first:
        state, xr, qkv, lse_t, o, a_low = got
        return state, xr, None, None, qkv, lse_t, o, a_low
    return got


def ff_fwd_kernel(layer, scal, state, a_mine, a_theirs, ob, gain, shift, ub, own_up, own_down, *refs):
    moved = refs[:5]
    h, hr, normed, recip, g, gp, f_low, wu, wd, sems = refs[5:]
    step = pl.program_id(0)

    @pl.when(step == 0)
    def _():
        fetch_ff(scal, layer, own_up, own_down, moved, wu, wd, sems)

    z = state[...] + (a_mine[...].astype(f32) + a_theirs[...].astype(f32)) + ob[layer, 0:1]
    new, n, r = norm_forward(z, gain[layer, 0:1], shift[layer, 0:1])
    h[...] = new
    low = new.astype(bf16)
    hr[...] = low
    normed[...] = n
    recip[...] = r
    acc = None
    for k in range(wu.shape[0]):
        u = dot_nn(low, wu[k]) + ub[k : k + 1]
        phi = 0.5 * (1.0 + lax.erf(u * math.sqrt(0.5)))
        act = (u * phi).astype(bf16)
        g[k] = act
        gp[k] = (phi + u * (jnp.exp(-0.5 * u * u) * (1.0 / math.sqrt(2 * math.pi)))).astype(bf16)
        got = dot_nn(act, wd[k])
        acc = got if acc is None else acc + got
    f_low[...] = acc.astype(bf16)


def ff_scratch(n_t, width, half):
    return [
        pltpu.VMEM((n_t, width, half), bf16),
        pltpu.VMEM((n_t, half, width), bf16),
        pltpu.SemaphoreType.DMA((14,)),
    ]


def ff_fwd(layer, scal, state, a_mine, a_theirs, norms, ub, own_up, own_down, moved):
    seq, width = state.shape
    n_t, half = ub.shape
    rows = 256
    by_row = pl.BlockSpec((rows, width), lambda i: (i, 0))
    whole = lambda v: pl.BlockSpec(v.shape, lambda i: (0,) * v.ndim)
    by_quarter = pl.BlockSpec((n_t, rows, half), lambda i: (0, i, 0))
    return pl.pallas_call(
        functools.partial(ff_fwd_kernel, layer),
        grid=(seq // rows,),
        out_shape=[
            shape((seq, width), f32),
            shape((seq, width), bf16),
            shape((seq, width), f32),
            shape((seq, 1), f32),
            shape((n_t, seq, half), bf16),
            shape((n_t, seq, half), bf16),
            shape((seq, width), bf16),
        ],
        in_specs=[SMEM, by_row, by_row, by_row] + [whole(v) for v in norms] + [whole(ub)] + [ANY] * 7,
        out_specs=[
            by_row,
            by_row,
            by_row,
            pl.BlockSpec((rows, 1), lambda i: (i, 0)),
            by_quarter,
            by_quarter,
            by_row,
        ],
        scratch_shapes=ff_scratch(n_t, width, half),
        compiler_params=params(),
        cost_estimate=cost(11),
        name="ff_fwd",
    )(scal, state, a_mine, a_theirs, *norms, ub, own_up, own_down, *moved)


def ff_bwd_kernel(last, layer, scal, *refs):
    refs = list(refs)
    if last:
        h, f_mine, f_theirs, c_mine, c_theirs = refs[:5]
        refs = refs[5:]
    else:
        dz_in, x_mine, x_theirs, normed, recip = refs[:5]
        refs = refs[5:]
    ob, gain, shift, gp, own_up, own_down = refs[:6]
    moved = refs[6:11]
    refs = refs[11:]
    if last:
        out_low = refs.pop(0)
    dz2, dzr2, du, dh_low, small, ub_sum, wu, wd, sems = refs
    step = pl.program_id(0)

    @pl.when(step == 0)
    def _():
        small[...] = jnp.zeros_like(small)
        ub_sum[...] = jnp.zeros_like(ub_sum)
        fetch_ff(scal, layer, own_up, own_down, moved, wu, wd, sems)

    if last:
        z = h[...] + (f_mine[...].astype(f32) + f_theirs[...].astype(f32)) + ob[layer, 1:2]
        new, n, r = norm_forward(z, gain[layer, 1:2], shift[layer, 1:2])
        out_low[...] = new.astype(bf16)
        dy = jnp.where(step == scal[0], c_mine[...], c_theirs[...]).astype(f32)
    else:
        dy = dz_in[...] + (x_mine[...].astype(f32) + x_theirs[...].astype(f32))
        n, r = normed[...], recip[...]
    dz = norm_backward(dy, n, r, gain[layer, 1:2])
    dz2[...] = dz
    low = dz.astype(bf16)
    dzr2[...] = low
    small[0:1] += jnp.sum(dy * n, 0, keepdims=True)
    small[1:2] += jnp.sum(dy, 0, keepdims=True)
    small[2:3] += jnp.sum(dz, 0, keepdims=True)
    acc = None
    for k in range(wu.shape[0]):
        dg = dot_nt(low, wd[k])
        back = (dg * gp[k].astype(f32)).astype(bf16)
        du[k] = back
        ub_sum[k : k + 1] += jnp.sum(back.astype(f32), 0, keepdims=True)
        got = dot_nt(back, wu[k])
        acc = got if acc is None else acc + got
    dh_low[...] = acc.astype(bf16)


def ff_bwd(layer, scal, rows_in, norms, gp, own_up, own_down, moved, last):
    width = own_up.shape[1]
    n_t, seq, half = gp.shape
    rows = 256
    by_row = pl.BlockSpec((rows, width), lambda i: (i, 0))
    whole = lambda v: pl.BlockSpec(v.shape, lambda i: (0,) * v.ndim)
    by_quarter = pl.BlockSpec((n_t, rows, half), lambda i: (0, i, 0))
    if last:
        specs = [by_row] * 3 + [whole(rows_in[3]), whole(rows_in[4])]
    else:
        specs = [by_row] * 4 + [pl.BlockSpec((rows, 1), lambda i: (i, 0))]
    outs = [
        shape((seq, width), f32),
        shape((seq, width), bf16),
        shape((n_t, seq, half), bf16),
        shape((seq, width), bf16),
        shape((8, width), f32),
        shape((n_t, half), f32),
    ]
    out_specs = [by_row, by_row, by_quarter, by_row, pl.BlockSpec((8, width), lambda i: (0, 0)), pl.BlockSpec((n_t, half), lambda i: (0, 0))]
    if last:
        outs = [shape((seq, width), bf16)] + outs
        out_specs = [by_row] + out_specs
    return pl.pallas_call(
        functools.partial(ff_bwd_kernel, last, layer),
        grid=(seq // rows,),
        out_shape=outs,
        in_specs=[SMEM] + specs + [whole(v) for v in norms] + [by_quarter] + [ANY] * 7,
        out_specs=out_specs,
        scratch_shapes=ff_scratch(n_t, width, half),
        compiler_params=params(),
        cost_estimate=cost(11),
        name="ff_bwd",
    )(scal, *rows_in, *norms, gp, own_up, own_down, *moved)


SEND = ((2, 3), (1, 3))
NEXT = (1, 2)


def ff_dw_kernel(z_first, scal, g, du, hr, dzr2, *refs):
    outs, (su, sd, sems) = refs[:-3], refs[-3:]
    place = scal[1]
    n_t, width, half = su.shape
    part, rows = width // 4, half // 4

    def target(s, j):
        send, nxt, keep = outs[3 * s : 3 * s + 3]
        if j in SEND[s]:
            return send.at[SEND[s].index(j)]
        return nxt if j == NEXT[s] else keep

    def quarter(k):
        return lax.rem(scal[3] + n_t - k, n_t)

    copies = []

    def start(src, dst):
        copies.append(pltpu.make_async_copy(src, dst, sems.at[len(copies)]))
        copies[-1].start()

    chunk = 256
    for k in range(n_t):
        for c in range(width // chunk):
            at = pl.ds(c * chunk, chunk)
            su[k, at] = dot_tn(hr[:, at], du[k]).astype(bf16)
        if z_first:
            for p in range(4):
                start(su.at[k, pl.ds(p * part, part)], outs[0].at[quarter(k), p, 0])
    if not z_first:
        for j in range(4):
            at = pl.ds(pl.multiple_of((j ^ place) * part, part), part)
            start(su.at[:, at], target(0, j))
    for k in range(n_t):
        sd[k] = dot_tn(g[k], dzr2[...]).astype(bf16)
        if z_first:
            for p in range(4):
                for n in range(2):
                    start(
                        sd.at[k, pl.ds(p * rows, rows), pl.ds(n * half, half)],
                        outs[0].at[quarter(k), p, 1, pl.ds(n * rows, rows)],
                    )
    if not z_first:
        for j in range(4):
            at = pl.ds(pl.multiple_of((j ^ place) * rows, rows), rows)
            for n in range(2):
                start(sd.at[:, at, pl.ds(n * half, half)], target(1, j).at[:, pl.ds(n * rows, rows)])
    for c in copies:
        c.wait()


def ff_dw(scal, g, du, hr, dzr2, z_first):
    n_t, _, half = g.shape
    width = hr.shape[1]
    one = (n_t, width // 4, half)
    if z_first:
        outs = [shape((n_t, 4, 2, width // 4, half), bf16)]
    else:
        outs = [shape((2,) + one, bf16), shape(one, bf16), shape(one, bf16)] * 2
    return pl.pallas_call(
        functools.partial(ff_dw_kernel, z_first),
        out_shape=outs,
        in_specs=[SMEM] + [VMEM] * 4,
        out_specs=[ANY] * len(outs),
        scratch_shapes=[
            pltpu.VMEM((n_t, width, half), bf16),
            pltpu.VMEM((n_t, half, width), bf16),
            pltpu.SemaphoreType.DMA((12 * n_t,)),
        ],
        compiler_params=params(),
        cost_estimate=cost(6),
        name="ff_dw",
    )(scal, g, du, hr, dzr2)


def attn_bwd_kernel(layer, scal, dz2, h_mine, h_theirs, normed, recip, gain, qkv, lse_t, o, seg_row, seg_col, own_qkv, own_out, *refs):
    a_refs, b_refs = refs[:4], refs[4:8]
    dz1, dzr1, d4, dx_low, small, w, mask, do, sems = refs[8:]
    wait = fetch_attn(scal, layer, own_qkv, own_out, a_refs, b_refs, w, sems)
    slots = scal[2]
    seq, width = dz1.shape
    small[...] = jnp.zeros_like(small)

    @pl.loop(0, seq // 128)
    def _(i):
        at = pl.ds(pl.multiple_of(i * 128, 128), 128)
        dh = dz2[at] + (h_mine[at].astype(f32) + h_theirs[at].astype(f32))
        n = normed[at]
        dz = norm_backward(dh, n, recip[at], gain[layer, 0:1])
        dz1[at] = dz
        dzr1[at] = dz.astype(bf16)
        small[0:1] += jnp.sum(dh * n, 0, keepdims=True)
        small[1:2] += jnp.sum(dh, 0, keepdims=True)
        small[2:3] += jnp.sum(dz, 0, keepdims=True)

    ki = lax.broadcasted_iota(jnp.int32, (seq, seq), 0)
    qi = lax.broadcasted_iota(jnp.int32, (seq, seq), 1)
    visible = (seg_col[...] == seg_row[...]) & ((ki < slots) | (qi >= slots))
    mask[...] = jnp.where(visible, 0.0, masked_fill)
    wait()
    rows = 256
    for i in range(seq // rows):
        at = pl.ds(i * rows, rows)
        do[at] = dot_nt(dzr1[at], w[3]).astype(bf16)
    d4[3] = o[...]
    pairs = qkv.shape[2] // 128
    tile = 256
    scale = 1.0 / math.sqrt(HEAD_DIM)
    for g in range(pairs):
        cs = pl.ds(g * 128, 128)
        k2 = qkv[1, :, cs] * jnp.asarray(scale, bf16)
        v2 = qkv[2, :, cs]
        dv = dk = None
        for i in range(seq // tile):
            at = pl.ds(i * tile, tile)
            q2 = qkv[0, at, cs]
            do2 = do[at, cs]
            bias = mask[:, at]
            dq = None
            for hh in range(2):
                all_half = lane_half(seq, hh)
                tile_half = lane_half(tile, hh)
                km = jnp.where(all_half, k2, jnp.zeros_like(k2))
                vm = jnp.where(all_half, v2, jnp.zeros_like(v2))
                qm = jnp.where(tile_half, q2, jnp.zeros_like(q2))
                dom = jnp.where(tile_half, do2, jnp.zeros_like(do2))
                head = 2 * g + hh
                s = dot_nt(km, q2) + bias
                pr = jnp.exp(s - lse_t[head : head + 1, at])
                dp = dot_nt(vm, do2)
                delta = jnp.sum(pr * dp, 0, keepdims=True)
                ds = (pr * (dp - delta)).astype(bf16)
                got_v = dot_nn(pr.astype(bf16), dom)
                got_k = dot_nn(ds, qm)
                got_q = dot_nn(jnp.transpose(km), ds)
                dv = got_v if dv is None else dv + got_v
                dk = got_k if dk is None else dk + got_k
                dq = got_q if dq is None else dq + got_q
            dqr = jnp.transpose(dq)
            d4[0, at, cs] = dqr.astype(bf16)
        dkr = (dk * scale).astype(bf16)
        dvr = dv.astype(bf16)
        d4[1, :, cs] = dkr
        d4[2, :, cs] = dvr
    wide = d4.shape[2]
    small[3:4, 0:wide] = jnp.sum(d4[0].astype(f32), 0, keepdims=True)
    small[3:4, wide : 2 * wide] = jnp.sum(d4[2].astype(f32), 0, keepdims=True)
    for i in range(seq // rows):
        at = pl.ds(i * rows, rows)
        acc = dot_nn(d4[0, at], w[0]) + dot_nn(d4[1, at], w[1]) + dot_nn(d4[2, at], w[2])
        dx_low[at] = acc.astype(bf16)


def attn_bwd(layer, scal, dz2, h_mine, h_theirs, normed, recip, gain, qkv, lse_t, o, seg_row, seg_col, own_qkv, own_out, a_refs, b_refs):
    seq, width = dz2.shape
    wide = qkv.shape[2]
    return pl.pallas_call(
        functools.partial(attn_bwd_kernel, layer),
        out_shape=[
            shape((seq, width), f32),
            shape((seq, width), bf16),
            shape((4, seq, wide), bf16),
            shape((seq, width), bf16),
            shape((8, width), f32),
        ],
        in_specs=[SMEM] + [VMEM] * 11 + [ANY] * 10,
        out_specs=[VMEM] * 5,
        scratch_shapes=[
            pltpu.VMEM((4, wide, width), bf16),
            pltpu.VMEM((seq, seq), f32),
            pltpu.VMEM((seq, wide), bf16),
            pltpu.SemaphoreType.DMA((8,)),
        ],
        compiler_params=params(),
        cost_estimate=cost(14),
        name="attn_bwd",
    )(scal, dz2, h_mine, h_theirs, normed, recip, gain, qkv, lse_t, o, seg_row, seg_col, own_qkv, own_out, *a_refs, *b_refs)


def attn_dw_kernel(scal, d4, xr, dzr1, *outs):
    place = scal[1]
    cols = d4.shape[2] // 2
    for j in range(4):
        t = j ^ place
        right = jnp.where(t == 3, dzr1[...], xr[...])
        got = dot_tn(d4[t], right).astype(bf16)
        for s in range(SLOTS):
            send, nxt, keep = outs[3 * s : 3 * s + 3]
            val = got[s * cols : (s + 1) * cols]
            if j in SEND[s]:
                send[SEND[s].index(j), 0] = val
            elif j == NEXT[s]:
                nxt[0] = val
            else:
                keep[0] = val


def attn_dw(scal, d4, xr, dzr1):
    cols, width = d4.shape[2] // 2, xr.shape[1]
    outs = [shape((2, 1, cols, width), bf16), shape((1, cols, width), bf16), shape((1, cols, width), bf16)] * 2
    return pl.pallas_call(
        attn_dw_kernel,
        out_shape=outs,
        in_specs=[SMEM] + [VMEM] * 3,
        out_specs=[VMEM] * 6,
        compiler_params=params(),
        cost_estimate=cost(4.5),
        name="attn_dw",
    )(scal, d4, xr, dzr1)


def low_sum(*parts):
    total = parts[0].astype(f32)
    for v in parts[1:]:
        total = total + v.astype(f32)
    return total.astype(bf16)


def piece_call(kernel, outs, us, name, scal, *ins):
    specs, args = [], []
    for v in ins:
        if isinstance(v, tuple):
            v, at = v
            n = v.ndim
            specs.append(pl.BlockSpec((1,) + v.shape[1:], lambda i, at=at, n=n: (at,) + (0,) * (n - 1)))
        else:
            n = v.ndim
            specs.append(pl.BlockSpec(v.shape, lambda i, n=n: (0,) * n))
        args.append(v)
    return pl.pallas_call(
        kernel,
        grid=(1,),
        out_shape=outs,
        in_specs=[SMEM] + specs,
        out_specs=[pl.BlockSpec(v.shape, lambda i, n=len(v.shape): (0,) * n) for v in outs],
        compiler_params=params(),
        cost_estimate=cost(us),
        name=name,
    )(scal, *args)


def add2_kernel(scal, nxt_a, got_a, nxt_b, got_b, out_a, out_b):
    out_a[...] = low_sum(nxt_a[...], got_a[0])
    out_b[...] = low_sum(nxt_b[...], got_b[0])


def sum_kernel(scal, keep_a, got_a, more_a, keep_b, got_b, more_b, out_a, out_b):
    out_a[...] = low_sum(keep_a[...], got_a[0], more_a[...])
    out_b[...] = low_sum(keep_b[...], got_b[0], more_b[...])


def quarter_sum_kernel(scal, keep_a, got_a, more_a, keep_b, got_b, more_b, out):
    n_t = out.shape[0]
    for k in range(n_t):
        q = lax.rem(scal[3] + n_t - k, n_t)
        out[q, 0] = low_sum(keep_a[k], got_a[0, k], more_a[k])
        out[q, 1] = low_sum(keep_b[k], got_b[0, k], more_b[k])


def pick_kernel(scal, every, out, ub):
    n_t, rows = every.shape[0], out.shape[2]
    for k in range(n_t):
        q = lax.rem(scal[3] + n_t - k, n_t)
        ub[k : k + 1] = jnp.sum(every[q, 2 * rows : 2 * rows + 3].astype(f32), 0, keepdims=True)
        if k:
            for n in range(2):
                out[n, k - 1] = every[q, n * rows : (n + 1) * rows]


def pick(scal, every, rows):
    n_t, _, half = every.shape
    return pl.pallas_call(
        pick_kernel,
        out_shape=[shape((2, n_t - 1, rows, half), bf16), shape((n_t, half), f32)],
        in_specs=[SMEM, VMEM],
        out_specs=[VMEM, VMEM],
        compiler_params=params(),
        cost_estimate=cost(1.5),
        name="pick_quarters",
    )(scal, every)


def split_kernel(scal, every, *outs):
    place = scal[1]
    for s in range(SLOTS):
        send, nxt, keep = outs[3 * s : 3 * s + 3]
        for j in range(4):
            val = every[j ^ place, s]
            if j in SEND[s]:
                send[SEND[s].index(j), 0] = val
            elif j == NEXT[s]:
                nxt[0] = val
            else:
                keep[0] = val


def split_pieces(scal, every):
    _, _, rows, half = every.shape
    one = (1, rows, half)
    outs = [shape((2,) + one, bf16), shape(one, bf16), shape(one, bf16)] * 2
    return piece_call(split_kernel, outs, 1.5, "split_pieces", scal, every)


def tot_kernel(scal, a, moved_a, moved_b, out):
    @pl.when(scal[0] == 0)
    def _():
        out[...] = low_sum(a[...], moved_b[...])

    @pl.when(scal[0] != 0)
    def _():
        out[...] = low_sum(moved_a[...], moved_b[...])


def fin_kernel(scal, mine, theirs, out, half):
    rows = half.shape[1]
    out[...] = low_sum(mine[...], theirs[...])
    at = pl.ds(pl.multiple_of(scal[0] * rows, rows), rows)
    half[...] = out[:, at]


def halves(scal, mine, theirs):
    core = scal[0]
    rows = mine[0].shape[1]
    for j in range(1, 4):
        for ref, c in ((mine[j - 1], core), (theirs[j - 1], 1 - core)):
            yield j ^ scal[1], pl.multiple_of(c * rows, rows), rows, ref


def ff_out_kernel(n_alias, scal, mine, theirs, *refs):
    up, down = refs[n_alias:]
    _, _, part, half = mine.shape
    rows = half // 4
    for ref, c in ((mine, scal[0]), (theirs, 1 - scal[0])):
        off = pl.multiple_of(c * half, half)
        for p in range(4):
            up[0, pl.ds(p * part, part), pl.ds(off, half)] = ref[p, 0].astype(f32)
            at = pl.ds(pl.multiple_of(off + p * rows, rows), rows)
            for n in range(2):
                down[0, at, pl.ds(n * half, half)] = ref[p, 1, pl.ds(n * rows, rows)].astype(f32)


def attn_out_kernel(n_alias, scal, full, *refs):
    mine, theirs = refs[:3], refs[3:6]
    qkv, out = refs[6 + n_alias :]
    parts = [(scal[1], 0, full.shape[1], full)] + list(halves(scal, mine, theirs))
    for t, off, rows, ref in parts:
        val = ref[0].astype(f32)

        @pl.when(t < 3)
        def _(t=t, off=off, rows=rows, val=val):
            qkv[0, jnp.minimum(t, 2), pl.ds(off, rows)] = val

        @pl.when(t == 3)
        def _(off=off, rows=rows, val=val):
            out[0, pl.ds(off, rows)] = val


def out_call(kernel, name, layer, dims, scal, ins, before):
    whole = lambda v: pl.BlockSpec(v.shape, lambda i: (0,) * v.ndim)
    before = list(before or [])
    return pl.pallas_call(
        functools.partial(kernel, len(before)),
        grid=(1,),
        out_shape=[shape(d, f32) for d in dims],
        in_specs=[SMEM] + [whole(v) for v in ins] + [ANY] * len(before),
        out_specs=[pl.BlockSpec((1,) + d[1:], lambda i, n=len(d): (layer,) + (0,) * (n - 1)) for d in dims],
        input_output_aliases={1 + len(ins) + i: i for i in range(len(before))},
        compiler_params=params(),
        cost_estimate=cost(3),
        name=name,
    )(scal, *ins, *before)


def after(v, *others):
    return lax.optimization_barrier((v, *others))[0]


def local(
    block_input,
    w_qkv,
    qv_bias,
    w_out,
    out_bias,
    w_up,
    up_bias,
    w_down,
    norm_gain,
    norm_shift,
    segment_ids,
    slot_counts,
    cotangent,
):
    layers, width, _, cols = w_qkv.shape
    hidden = w_up.shape[2]
    seq = segment_ids.shape[1]
    n_dp, n_t = lax.axis_size("dp"), lax.axis_size("tensor")
    dp, z = lax.axis_index("dp"), lax.axis_index("tensor")
    core, place = dp & 1, (dp >> 1) & 3
    first = core == 0
    part = hidden // 4
    norms_in = (out_bias, norm_gain, norm_shift)

    def flip(v, bits, odd=False):
        pairs = [(i, i ^ bits) for i in range(n_dp) if not odd or i & 1]
        return lax.ppermute(v, "dp", pairs)

    def across(v):
        return flip(v, 1)

    def shift(v, by):
        pairs = []
        for i in range(n_dp):
            move = by[i & 1]
            if move:
                pairs += [(i * n_t + k, i * n_t + (k + move) % n_t) for k in range(n_t)]
        return lax.ppermute(v, ("dp", "tensor"), pairs)

    def rotate(v, by):
        return lax.ppermute(v, "tensor", [(i, (i + by) % n_t) for i in range(n_t)])

    def swap(v):
        pairs = []
        for i in range(n_dp):
            for k in range(n_t):
                if (i & 1) != (k & 1):
                    pairs.append((i * n_t + k, (i ^ 1) * n_t + (k ^ 1)))
        moved = lax.ppermute(v, ("dp", "tensor"), pairs)
        return jnp.where(core == (z & 1), v, moved)

    own_qkv = jnp.transpose(w_qkv, (0, 2, 3, 1))

    def attn_piece(l):
        qkv_piece = lax.dynamic_index_in_dim(own_qkv[l], jnp.minimum(place, 2), 0, False)
        return jnp.where(place == 3, w_out[l], qkv_piece)

    half = hidden // 2

    def ff_piece(l):
        up_piece = lax.dynamic_slice(w_up[l], (place * part, core * half), (part, half))
        down_piece = lax.dynamic_slice_in_dim(w_down[l], core * half + place * (half // 4), half // 4, 0)
        return jnp.concatenate([up_piece, down_piece[:, :half], down_piece[:, half:], up_packed[l]], 0)

    def ff_over_xy(every):
        own, ub = pick(scal, every, part)
        x, y = flip(own, 2), flip(own, 4)
        return (own, x, y, flip(x[0], 4), flip(y[1], 2)), ub

    def over_z(piece):
        return shift(piece, (1, 2)), shift(piece, (0, 3))

    def over_xy(b, a):
        bx = flip(b, 2)
        by = flip(b, 4)
        ay = flip(a, 4, True)
        ax = flip(a, 2, True)
        bd = flip(bx, 4)
        ad = flip(ay, 2, True)
        return (a, ax, ay, ad), (b, bx, by, bd)

    packed = jnp.concatenate([segment_ids, jnp.broadcast_to(slot_counts[:, None], (segment_ids.shape[0], 128))], 1)
    packed = jnp.where(core == (z & 1), packed, across(packed))
    packed = lax.dynamic_index_in_dim(packed, z >> 1, 0, False)
    segments, slot_count = packed[:seq], packed[seq]
    seg_row, seg_col = segments[None, :], segments[:, None]
    scal = jnp.stack([core, place, slot_count, z]).astype(jnp.int32)
    own_bias = qv_bias.reshape(1, -1)
    up_packed, qv_packed = pack_bias(jnp.stack([core, place]).astype(jnp.int32), up_bias, own_bias)
    piece = jnp.concatenate([attn_piece(0), qv_packed], 0)
    z_moved = [over_z(piece)]
    x_mine = swap(block_input)
    x_theirs = across(x_mine)
    ff_every = []
    for l in range(layers):
        if l:
            z_moved.append(over_z(after(attn_piece(l), ff_every[-1])))
        piece = ff_piece(l) if l == 0 else after(ff_piece(l), ff_every[-1])
        ff_every.append(lax.all_gather(piece, "tensor", axis=0))
    attn_w = [over_xy(*m) for m in z_moved]
    bias = (own_bias,) + z_moved[0][::-1]
    ff_w, ub = zip(*[ff_over_xy(e) for e in ff_every])

    rows_in = (x_mine, x_theirs)
    saved = []
    for l in range(layers):
        rows_in = (after(rows_in[0], ff_w[l][0]),) + rows_in[1:]
        state, xr, n2, r2, qkv, lse_t, o, a_low = attn_fwd(
            l, scal, rows_in, seg_row, seg_col, bias, own_qkv, w_out, *attn_w[l]
        )
        if l:
            saved[l - 1] += (n2, r2)
        if l + 1 < layers:
            state = after(state, *z_moved[l + 1])
        h, hr, n1, r1, g, gp, f_low = ff_fwd(
            l, scal, state, a_low, across(a_low), norms_in, ub[l], w_up, w_down, ff_w[l]
        )
        saved.append((xr, qkv, lse_t, o, hr, n1, r1, g, gp))
        rows_in = (h, f_low, across(f_low)) + norms_in

    class Chunk:
        def __init__(self, pieces):
            self.pieces = pieces
            self.got = (flip(pieces[0], 4), flip(pieces[3], 2))

        def second(self, *late):
            p, got = self.pieces, self.got
            nxt = after(p[1], *late)
            outs = [shape(nxt.shape, bf16)] * 2
            self.sec = piece_call(add2_kernel, outs, 1.2, "add_second", scal, nxt, (got[0], 1), p[4], (got[1], 1))
            self.more = (flip(self.sec[0], 2), flip(self.sec[1], 4))
            return self

        def plain_third(self, *late):
            p, got, more = self.pieces, self.got, self.more
            keep = after(p[2], *late)
            outs = [shape(keep.shape, bf16)] * 2
            self.sums = piece_call(
                sum_kernel, outs, 1.5, "add_third", scal, keep, (got[0], 0), more[0], p[5], (got[1], 0), more[1]
            )
            return self.sums

        def third(self, *late):
            a, b = self.plain_third(*late)
            self.moved = (shift(a, (0, n_t - 3)), shift(b, (n_t - 1, n_t - 2)))
            return self

        def fourth(self, *late):
            a = after(self.sums[0], *late)
            (total,) = piece_call(tot_kernel, [shape(a.shape, bf16)], 1.2, "add_fourth", scal, a, *self.moved)
            bits = 8
            while bits < n_dp:
                total = low_sum(total, flip(total, bits))
                bits *= 2
            self.total = total
            self.other = across(total)
            return self

        def fifth(self, *late):
            total = after(self.total, *late)
            n, rows, wide = total.shape
            outs = [shape(total.shape, bf16), shape((n, rows // 2, wide), bf16)]
            self.full, half = piece_call(fin_kernel, outs, 1.2, "add_fifth", scal, total, self.other)
            self.half = half
            self.mine = [flip(half, bits) for bits in (2, 4, 6)]
            self.theirs = [across(v) for v in self.mine]
            return self

    class FFChunk(Chunk):
        def __init__(self, pieces):
            self.z_first = len(pieces) == 1
            if self.z_first:
                self.total = lax.psum_scatter(pieces[0], "tensor", scatter_dimension=0, tiled=False)
            else:
                super().__init__(pieces)

        def split(self, *late):
            super().__init__(split_pieces(scal, after(self.total, *late)))
            return self

        def third(self, *late):
            if self.z_first:
                super_sums = self.plain_third(*late)
                self.total = jnp.concatenate(super_sums, 0)
                return self
            p, got, more = self.pieces, self.got, self.more
            keep = after(p[2], *late)
            n, rows, wide = keep.shape
            (self.sums,) = piece_call(
                quarter_sum_kernel,
                [shape((n, 2, rows, wide), bf16)],
                1.5,
                "add_quarters",
                scal,
                keep,
                (got[0], 0),
                more[0],
                p[5],
                (got[1], 0),
                more[1],
            )
            self.total = lax.psum_scatter(self.sums, "tensor", scatter_dimension=0, tiled=False)
            self.sums = (self.sums,)
            return self

        def fourth(self, *late):
            total = after(self.total, *late)
            bits = 8
            while bits < n_dp:
                total = low_sum(total, flip(total, bits))
                bits *= 2
            groups = [[i | j for j in (0, 2, 4, 6)] for i in range(n_dp) if not i & 6]
            self.mine = lax.all_gather(total, "dp", axis=0, axis_index_groups=groups)
            self.theirs = across(self.mine)
            return self

    chunks, smalls = [], []
    for l in reversed(range(layers)):
        last = l == layers - 1
        xr, qkv, lse_t, o, hr, n1, r1, g, gp = saved[l][:9]
        if last:
            c_mine = swap(cotangent)
            ff_rows = rows_in[:3] + (c_mine, across(c_mine))
        else:
            ff_rows = (dz1, dx_low, across(dx_low)) + saved[l][9:]
        got = ff_bwd(l, scal, ff_rows, norms_in, gp, w_up, w_down, ff_w[l], last)
        if last:
            out_low = got[0]
            got = got[1:]
        dz2, dzr2, du, dh_low, small2, ub_sum = got
        ff_pieces = ff_dw(scal, g, du, hr, dzr2, last)
        ff = FFChunk(ff_pieces)
        dh_theirs = across(dh_low)
        if chunks:
            chunks[1].second(ff_pieces[0])
            dz2 = after(dz2, *chunks[1].sec)
        dz2 = after(dz2, ff_pieces[0])
        dz1, dzr1, d4, dx_low, small1 = attn_bwd(
            l, scal, dz2, dh_low, dh_theirs, n1, r1, norm_gain, qkv, lse_t, o, seg_row, seg_col, own_qkv, w_out, *attn_w[l]
        )
        if chunks:
            chunks[1].third(dx_low)
            xr = after(xr, *chunks[1].sums)
        at_pieces = attn_dw(scal, d4, xr, dzr1)
        at = Chunk(at_pieces)
        dz1 = after(dz1, at_pieces[0])
        chunks += [ff, at]
        smalls.append((small1, small2, ub_sum))
    smalls = smalls[::-1]

    f1, a1, f0, a0 = chunks
    f0.second(at_pieces[2])
    a1.fourth(*f0.sec)
    a1.fifth()
    a0.second(a1.full)
    f0.third(*a0.sec)
    f1.split(*f0.sums)
    a0.third(f1.pieces[0])
    f1.second(*a0.sums)
    f1.third(*f1.sec)
    a0.fourth(*f1.sums)
    a0.fifth()
    f1.fourth(a0.full)
    f0.fourth(f1.mine)
    ff_dims = [(layers, width, hidden), (layers, hidden, width)]
    at_dims = [(layers, 3, cols, width), (layers, cols, width)]

    def ff_finish(l, c, before):
        return out_call(ff_out_kernel, "ff_out", l, ff_dims, scal, [c.mine, c.theirs], before)

    def at_finish(l, c, before):
        return out_call(attn_out_kernel, "attn_out", l, at_dims, scal, [c.full, *c.mine, *c.theirs], before)

    ff_out = ff_finish(0, f0, ff_finish(1, f1, None))
    at_out = at_finish(0, a0, at_finish(1, a1, None))

    out_half = lax.dynamic_slice_in_dim(out_low, core * (seq // 2), seq // 2, 0)
    mixed = swap(out_half)
    dx = dz1 + (dx_low.astype(f32) + across(dx_low).astype(f32))
    input_grad = swap(lax.dynamic_slice_in_dim(dx, core * (seq // 2), seq // 2, 0))

    once = jnp.where(first, 1.0, 0.0).astype(f32)
    norms = jnp.stack([jnp.concatenate([g[0][:3], g[1][:3]]) for g in smalls]) * once
    quarters = jnp.where(first, jnp.stack([z, z + n_t - 1]), jnp.stack([z + 1, z + 2])) % n_t
    spread = (quarters[:, None] == jnp.arange(n_t)[None]).astype(f32)
    qv_slots = jnp.stack([g[0][3].reshape(2, SLOTS, cols).transpose(1, 0, 2).reshape(SLOTS, -1) for g in smalls])
    qv_placed = jnp.sum(qv_slots[:, :, None] * spread[None, :, :, None], 1)
    ub_quarters = (z + n_t - jnp.arange(n_t)) % n_t
    ub_placed = jnp.take(jnp.stack([g[2] for g in smalls]), ub_quarters, axis=1)
    ub_placed = jnp.where(
        first,
        jnp.concatenate([ub_placed, jnp.zeros_like(ub_placed)], 2),
        jnp.concatenate([jnp.zeros_like(ub_placed), ub_placed], 2),
    )
    placed = jnp.concatenate([ub_placed, qv_placed], 2)
    flat = jnp.concatenate([norms.reshape(-1), placed.reshape(-1)]).reshape(-1, 128)
    bits = 1
    while bits < n_dp:
        flat = flat + flip(flat, bits)
        bits *= 2
    bits = 1
    while bits < n_t:
        flat = flat + lax.ppermute(flat, "tensor", [(i, i ^ bits) for i in range(n_t)])
        bits *= 2
    flat = flat.reshape(-1)
    norms = flat[: norms.size].reshape(layers, 2, 3, width)
    placed = lax.dynamic_index_in_dim(flat[norms.size :].reshape(placed.shape), z, 1, False)
    return (
        mixed,
        input_grad,
        jnp.transpose(at_out[0], (0, 3, 1, 2)),
        placed[:, hidden:].reshape(layers, 2, cols),
        at_out[1],
        norms[:, :, 2],
        ff_out[0],
        placed[:, :hidden],
        ff_out[1],
        norms[:, :, 0],
        norms[:, :, 1],
    )


def solution(mesh):
    placed = (
        P(("dp", "tensor"), None),
        P(None, None, None, "tensor"),
        P(None, None, "tensor"),
        P(None, "tensor", None),
        P(),
        P(None, None, "tensor"),
        P(None, "tensor"),
        P(None, "tensor", None),
        P(),
        P(),
        P("dp", None),
        P("dp"),
        P(("dp", "tensor"), None),
    )
    return jax.shard_map(
        local,
        mesh=mesh,
        in_specs=placed,
        out_specs=(
            P(("dp", "tensor"), None),
            P(("dp", "tensor"), None),
            P(None, None, None, "tensor"),
            P(None, None, "tensor"),
            P(None, "tensor", None),
            P(),
            P(None, None, "tensor"),
            P(None, "tensor"),
            P(None, "tensor", None),
            P(),
            P(),
        ),
        check_vma=False,
    )
```

```python
import functools
import math

import jax
import jax.numpy as jnp
from jax import lax
from jax.experimental import pallas as pl
from jax.experimental.pallas import tpu as pltpu
from jax.sharding import PartitionSpec as P

HEAD_DIM = 64
epsilon = 1e-06
masked_fill = -1e30
bf16 = jnp.bfloat16
f32 = jnp.float32
ANY = pl.BlockSpec(memory_space=pl.ANY)
SMEM = pl.BlockSpec(memory_space=pltpu.SMEM)
VMEM = pl.BlockSpec(memory_space=pltpu.VMEM)
HBM = pl.BlockSpec(memory_space=pltpu.HBM)
SLOTS = 2
PACE = 1.0


def dot_nn(left, right):
    return lax.dot_general(left, right, (((1,), (0,)), ((), ())), preferred_element_type=f32)


def dot_nt(left, right):
    return lax.dot_general(left, right, (((1,), (1,)), ((), ())), preferred_element_type=f32)


def dot_tn(left, right):
    return lax.dot_general(left, right, (((0,), (0,)), ((), ())), preferred_element_type=f32)


def norm_forward(summed, gain, shift):
    center = summed - jnp.mean(summed, -1, keepdims=True)
    recip = lax.rsqrt(jnp.mean(center * center, -1, keepdims=True) + epsilon)
    normed = center * recip
    return normed * gain + shift, normed, recip


def norm_backward(grad_rows, normed, recip, gain):
    scaled = grad_rows * gain
    first_mean = jnp.mean(scaled, -1, keepdims=True)
    second_mean = jnp.mean(scaled * normed, -1, keepdims=True)
    return recip * (scaled - first_mean - normed * second_mean)


def shape(dims, dtype):
    return jax.ShapeDtypeStruct(dims, dtype)


def params(mib):
    return pltpu.CompilerParams(vmem_limit_bytes=mib * 1024 * 1024)


def here():
    dp = lax.axis_index("dp")
    return dp & 1, (dp >> 1) & 3, lax.axis_index("tensor")


def cost(us):
    return pl.CostEstimate(flops=int(us * 1.1e9 * PACE), bytes_accessed=int(us * 3.6e6 * PACE), transcendentals=0)


def lane_half(rows, which):
    lane = lax.broadcasted_iota(jnp.int32, (rows, 2 * HEAD_DIM), 1)
    return (lane < HEAD_DIM) if which == 0 else (lane >= HEAD_DIM)


class Moves:
    def __init__(self, sems):
        self.sems, self.count, self.out = sems, 0, []

    def make(self, src, dst):
        self.count += 1
        return pltpu.make_async_copy(src, dst, self.sems.at[self.count - 1])

    def start(self, src, dst):
        copy = self.make(src, dst)
        copy.start()
        return copy

    def send(self, src, dst):
        self.out.append(self.start(src, dst))

    def finish(self):
        for copy in self.out:
            copy.wait()


def wait_all(copies):
    for c in copies:
        c.wait()


MOVES = 80
CHUNK = 256


def fetch_attn(moves, layer, own_qkv, own_out, a_refs, b_refs, w):
    core, place, _ = here()
    cols = own_out.shape[1]
    waits = []
    for j in range(4):
        t = j ^ place
        b = moves.start(b_refs[j].at[pl.ds(0, cols)], w.at[t, pl.ds(cols, cols)])
        dst = w.at[t, pl.ds(0, cols)]
        a = moves.make(a_refs[j].at[pl.ds(0, cols)], dst)
        sem = moves.sems.at[moves.count - 1]
        qkv_copy = pltpu.make_async_copy(own_qkv.at[layer, jnp.minimum(t, 2)], dst, sem)
        out_copy = pltpu.make_async_copy(own_out.at[layer], dst, sem)

        @pl.when(core != 0)
        def _(a=a):
            a.start()

        @pl.when((core == 0) & (t < 3))
        def _(qkv_copy=qkv_copy):
            qkv_copy.start()

        @pl.when((core == 0) & (t == 3))
        def _(out_copy=out_copy):
            out_copy.start()

        waits += [b, a]
    return waits


def fetch_ff(moves, layer, own_up, own_down, moved, wu, wd):
    core, place, _ = here()
    width, half = wu.shape[0], own_up.shape[2] // 2
    n_t = wu.shape[1] // half
    part, rows = width // 4, half // 4
    own, x, y, diag_up, diag_down = moved
    ups = [own.at[0], x.at[0], y.at[0], diag_up]
    downs = [own.at[1], x.at[1], y.at[1], diag_down]
    mine = pl.ds(pl.multiple_of(core * half, half), half)

    def up(k):
        if k == 0:
            return [moves.start(own_up.at[layer, :, mine], wu.at[:, pl.ds(0, half)])]
        got = []
        for j in range(4):
            at = pl.ds(pl.multiple_of((j ^ place) * part, part), part)
            got.append(moves.start(ups[j].at[k - 1], wu.at[at, pl.ds(k * half, half)]))
        return got

    def down(k):
        if k == 0:
            return [moves.start(own_down.at[layer, mine], wd.at[pl.ds(0, half)])]
        got = []
        for j in range(4):
            at = pl.ds(pl.multiple_of(k * half + (j ^ place) * rows, rows), rows)
            for n in range(2):
                src = downs[j].at[k - 1, pl.ds(n * rows, rows)]
                got.append(moves.start(src, wd.at[at, pl.ds(n * half, half)]))
        return got

    return up, down, n_t


def chunk_waits(waits, chunk, half):
    start, end = chunk * CHUNK, (chunk + 1) * CHUNK
    for k, copies in enumerate(waits):
        if start <= k * half < end:
            wait_all(copies)


BIAS_ROWS = 16


def split_rows(v):
    parts = []
    for _ in range(3):
        low = v.astype(bf16)
        parts.append(low)
        v = v - low.astype(f32)
    n = sum(p.shape[0] for p in parts)
    return jnp.concatenate(parts + [jnp.zeros((BIAS_ROWS - n, v.shape[1]), bf16)], 0)


def prepare_kernel(own_qkv, own_out, own_up, own_down, up_bias, qv_bias, segments, counts, *refs):
    layers = own_out.shape[0]
    attn, ff, packed, sems = refs[:layers], refs[layers : 2 * layers], refs[2 * layers], refs[2 * layers + 1]
    core, place, _ = here()
    cols, half = own_out.shape[1], up_bias.shape[1] // 2
    part, rows = own_up.shape[1] // 4, half // 4
    copies = []
    for l in range(layers):
        weights = attn[l].at[pl.ds(0, cols)]

        @pl.when(place < 3)
        def _(l=l, weights=weights):
            pltpu.make_async_copy(own_qkv.at[l, jnp.minimum(place, 2)], weights, sems.at[4 * l]).start()

        @pl.when(place == 3)
        def _(l=l, weights=weights):
            pltpu.make_async_copy(own_out.at[l], weights, sems.at[4 * l]).start()

        copies.append(pltpu.make_async_copy(own_out.at[l], weights, sems.at[4 * l]))
        up = own_up.at[l, pl.ds(pl.multiple_of(place * part, part), part), pl.ds(pl.multiple_of(core * half, half), half)]
        copies.append(pltpu.make_async_copy(up, ff[l].at[pl.ds(0, part)], sems.at[4 * l + 1]))
        copies[-1].start()
        at = pl.ds(pl.multiple_of(core * half + place * rows, rows), rows)
        for n in range(2):
            down = own_down.at[l, at, pl.ds(n * half, half)]
            copies.append(pltpu.make_async_copy(down, ff[l].at[pl.ds(part + n * rows, rows)], sems.at[4 * l + 2 + n]))
            copies[-1].start()
    for l in range(layers):
        row = jnp.where(core == 0, up_bias[l : l + 1, :half], up_bias[l : l + 1, half:])
        ff[l][2 * part :] = split_rows(row)
    attn[0][cols:] = split_rows(qv_bias[...])
    n, seq = segments.shape
    packed[:, :seq] = segments[...]
    for i in range(n):
        packed[i : i + 1, seq:] = jnp.full((1, packed.shape[1] - seq), counts[i], jnp.int32)
    for c in copies:
        c.wait()


def prepare(own_qkv, own_out, own_up, own_down, up_bias, qv_bias, segments, counts):
    layers, cols, width = own_out.shape
    half = up_bias.shape[1] // 2
    outs = [shape((cols + (0 if l else BIAS_ROWS), width), bf16) for l in range(layers)]
    outs += [shape((width // 2 + BIAS_ROWS, half), bf16)] * layers
    outs += [shape((segments.shape[0], segments.shape[1] + 128), jnp.int32)]
    got = pl.pallas_call(
        prepare_kernel,
        out_shape=outs,
        in_specs=[HBM] * 4 + [VMEM] * 3 + [SMEM],
        out_specs=[VMEM] * len(outs),
        scratch_shapes=[pltpu.SemaphoreType.DMA((4 * layers,))],
        compiler_params=params(56),
        cost_estimate=cost(2),
        name="prepare",
    )(own_qkv, own_out, own_up, own_down, up_bias, qv_bias, segments, counts)
    return got[:layers], got[layers : 2 * layers], got[2 * layers]


def mask_kernel(mine, theirs, out, out_t):
    core, _, z = here()
    row = pl.ds(z >> 1, 1)
    packed = jnp.where(core == (z & 1), mine[row], theirs[row])
    seq = out.shape[0]
    segments, slots = packed[:, :seq].astype(f32), packed[:, seq : seq + 1]
    column = jnp.transpose(jnp.broadcast_to(segments, (128, seq)))[:, 0:1]
    same = column == segments
    down = lax.broadcasted_iota(jnp.int32, (seq, seq), 0)
    along = lax.broadcasted_iota(jnp.int32, (seq, seq), 1)
    out[...] = jnp.where(same & ((along < slots) | (down >= slots)), 0.0, masked_fill)
    out_t[...] = jnp.where(same & ((down < slots) | (along >= slots)), 0.0, masked_fill)


def masks(mine, theirs):
    seq = mine.shape[1] - 128
    return pl.pallas_call(
        mask_kernel,
        out_shape=[shape((seq, seq), f32)] * 2,
        in_specs=[VMEM, VMEM],
        out_specs=[VMEM] * 2,
        compiler_params=params(12),
        cost_estimate=cost(2),
        name="masks",
    )(mine, theirs)


def attn_fwd_kernel(layer, *refs):
    refs = list(refs)
    first = layer == 0
    rows_in = refs[: 2 if first else 3]
    refs = refs[len(rows_in) :]
    if not first:
        ob, gain, shift = refs[:3]
        refs = refs[3:]
    own_bias, mask_in, a_bias, b_bias, own_qkv, own_out = refs[:6]
    a_refs, b_refs = refs[6:10], refs[10:14]
    refs = refs[14:]
    n_out = 5 if first else 7
    outs, refs = refs[:n_out], refs[n_out:]
    bufs, refs = refs[: len(rows_in)], refs[len(rows_in) :]
    vals, refs = refs[:n_out], refs[n_out:]
    mask, w, lse, packed, sems = refs
    xr = vals[0]
    qkv, lse_t, o, a_low = vals[-4:]
    core, _, _ = here()
    seq, width = xr.shape
    half, cols = seq // 2, own_out.shape[1]
    moves = Moves(sems)
    if first:
        at = [pl.ds(pl.multiple_of(c * half, half), half) for c in (core, 1 - core)]
        row_waits = [moves.start(src, xr.at[a]) for src, a in zip(rows_in, at)]
    else:
        row_waits = [
            [moves.start(src.at[pl.ds(i * half, half)], buf.at[pl.ds(i * half, half)]) for src, buf in zip(rows_in, bufs)]
            for i in range(2)
        ]
    bias_waits = [moves.start(ref.at[pl.ds(cols, BIAS_ROWS)], packed.at[n]) for n, ref in enumerate((a_bias, b_bias))]
    weight_waits = fetch_attn(moves, layer, own_qkv, own_out, a_refs, b_refs, w)
    mask_wait = moves.start(mask_in, mask)

    if first:
        wait_all(row_waits)
        moves.send(xr, outs[0])
    else:
        normed, recip = vals[1:3]
        h_in, f_mine, f_theirs = bufs
        for i in range(seq // 128):
            if i * 128 % half == 0:
                wait_all(row_waits[i * 128 // half])
            at = pl.ds(i * 128, 128)
            h = h_in[at] * gain[layer - 1, 0:1] + shift[layer - 1, 0:1]
            z = h + (f_mine[at].astype(f32) + f_theirs[at].astype(f32)) + ob[layer - 1, 1:2]
            new, n, r = norm_forward(z, gain[layer - 1, 1:2], shift[layer - 1, 1:2])
            xr[at] = new.astype(bf16)
            normed[at] = n
            recip[at] = r
        for n in range(3):
            moves.send(vals[n], outs[n])

    wait_all(bias_waits)
    a_row, b_row = (jnp.sum(packed[n, 0:3].astype(f32), 0, keepdims=True) for n in range(2))
    a_row = jnp.where(core == 0, own_bias[...], a_row)
    qb = []
    for i in range(2):
        base = (2 * layer + i) * cols
        qb.append(jnp.concatenate([a_row[:, base : base + cols], b_row[:, base : base + cols]], 1))
    wait_all(weight_waits)
    rows = 256
    for t in range(3):
        for i in range(seq // rows):
            at = pl.ds(i * rows, rows)
            acc = dot_nt(xr[at], w[t])
            if t != 1:
                acc = acc + qb[t // 2]
            qkv[t, at] = acc.astype(bf16)
    moves.send(qkv, outs[-4])
    mask_wait.wait()
    pairs = qkv.shape[2] // 128
    tile = 128
    lane = lax.broadcasted_iota(jnp.int32, (tile, 128), 1)

    @pl.loop(0, seq // tile)
    def _(i):
        at = pl.ds(pl.multiple_of(i * tile, tile), tile)
        bias = mask[at]
        keep = jnp.zeros((tile, 128), f32)
        for g in range(pairs):
            cs = pl.ds(g * 128, 128)
            q2 = qkv[0, at, cs] * jnp.asarray(1.0 / math.sqrt(HEAD_DIM), bf16)
            k2 = qkv[1, :, cs]
            v2 = qkv[2, :, cs]
            acc = None
            for hh in range(2):
                qm = jnp.where(lane_half(tile, hh), q2, jnp.zeros_like(q2))
                s = dot_nt(qm, k2) + bias
                top = jnp.max(s, -1, keepdims=True)
                e = jnp.exp(s - top)
                d = jnp.sum(e, -1, keepdims=True)
                pr = (e * (1.0 / d)).astype(bf16)
                keep = jnp.where(lane == 2 * g + hh, top + jnp.log(d), keep)
                vm = jnp.where(lane_half(seq, hh), v2, jnp.zeros_like(v2))
                got = dot_nn(pr, vm)
                acc = got if acc is None else acc + got
            o[at, cs] = acc.astype(bf16)
        lse[at] = keep

    moves.send(o, outs[-2])
    for i in range(seq // rows):
        at = pl.ds(i * rows, rows)
        a_low[at] = dot_nn(o[at], w[3]).astype(bf16)
        moves.send(a_low.at[at], outs[-1].at[at])
    lse_t[...] = jnp.transpose(lse[...])[0:8]
    moves.send(lse_t, outs[-3])
    moves.finish()


def attn_fwd(layer, rows_in, mask, bias, own_qkv, own_out, a_refs, b_refs):
    first = layer == 0
    seq, width, cols = mask.shape[0], own_out.shape[2], own_out.shape[1]
    wide = SLOTS * cols
    outs = [shape((seq, width), bf16)]
    if not first:
        outs += [shape((seq, width), f32), shape((seq, 1), f32)]
    outs += [
        shape((3, seq, wide), bf16),
        shape((8, seq), f32),
        shape((seq, wide), bf16),
        shape((seq, width), bf16),
    ]
    moving = 2 if first else 3
    small = rows_in[moving:]
    got = pl.pallas_call(
        functools.partial(attn_fwd_kernel, layer),
        out_shape=outs,
        in_specs=[ANY] * moving + [VMEM] * (len(small) + 1) + [ANY] * 13,
        out_specs=[HBM] * len(outs),
        scratch_shapes=[pltpu.VMEM(v.shape, v.dtype) for v in rows_in[:moving]]
        + [pltpu.VMEM(v.shape, v.dtype) for v in outs]
        + [
            pltpu.VMEM((seq, seq), f32),
            pltpu.VMEM((4, wide, width), bf16),
            pltpu.VMEM((seq, 128), f32),
            pltpu.VMEM((2, BIAS_ROWS, width), bf16),
            pltpu.SemaphoreType.DMA((MOVES,)),
        ],
        compiler_params=params(56),
        cost_estimate=cost(10),
        name="attn_fwd",
    )(*rows_in, bias[0], mask, *bias[1:], own_qkv, own_out, *a_refs, *b_refs)
    if first:
        xr, qkv, lse_t, o, a_low = got
        return xr, None, None, qkv, lse_t, o, a_low
    return got


def ff_fwd_kernel(layer, state_in, a_mine, a_theirs, ob, gain, shift, ub, own_up, own_down, *refs):
    moved, outs = refs[:5], refs[5:11]
    state, am, at_, hr, normed, recip, g, gp, f_low, wu, wd, sems = refs[11:]
    seq = state.shape[0]
    moves = Moves(sems)
    rows = 256
    tiles = [pl.ds(i * rows, rows) for i in range(seq // rows)]
    ins = ((state_in, state), (a_mine, am), (a_theirs, at_))
    row_waits = [[moves.start(src.at[at], dst.at[at]) for src, dst in ins] for at in tiles]
    up, down, n_t = fetch_ff(moves, layer, own_up, own_down, moved, wu, wd)
    up_waits = [up(k) for k in range(n_t)]
    down_waits = [down(k) for k in range(n_t)]
    half = wu.shape[1] // n_t
    for i, at in enumerate(tiles):
        wait_all(row_waits[i])
        entered = state[at].astype(f32)
        if layer:
            entered = entered * gain[layer - 1, 1:2] + shift[layer - 1, 1:2]
        z = entered + (am[at].astype(f32) + at_[at].astype(f32)) + ob[layer, 0:1]
        new, n, r = norm_forward(z, gain[layer, 0:1], shift[layer, 0:1])
        hr[at] = new.astype(bf16)
        normed[at] = n
        recip[at] = r
        for val, out in zip((hr, normed, recip), outs):
            moves.send(val.at[at], out.at[at])
    bias = jnp.concatenate([ub[k : k + 1] for k in range(ub.shape[0])], 1)
    for c in range(wu.shape[1] // CHUNK):
        cs = pl.ds(c * CHUNK, CHUNK)
        chunk_waits(up_waits, c, half)
        u = dot_nn(hr[...], wu[:, cs]) + bias[:, c * CHUNK : (c + 1) * CHUNK]
        phi = 0.5 * (1.0 + lax.erf(u * math.sqrt(0.5)))
        g[:, cs] = (u * phi).astype(bf16)
        gp[:, cs] = (phi + u * (jnp.exp(-0.5 * u * u) * (1.0 / math.sqrt(2 * math.pi)))).astype(bf16)
        moves.send(gp.at[:, cs], outs[4].at[:, cs])
    moves.send(g, outs[3])
    for copies in down_waits:
        wait_all(copies)
    for c in range(wd.shape[1] // CHUNK):
        cs = pl.ds(c * CHUNK, CHUNK)
        f_low[:, cs] = dot_nn(g[...], wd[:, cs]).astype(bf16)
        moves.send(f_low.at[:, cs], outs[5].at[:, cs])
    moves.finish()


def ff_fwd(layer, state, a_mine, a_theirs, norms, ub, own_up, own_down, moved):
    seq, width = state.shape
    n_t, half = ub.shape
    outs = [
        shape((seq, width), bf16),
        shape((seq, width), f32),
        shape((seq, 1), f32),
        shape((seq, n_t * half), bf16),
        shape((seq, n_t * half), bf16),
        shape((seq, width), bf16),
    ]
    return pl.pallas_call(
        functools.partial(ff_fwd_kernel, layer),
        out_shape=outs,
        in_specs=[ANY] * 3 + [VMEM] * 4 + [ANY] * 7,
        out_specs=[HBM] * len(outs),
        scratch_shapes=[pltpu.VMEM(v.shape, v.dtype) for v in (state, a_mine, a_theirs)]
        + [pltpu.VMEM(v.shape, v.dtype) for v in outs]
        + [
            pltpu.VMEM((width, n_t * half), bf16),
            pltpu.VMEM((n_t * half, width), bf16),
            pltpu.SemaphoreType.DMA((MOVES,)),
        ],
        compiler_params=params(56),
        cost_estimate=cost(8),
        name="ff_fwd",
    )(state, a_mine, a_theirs, *norms, ub, own_up, own_down, *moved)


def ff_bwd_kernel(last, layer, *refs):
    rows_in, refs = refs[:5], refs[5:]
    ob, gain, shift, gp_in, own_up, own_down = refs[:6]
    moved, refs = refs[6:11], refs[11:]
    n_out = 7 if last else 6
    outs, refs = refs[:n_out], refs[n_out:]
    bufs, gp, refs = refs[:5], refs[5], refs[6:]
    vals, refs = refs[:n_out], refs[n_out:]
    wu, wd, sems = refs
    dz2, dzr2, du, dh_low, small, ub_sum = vals[-6:]
    core, _, _ = here()
    seq = dz2.shape[0]
    moves = Moves(sems)
    rows = 256
    tiles = [pl.ds(i * rows, rows) for i in range(seq // rows)]
    if last:
        row_waits = [[moves.start(src.at[at], dst.at[at]) for src, dst in zip(rows_in[:3], bufs)] for at in tiles]
        cot_waits = [moves.start(src, dst) for src, dst in zip(rows_in[3:], bufs[3:])]
    else:
        row_waits = [[moves.start(src.at[at], dst.at[at]) for src, dst in zip(rows_in, bufs)] for at in tiles]
    up, down, n_t = fetch_ff(moves, layer, own_up, own_down, moved, wu, wd)
    half = wu.shape[1] // n_t
    down_waits, gp_waits = [], []
    for k in range(n_t):
        down_waits.append(down(k))
        for c in range(gp.shape[1] // CHUNK):
            if k * half <= c * CHUNK < (k + 1) * half:
                cs = pl.ds(c * CHUNK, CHUNK)
                gp_waits.append(moves.start(gp_in.at[:, cs], gp.at[:, cs]))
    up_waits = [up(k) for k in range(n_t)]
    small[...] = jnp.zeros_like(small)
    for i, at in enumerate(tiles):
        wait_all(row_waits[i])
        if last:
            h_in, f_mine, f_theirs, c_mine, c_theirs = bufs
            h = h_in[at] * gain[layer, 0:1] + shift[layer, 0:1]
            z = h + (f_mine[at].astype(f32) + f_theirs[at].astype(f32)) + ob[layer, 1:2]
            new, n, r = norm_forward(z, gain[layer, 1:2], shift[layer, 1:2])
            vals[0][at] = new.astype(bf16)
            if i == 0:
                wait_all(cot_waits)
            dy = jnp.where(core == i, c_mine[...], c_theirs[...]).astype(f32)
        else:
            dz_in, x_mine, x_theirs, normed, recip = bufs
            dy = dz_in[at] + (x_mine[at].astype(f32) + x_theirs[at].astype(f32))
            n, r = normed[at], recip[at]
        dz = norm_backward(dy, n, r, gain[layer, 1:2])
        dz2[at] = dz
        low = dz.astype(bf16)
        dzr2[at] = low
        if last:
            moves.send(vals[0].at[at], outs[0].at[at])
        moves.send(dz2.at[at], outs[-6].at[at])
        moves.send(dzr2.at[at], outs[-5].at[at])
        small[0:1] += jnp.sum(dy * n, 0, keepdims=True)
        small[1:2] += jnp.sum(dy, 0, keepdims=True)
        small[2:3] += jnp.sum(dz, 0, keepdims=True)
    for c in range(wd.shape[0] // CHUNK):
        cs = pl.ds(c * CHUNK, CHUNK)
        chunk_waits(down_waits, c, half)
        gp_waits[c].wait()
        back = (dot_nt(dzr2[...], wd[cs]) * gp[:, cs].astype(f32)).astype(bf16)
        du[:, cs] = back
        ub_sum[:, cs] = jnp.sum(back.astype(f32), 0, keepdims=True)
        moves.send(du.at[:, cs], outs[-4].at[:, cs])
    moves.send(small, outs[-2])
    moves.send(ub_sum, outs[-1])
    for copies in up_waits:
        wait_all(copies)
    for c in range(wu.shape[0] // CHUNK):
        cs = pl.ds(c * CHUNK, CHUNK)
        dh_low[:, cs] = dot_nt(du[...], wu[cs]).astype(bf16)
        moves.send(dh_low.at[:, cs], outs[-3].at[:, cs])
    moves.finish()


def ff_bwd(layer, rows_in, norms, gp, own_up, own_down, moved, last):
    width = own_up.shape[1]
    seq, wide = gp.shape
    outs = [
        shape((seq, width), f32),
        shape((seq, width), bf16),
        shape((seq, wide), bf16),
        shape((seq, width), bf16),
        shape((8, width), f32),
        shape((1, wide), f32),
    ]
    if last:
        outs = [shape((seq, width), bf16)] + outs
    return pl.pallas_call(
        functools.partial(ff_bwd_kernel, last, layer),
        out_shape=outs,
        in_specs=[ANY] * 5 + [VMEM] * 3 + [ANY] * 8,
        out_specs=[HBM] * len(outs),
        scratch_shapes=[pltpu.VMEM(v.shape, v.dtype) for v in (*rows_in, gp)]
        + [pltpu.VMEM(v.shape, v.dtype) for v in outs]
        + [
            pltpu.VMEM((width, wide), bf16),
            pltpu.VMEM((wide, width), bf16),
            pltpu.SemaphoreType.DMA((MOVES,)),
        ],
        compiler_params=params(56),
        cost_estimate=cost(9),
        name="ff_bwd",
    )(*rows_in, *norms, gp, own_up, own_down, *moved)


SEND = ((2, 3), (1, 3))
NEXT = (1, 2)


def ff_dw_kernel(z_first, *refs):
    ins, outs = refs[:4], refs[4:-8]
    g, du, hr, dzr2, su, sd, in_sems, sems = refs[-8:]
    _, place, z = here()
    n_t, width, half = su.shape
    part, rows = width // 4, half // 4

    def target(s, j):
        send, nxt, keep = outs[3 * s : 3 * s + 3]
        if j in SEND[s]:
            return send.at[SEND[s].index(j)]
        return nxt if j == NEXT[s] else keep

    def quarter(k):
        return lax.rem(z + n_t - k, n_t)

    copies = []

    def start(src, dst):
        copies.append(pltpu.make_async_copy(src, dst, sems.at[len(copies)]))
        copies[-1].start()

    moves = Moves(in_sems)
    pair = 2 * half
    hr_wait = moves.start(ins[2], hr)
    du_waits = [moves.start(ins[1].at[:, pl.ds(m * pair, pair)], du.at[:, pl.ds(m * pair, pair)]) for m in range(n_t // 2)]
    dzr2_wait = moves.start(ins[3], dzr2)
    g_waits = [moves.start(ins[0].at[:, pl.ds(m * pair, pair)], g.at[:, pl.ds(m * pair, pair)]) for m in range(n_t // 2)]
    hr_wait.wait()
    for m in range(n_t // 2):
        du_waits[m].wait()
        for c in range(width // CHUNK):
            at = pl.ds(c * CHUNK, CHUNK)
            got = dot_tn(hr[:, at], du[:, m * pair : (m + 1) * pair]).astype(bf16)
            for k in (2 * m, 2 * m + 1):
                su[k, at] = got[:, (k - 2 * m) * half : (k - 2 * m + 1) * half]
        if z_first:
            for k in (2 * m, 2 * m + 1):
                for p in range(4):
                    start(su.at[k, pl.ds(p * part, part)], outs[0].at[quarter(k), p, 0])
    if not z_first:
        for j in range(4):
            at = pl.ds(pl.multiple_of((j ^ place) * part, part), part)
            start(su.at[:, at], target(0, j))
    dzr2_wait.wait()
    for m in range(n_t // 2):
        g_waits[m].wait()
        for c in range(pair // CHUNK):
            at = pl.ds(m * pair + c * CHUNK, CHUNK)
            sd[at] = dot_tn(g[:, at], dzr2[...]).astype(bf16)
        if z_first:
            for k in (2 * m, 2 * m + 1):
                for p in range(4):
                    for n in range(2):
                        start(
                            sd.at[pl.ds(k * half + p * rows, rows), pl.ds(n * half, half)],
                            outs[0].at[quarter(k), p, 1, pl.ds(n * rows, rows)],
                        )
    if not z_first:
        for j in range(4):
            for k in range(n_t):
                at = pl.ds(pl.multiple_of(k * half + (j ^ place) * rows, rows), rows)
                for n in range(2):
                    start(sd.at[at, pl.ds(n * half, half)], target(1, j).at[k, pl.ds(n * rows, rows)])
    for c in copies:
        c.wait()


def ff_dw(g, du, hr, dzr2, z_first):
    width = hr.shape[1]
    half = width // 2
    n_t = g.shape[1] // half
    one = (n_t, width // 4, half)
    if z_first:
        outs = [shape((n_t, 4, 2, width // 4, half), bf16)]
    else:
        outs = [shape((2,) + one, bf16), shape(one, bf16), shape(one, bf16)] * 2
    return pl.pallas_call(
        functools.partial(ff_dw_kernel, z_first),
        out_shape=outs,
        in_specs=[ANY] * 4,
        out_specs=[HBM] * len(outs),
        scratch_shapes=[pltpu.VMEM(v.shape, v.dtype) for v in (g, du, hr, dzr2)]
        + [
            pltpu.VMEM((n_t, width, half), bf16),
            pltpu.VMEM((n_t * half, width), bf16),
            pltpu.SemaphoreType.DMA((2 + 2 * n_t,)),
            pltpu.SemaphoreType.DMA((12 * n_t,)),
        ],
        compiler_params=params(56),
        cost_estimate=cost(5),
        name="ff_dw",
    )(g, du, hr, dzr2)


def attn_bwd_kernel(layer, *refs):
    rows_in, refs = refs[:4], refs[4:]
    recip, gain, qkv_in, lse_t, o, mask_in, own_qkv, own_out = refs[:8]
    a_refs, b_refs, refs = refs[8:12], refs[12:16], refs[16:]
    outs, refs = refs[:5], refs[5:]
    bufs, refs = refs[:4], refs[4:]
    dz1, dzr1, d4, dx_low, small, qkv, mask, w, do, sems = refs
    dz2, h_mine, h_theirs, normed = bufs
    seq, width = dz1.shape
    moves = Moves(sems)
    half = seq // 2
    row_waits = []
    for i in range(2):
        at = pl.ds(i * half, half)
        row_waits.append([moves.start(src.at[at], dst.at[at]) for src, dst in zip(rows_in, bufs)])
    weight_waits = fetch_attn(moves, layer, own_qkv, own_out, a_refs, b_refs, w)
    qkv_wait = moves.start(qkv_in, qkv)
    mask_wait = moves.start(mask_in, mask)
    o_wait = moves.start(o, d4.at[3])
    small[...] = jnp.zeros_like(small)
    for i in range(seq // 128):
        if i * 128 % half == 0:
            wait_all(row_waits[i * 128 // half])
        at = pl.ds(i * 128, 128)
        dh = dz2[at] + (h_mine[at].astype(f32) + h_theirs[at].astype(f32))
        n = normed[at]
        dz = norm_backward(dh, n, recip[at], gain[layer, 0:1])
        dz1[at] = dz
        dzr1[at] = dz.astype(bf16)
        small[0:1] += jnp.sum(dh * n, 0, keepdims=True)
        small[1:2] += jnp.sum(dh, 0, keepdims=True)
        small[2:3] += jnp.sum(dz, 0, keepdims=True)
    moves.send(dz1, outs[0])
    moves.send(dzr1, outs[1])
    wait_all(weight_waits)
    rows = 256
    for i in range(seq // rows):
        at = pl.ds(i * rows, rows)
        do[at] = dot_nt(dzr1[at], w[3]).astype(bf16)
    qkv_wait.wait()
    mask_wait.wait()
    pairs = qkv.shape[2] // 128
    tile = 256
    scale = 1.0 / math.sqrt(HEAD_DIM)
    for g in range(pairs):
        cs = pl.ds(g * 128, 128)
        k2 = qkv[1, :, cs] * jnp.asarray(scale, bf16)
        v2 = qkv[2, :, cs]
        dv = dk = None
        for i in range(seq // tile):
            at = pl.ds(i * tile, tile)
            q2 = qkv[0, at, cs]
            do2 = do[at, cs]
            bias = mask[:, at]
            dq = None
            for hh in range(2):
                all_half = lane_half(seq, hh)
                tile_half = lane_half(tile, hh)
                km = jnp.where(all_half, k2, jnp.zeros_like(k2))
                vm = jnp.where(all_half, v2, jnp.zeros_like(v2))
                qm = jnp.where(tile_half, q2, jnp.zeros_like(q2))
                dom = jnp.where(tile_half, do2, jnp.zeros_like(do2))
                head = 2 * g + hh
                s = dot_nt(km, q2) + bias
                pr = jnp.exp(s - lse_t[head : head + 1, at])
                dp = dot_nt(vm, do2)
                delta = jnp.sum(pr * dp, 0, keepdims=True)
                ds = (pr * (dp - delta)).astype(bf16)
                got_v = dot_nn(pr.astype(bf16), dom)
                got_k = dot_nn(ds, qm)
                got_q = dot_nn(jnp.transpose(km), ds)
                dv = got_v if dv is None else dv + got_v
                dk = got_k if dk is None else dk + got_k
                dq = got_q if dq is None else dq + got_q
            dqr = jnp.transpose(dq)
            d4[0, at, cs] = dqr.astype(bf16)
        d4[1, :, cs] = (dk * scale).astype(bf16)
        d4[2, :, cs] = dv.astype(bf16)
    o_wait.wait()
    moves.send(d4, outs[2])
    wide = d4.shape[2]
    small[3:4, 0:wide] = jnp.sum(d4[0].astype(f32), 0, keepdims=True)
    small[3:4, wide : 2 * wide] = jnp.sum(d4[2].astype(f32), 0, keepdims=True)
    for i in range(seq // rows):
        at = pl.ds(i * rows, rows)
        acc = dot_nn(d4[0, at], w[0]) + dot_nn(d4[1, at], w[1]) + dot_nn(d4[2, at], w[2])
        dx_low[at] = acc.astype(bf16)
        moves.send(dx_low.at[at], outs[3].at[at])
    moves.send(small, outs[4])
    moves.finish()


def attn_bwd(layer, dz2, h_mine, h_theirs, normed, recip, gain, qkv, lse_t, o, mask, own_qkv, own_out, a_refs, b_refs):
    seq, width = dz2.shape
    wide = qkv.shape[2]
    outs = [
        shape((seq, width), f32),
        shape((seq, width), bf16),
        shape((4, seq, wide), bf16),
        shape((seq, width), bf16),
        shape((8, width), f32),
    ]
    rows_in = (dz2, h_mine, h_theirs, normed)
    return pl.pallas_call(
        functools.partial(attn_bwd_kernel, layer),
        out_shape=outs,
        in_specs=[ANY] * 4 + [VMEM] * 2 + [ANY, VMEM] + [ANY] * 12,
        out_specs=[HBM] * 5,
        scratch_shapes=[pltpu.VMEM(v.shape, v.dtype) for v in (*rows_in, *outs, qkv, mask)]
        + [
            pltpu.VMEM((4, wide, width), bf16),
            pltpu.VMEM((seq, wide), bf16),
            pltpu.SemaphoreType.DMA((MOVES,)),
        ],
        compiler_params=params(56),
        cost_estimate=cost(12),
        name="attn_bwd",
    )(*rows_in, recip, gain, qkv, lse_t, o, mask, own_qkv, own_out, *a_refs, *b_refs)


def attn_dw_kernel(*refs):
    ins, outs = refs[:3], refs[3:5]
    d4, right, full, sems = refs[5:]
    core, place, _ = here()
    cols = d4.shape[2] // SLOTS
    count, half = outs[0].shape[3:]
    moves = Moves(sems)
    waits = [moves.start(ins[1], right.at[0]), moves.start(ins[2], right.at[1])]
    d4_waits = [moves.start(ins[0].at[j ^ place], d4.at[j ^ place]) for j in range(4)]
    wait_all(waits)
    for j in range(4):
        t = j ^ place
        d4_waits[j].wait()
        full[j] = dot_tn(d4[t], right[t // 3]).astype(bf16)
        for s in range(SLOTS):
            for out, c in zip(outs, (core, 1 - core)):
                at = pl.ds(pl.multiple_of(s * cols + c * count, count), count)
                for n in range(2):
                    moves.send(full.at[j, at, pl.ds(n * half, half)], out.at[s, j, n])
    moves.finish()


def attn_dw(d4, xr, dzr1):
    wide, width = d4.shape[2], xr.shape[1]
    out = shape((SLOTS, 4, 2, wide // 4, width // 2), bf16)
    return pl.pallas_call(
        attn_dw_kernel,
        out_shape=[out, out],
        in_specs=[ANY] * 3,
        out_specs=[HBM] * 2,
        scratch_shapes=[
            pltpu.VMEM(d4.shape, bf16),
            pltpu.VMEM((2,) + xr.shape, bf16),
            pltpu.VMEM((4, wide, width), bf16),
            pltpu.SemaphoreType.DMA((MOVES,)),
        ],
        compiler_params=params(56),
        cost_estimate=cost(3.5),
        name="attn_dw",
    )(d4, xr, dzr1)


def arrange_kernel(mine, theirs, *outs):
    first = here()[0] == 0
    for ref, same in ((mine, first), (theirs, jnp.logical_not(first))):
        for s in range(SLOTS):
            k = jnp.where(same, s, 3 - s)
            for n in range(2):
                send, nxt, keep = outs[3 * n : 3 * n + 3]
                for j in range(4):
                    val = ref[s, j, n]
                    if j in SEND[n]:
                        send[SEND[n].index(j), k] = val
                    elif j == NEXT[n]:
                        nxt[k] = val
                    else:
                        keep[k] = val


def low_sum(*parts):
    total = parts[0].astype(f32)
    for v in parts[1:]:
        total = total + v.astype(f32)
    return total.astype(bf16)


def small_call(kernel, outs, us, name, *ins):
    n, m = len(ins), len(outs)

    def body(*refs):
        bufs, sems = refs[n + m : -1], refs[-1]
        copies = [pltpu.make_async_copy(src, dst, sems.at[i]) for i, (src, dst) in enumerate(zip(refs[:n], bufs))]
        for c in copies:
            c.start()
        for c in copies:
            c.wait()
        kernel(*bufs, *refs[n : n + m])

    return pl.pallas_call(
        body,
        out_shape=outs,
        in_specs=[ANY] * n,
        out_specs=[VMEM] * m,
        scratch_shapes=[pltpu.VMEM(v.shape, v.dtype) for v in ins] + [pltpu.SemaphoreType.DMA((n,))],
        compiler_params=params(16),
        cost_estimate=cost(us * 0.01),
        name=name,
    )(*ins)


def second_kernel(nxt_a, got_a, nxt_b, got_b, out_a, out_b):
    out_a[...] = low_sum(nxt_a[...], got_a[1])
    out_b[...] = low_sum(nxt_b[...], got_b[1])


def third_kernel(*refs):
    out = refs[-1]
    n_t = out.shape[0]
    z = here()[2]
    row = 0
    for c in range(len(refs) // 6):
        ins = refs[6 * c : 6 * c + 6]
        rows = ins[0].shape[1]
        for n in range(2):
            keep, got, more = ins[3 * n : 3 * n + 3]
            for k in range(n_t):
                q = lax.rem(z + n_t - k, n_t)
                out[q, n, row : row + rows] = low_sum(keep[k], got[0, k], more[k])
        row += rows


def merge_kernel(keep_a, got_a, more_a, keep_b, got_b, more_b, attn, out):
    rows = keep_a.shape[1]
    out[0, :rows] = low_sum(keep_a[0], got_a[0, 0], more_a[0])
    out[1, :rows] = low_sum(keep_b[0], got_b[0, 0], more_b[0])
    out[:, rows:] = attn[...]


def split_kernel(every, *outs):
    _, place, _ = here()
    for s in range(SLOTS):
        send, nxt, keep = outs[3 * s : 3 * s + 3]
        for j in range(4):
            val = every[j ^ place, s]
            if j in SEND[s]:
                send[SEND[s].index(j), 0] = val
            elif j == NEXT[s]:
                nxt[0] = val
            else:
                keep[0] = val


def pick_kernel(every, out, ub):
    n_t, rows = every.shape[0], out.shape[2]
    z = here()[2]
    for k in range(n_t):
        q = lax.rem(z + n_t - k, n_t)
        ub[k : k + 1] = jnp.sum(every[q, 2 * rows : 2 * rows + 3].astype(f32), 0, keepdims=True)
        if k:
            for n in range(2):
                out[n, k - 1] = every[q, n * rows : (n + 1) * rows]


def pack_kernel(*refs):
    out = refs[-1]
    layers = (len(refs) - 1) // 3
    small1, small2, ub = refs[:layers], refs[layers : 2 * layers], refs[2 * layers : 3 * layers]
    core, _, z = here()
    half = out.shape[1] // 2
    n_t = ub[0].shape[1] // half
    cols = half // 2
    once = jnp.where(core == 0, 1.0, 0.0).astype(f32)
    for l in range(layers):
        out[6 * l : 6 * l + 3] = small1[l][0:3] * once
        out[6 * l + 3 : 6 * l + 6] = small2[l][0:3] * once
    none = jnp.zeros((1, half), f32)
    for l in range(layers):
        for q in range(n_t):
            row = none
            for k in range(n_t):
                row = jnp.where(lax.rem(z + n_t - k, n_t) == q, ub[l][:, k * half : (k + 1) * half], row)
            left = jnp.where(core == 0, row, none)
            out[6 * layers + n_t * l + q : 6 * layers + n_t * l + q + 1] = jnp.concatenate([left, row - left], 1)
    slot_k = (jnp.where(core == 0, 0, 3), jnp.where(core == 0, 1, 2))
    none = jnp.zeros((1, cols), f32)
    for q in range(n_t):
        parts = []
        for l in range(layers):
            for i in range(2):
                row = none
                for s in range(SLOTS):
                    at = i * half + s * cols
                    here_q = lax.rem(z + n_t - slot_k[s], n_t) == q
                    row = jnp.where(here_q, small1[l][3:4, at : at + cols], row)
                parts.append(row)
        at = (6 + n_t) * layers + q
        out[at : at + 1] = jnp.concatenate(parts, 1)


def unpack_kernel(flat, gain, shift, bias, up, qv):
    layers, _, cols = qv.shape
    n_t = (flat.shape[0] - 6 * layers) // (layers + 1)
    z = here()[2]

    def own(first):
        row = flat[first : first + 1]
        for q in range(1, n_t):
            row = jnp.where(z == q, flat[first + q : first + q + 1], row)
        return row

    row = own((6 + n_t) * layers)
    for l in range(layers):
        for n in range(2):
            at = 6 * l + 3 * n
            gain[l, n : n + 1] = flat[at : at + 1]
            shift[l, n : n + 1] = flat[at + 1 : at + 2]
            bias[l, n : n + 1] = flat[at + 2 : at + 3]
            qv[l, n : n + 1] = row[:, (2 * l + n) * cols : (2 * l + n + 1) * cols]
        up[l : l + 1] = own(6 * layers + n_t * l)


def out_kernel(layer, n_alias, *refs):
    mine, theirs = refs[:4], refs[4:8]
    up, down, qkv, out, wide, sems = refs[8 + n_alias :]
    core, place, _ = here()
    part, half, cols = up.shape[1] // 4, up.shape[2] // 2, out.shape[1]
    rows, count = half // 4, cols // 2
    copies = []

    def start(src, dst):
        copies.append(pltpu.make_async_copy(src, dst, sems.at[len(copies)]))
        copies[-1].start()

    for n, (pieces, c) in enumerate(((mine, core), (theirs, 1 - core))):
        off = pl.multiple_of(c * half, half)
        for j, ref in enumerate(pieces):
            p = j ^ place
            buf = wide.at[n, j]
            buf[...] = ref[...].astype(f32)
            start(buf.at[0, pl.ds(0, part)], up.at[layer, pl.ds(pl.multiple_of(p * part, part), part), pl.ds(off, half)])
            for m in range(2):
                lanes = pl.ds(m * half, half)
                at = pl.ds(pl.multiple_of(c * half + p * rows, rows), rows)
                start(buf.at[1, pl.ds(m * rows, rows)], down.at[layer, at, lanes])
                src, sem = buf.at[m, pl.ds(part, count)], sems.at[len(copies)]
                at = pl.ds(pl.multiple_of(c * count, count), count)
                to_qkv = pltpu.make_async_copy(src, qkv.at[layer, jnp.minimum(p, 2), at, lanes], sem)
                to_out = pltpu.make_async_copy(src, out.at[layer, at, lanes], sem)

                @pl.when(p < 3)
                def _(to_qkv=to_qkv):
                    to_qkv.start()

                @pl.when(p == 3)
                def _(to_out=to_out):
                    to_out.start()

                copies.append(to_out)
    for c in copies:
        c.wait()


def outputs(layer, dims, mine, theirs, before):
    before = list(before or [])
    n = len(mine) + len(theirs)
    return pl.pallas_call(
        functools.partial(out_kernel, layer, len(before)),
        out_shape=[shape(d, f32) for d in dims],
        in_specs=[VMEM] * n + [HBM] * len(before),
        out_specs=[HBM] * len(dims),
        scratch_shapes=[
            pltpu.VMEM((2, 4) + mine[0].shape, f32),
            pltpu.SemaphoreType.DMA((5 * n,)),
        ],
        input_output_aliases={n + i: i for i in range(len(before))},
        compiler_params=params(24),
        cost_estimate=cost(4),
        name="gradients_out",
    )(*mine, *theirs, *before)


def after(v, *others):
    return lax.optimization_barrier((v, *others))[0]


def local(
    block_input,
    w_qkv,
    qv_bias,
    w_out,
    out_bias,
    w_up,
    up_bias,
    w_down,
    norm_gain,
    norm_shift,
    segment_ids,
    slot_counts,
    cotangent,
):
    layers, width, _, cols = w_qkv.shape
    hidden = w_up.shape[2]
    seq = segment_ids.shape[1]
    n_dp, n_t = lax.axis_size("dp"), lax.axis_size("tensor")
    dp, z = lax.axis_index("dp"), lax.axis_index("tensor")
    core, place = dp & 1, (dp >> 1) & 3
    first = core == 0
    part, half = hidden // 4, hidden // 2
    norms_in = (out_bias, norm_gain, norm_shift)

    def send(v, axis, pairs, name):
        with jax.named_scope(name):
            return lax.ppermute(v, axis, pairs)

    def flip(v, bits, name, odd=False):
        return send(v, "dp", [(i, i ^ bits) for i in range(n_dp) if not odd or i & 1], name)

    def across(v, name):
        return flip(v, 1, name)

    def shift(v, by, name):
        pairs = []
        for i in range(n_dp):
            move = by[i & 1]
            if move:
                pairs += [(i * n_t + k, i * n_t + (k + move) % n_t) for k in range(n_t)]
        return send(v, ("dp", "tensor"), pairs, name)

    def swap(v, name):
        pairs = []
        for i in range(n_dp):
            for k in range(n_t):
                if (i & 1) != (k & 1):
                    pairs.append((i * n_t + k, (i ^ 1) * n_t + (k ^ 1)))
        moved = send(v, ("dp", "tensor"), pairs, name)
        return jnp.where(core == (z & 1), v, moved)

    own_qkv = jnp.transpose(w_qkv, (0, 2, 3, 1))
    own_bias = qv_bias.reshape(1, -1)

    def attn_over_z(piece, l):
        return shift(piece, (1, 2), f"attn{l}_z_b"), shift(piece, (0, 3), f"attn{l}_z_a")

    def attn_over_xy(b, a, l, *late):
        name = f"attn{l}_"
        bx = flip(b, 2, name + "b_x")
        by = flip(b, 4, name + "b_y")
        ay = flip(a, 4, name + "a_y", True)
        ax = flip(a, 2, name + "a_x", True)
        bd = flip(after(bx, *late), 4, name + "b_xy")
        ad = flip(after(ay, *late), 2, name + "a_yx", True)
        return (a, ax, ay, ad), (b, bx, by, bd)

    def ff_over_xy(own, l):
        x, y = flip(own, 2, f"ff{l}_x"), flip(own, 4, f"ff{l}_y")
        return own, x, y, flip(x[0], 4, f"ff{l}_xy"), flip(y[1], 2, f"ff{l}_yx")

    x_mine = swap(block_input, "x_swap")
    attn_piece, ff_piece, packed = prepare(own_qkv, w_out, w_up, w_down, up_bias, own_bias, segment_ids, slot_counts)
    mask, mask_t = masks(packed, across(packed, "seg"))
    x_theirs = across(x_mine, "x_across")

    def ff_over_z(l, *late):
        with jax.named_scope(f"ff{l}_z"):
            return lax.all_gather(after(ff_piece[l], *late), "tensor", axis=0)

    def take(every, l, *late):
        outs = [shape((2, n_t - 1, part, half), bf16), shape((n_t, half), f32)]
        own, ub = small_call(pick_kernel, outs, 1.5, "pick_quarters", after(every, *late))
        return ff_over_xy(own, l), ub

    attn0_z = attn_over_z(attn_piece[0], 0)
    ff0_z = ff_over_z(0, x_mine)
    attn0 = attn_over_xy(after(attn0_z[0], mask, x_mine), after(attn0_z[1], mask, x_mine), 0, x_theirs)
    attn1_z = attn_over_z(after(attn_piece[1], *attn0[0], *attn0[1]), 1)
    ff1_z = ff_over_z(1, *attn1_z)
    ff0, ub0 = take(ff0_z, 0, *attn0[0], *attn0[1])
    attn1 = attn_over_xy(*attn1_z, 1)
    attn_w, ff_z = [attn0, attn1], [ff0_z, ff1_z]
    bias = (own_bias,) + attn0_z[::-1]

    rows_in = (after(x_mine, ff0[0]), x_theirs)
    saved = []
    ff_w, ubs = [ff0], [ub0]
    for l in range(layers):
        xr, n2, r2, qkv, lse_t, o, a_low = attn_fwd(l, rows_in, mask, bias, own_qkv, w_out, *attn_w[l])
        state = n2 if l else xr
        if l:
            saved[l - 1] += (n2, r2)
        else:
            ff1, ub1 = take(ff1_z, 1, *ff0)
            ff_w.append(ff1)
            ubs.append(ub1)
            state = after(state, ff1[0], *attn1[0], *attn1[1])
        hr, n1, r1, g, gp, f_low = ff_fwd(
            l, state, a_low, across(a_low, f"a{l}"), norms_in, ubs[l], w_up, w_down, ff_w[l]
        )
        saved.append((xr, qkv, lse_t, o, hr, n1, r1, g, gp))
        rows_in = (after(n1, ff1[1], ff1[2]), f_low, across(f_low, f"f{l}")) + norms_in

    class Sums:
        def __init__(self, name):
            self.name = name

        def first(self, pieces):
            self.pieces = pieces
            self.got = (flip(pieces[0], 4, self.name + "_1a"), flip(pieces[3], 2, self.name + "_1b"))
            return self

        def second(self, *late):
            p, got = self.pieces, self.got
            nxt = after(p[1], *late)
            outs = [shape(nxt.shape, bf16)] * 2
            self.sec = small_call(second_kernel, outs, 1.2, "add_second", nxt, got[0], p[4], got[1])
            self.more = (flip(self.sec[0], 2, self.name + "_2a"), flip(self.sec[1], 4, self.name + "_2b"))
            return self

        def parts(self):
            p, got, more = self.pieces, self.got, self.more
            return [p[2], got[0], more[0], p[5], got[1], more[1]]

    def over_z(every):
        with jax.named_scope("sums_z"):
            return lax.psum_scatter(every, "tensor", scatter_dimension=0)

    def third(chunks, *late):
        ins = [v for c in chunks for v in c.parts()]
        rows = sum(c.pieces[2].shape[1] for c in chunks)
        outs = [shape((n_t, 2, rows, half), bf16)]
        (every,) = small_call(third_kernel, outs, 1.5, "add_third", after(ins[0], *late), *ins[1:])
        return every, over_z(every)

    def attn_first(name, mine, theirs):
        one = (n_t, cols // 2, half)
        outs = [shape((2,) + one, bf16), shape(one, bf16), shape(one, bf16)] * 2
        return Sums(name).first(small_call(arrange_kernel, outs, 1.5, "arrange", mine, theirs))

    def split(total, *late):
        one = (1, part, half)
        outs = [shape((2,) + one, bf16), shape(one, bf16), shape(one, bf16)] * 2
        return Sums("gf1").first(small_call(split_kernel, outs, 1.5, "split_pieces", after(total, *late)))

    def spread(total, name):
        bits = 8
        while bits < n_dp:
            total = low_sum(total, flip(total, bits, name + "_rest"))
            bits *= 2
        mine = [total] + [flip(total, bits, f"{name}_c{bits}") for bits in (2, 4, 6)]
        return mine, [across(v, f"{name}_cc{n}") for n, v in enumerate(mine)]

    def finish(l, mine, theirs, before, *late):
        dims = [(layers, width, hidden), (layers, hidden, width), (layers, 3, cols, width), (layers, cols, width)]
        return outputs(l, dims, [after(mine[0], *late)] + mine[1:], theirs, before)

    a1 = None
    smalls = []
    for l in reversed(range(layers)):
        last = l == layers - 1
        xr, qkv, lse_t, o, hr, n1, r1, g, gp = saved[l][:9]
        if last:
            c_mine = swap(cotangent, "cot_swap")
            ff_rows = rows_in[:3] + (c_mine, across(c_mine, "cot_across"))
        else:
            ff_rows = (dz1, dx_low, across(dx_low, f"dx{l}")) + saved[l][9:]
        got = ff_bwd(l, ff_rows, norms_in, gp, w_up, w_down, ff_w[l], last)
        if last:
            out_half = lax.dynamic_slice_in_dim(got[0], core * (seq // 2), seq // 2, 0)
            got = got[1:]
        dz2, dzr2, du, dh_low, small2, ub_sum = got
        if a1:
            a1.second(dzr2)
            dzr2 = after(dzr2, *a1.sec)
        ff_pieces = ff_dw(g, du, hr, dzr2, last)
        if last:
            f1_total = over_z(ff_pieces[0])
        else:
            first_out = [after(ff_pieces[0], *a1.more), *ff_pieces[1:3], after(ff_pieces[3], *a1.more), *ff_pieces[4:]]
            f0 = Sums("gf0").first(first_out)
        dh_theirs = across(dh_low, f"dh{l}")
        dz2 = after(dz2, ff_pieces[0])
        if a1:
            dz2 = after(dz2, *a1.more)
        dz1, dzr1, d4, dx_low, small1 = attn_bwd(
            l, dz2, dh_low, dh_theirs, n1, r1, norm_gain, qkv, lse_t, o, mask_t, own_qkv, w_out, *attn_w[l]
        )
        at_pieces = attn_dw(d4, xr, dzr1)
        at_theirs = across(at_pieces[1], f"ga{l}_core")
        if last:
            a1 = attn_first("ga1", at_pieces[0], at_theirs)
            dz1 = after(dz1, a1.pieces[0])
        smalls.append((small1, small2, ub_sum))
    smalls = smalls[::-1]

    dx = dz1 + (dx_low.astype(f32) + across(dx_low, "dx_last").astype(f32))
    input_grad = swap(lax.dynamic_slice_in_dim(dx, core * (seq // 2), seq // 2, 0), "grad_swap")

    def more_flat(flat, axis, bits, *late):
        n = lax.axis_size(axis)
        return flat + send(after(flat, *late), axis, [(i, i ^ bits) for i in range(n)], f"flat_{axis}{bits}")

    n_rows = (6 + n_t) * layers + n_t
    (flat,) = small_call(
        pack_kernel,
        [shape((n_rows, width), f32)],
        1.5,
        "pack_small",
        *[g[0] for g in smalls],
        *[g[1] for g in smalls],
        *[g[2] for g in smalls],
    )
    f0.second(at_pieces[0], dx)
    mixed = swap(after(out_half, *f0.sec), "mixed_swap")
    a0 = attn_first("ga0", after(at_pieces[0], *f0.sec), at_theirs)
    a1_every, a1_total = third([a1], a0.pieces[0])
    flat = more_flat(flat, "dp", 1, a1_every)
    a0.second(flat)
    flat = more_flat(flat, "dp", 2, *a0.sec)
    l0_every, l0_total = third([f0, a0], flat, input_grad, mixed)
    f1 = split(f1_total, l0_every)
    flat = more_flat(flat, "dp", 4, f1.pieces[0])
    bits = 8
    while bits < n_dp:
        flat = more_flat(flat, "dp", bits)
        bits *= 2
    f1.second(flat)
    flat = more_flat(flat, "tensor", 1, *f1.sec)
    ins = f1.parts()
    ins[0] = after(ins[0], flat)
    (l1_total,) = small_call(merge_kernel, [shape((2, part + cols // 2, half), bf16)], 1.5, "merge", *ins, a1_total)
    flat = more_flat(flat, "tensor", 2, l1_total)
    l1 = spread(l1_total, "l1")
    l0 = spread(after(l0_total, *l1[0]), "l0")
    grads = finish(1, *l1, None, l0_total, flat)
    grads = finish(0, *l0, grads)
    grad_gain, grad_shift, grad_out_bias, grad_up_bias, grad_qv_bias = small_call(
        unpack_kernel,
        [shape((layers, 2, width), f32)] * 3 + [shape((layers, hidden), f32), shape((layers, 2, cols), f32)],
        1.5,
        "unpack_small",
        flat,
    )
    return (
        mixed,
        input_grad,
        jnp.transpose(grads[2], (0, 3, 1, 2)),
        grad_qv_bias,
        grads[3],
        grad_out_bias,
        grads[0],
        grad_up_bias,
        grads[1],
        grad_gain,
        grad_shift,
    )


def solution(mesh):
    placed = (
        P(("dp", "tensor"), None),
        P(None, None, None, "tensor"),
        P(None, None, "tensor"),
        P(None, "tensor", None),
        P(),
        P(None, None, "tensor"),
        P(None, "tensor"),
        P(None, "tensor", None),
        P(),
        P(),
        P("dp", None),
        P("dp"),
        P(("dp", "tensor"), None),
    )
    return jax.shard_map(
        local,
        mesh=mesh,
        in_specs=placed,
        out_specs=(
            P(("dp", "tensor"), None),
            P(("dp", "tensor"), None),
            P(None, None, None, "tensor"),
            P(None, None, "tensor"),
            P(None, "tensor", None),
            P(),
            P(None, None, "tensor"),
            P(None, "tensor"),
            P(None, "tensor", None),
            P(),
            P(),
        ),
        check_vma=False,
    )
```

```python
import functools
import math

import jax
import jax.numpy as jnp
from jax import lax
from jax.experimental import pallas as pl
from jax.experimental.pallas import tpu as pltpu
from jax.sharding import PartitionSpec as P

HEAD_DIM = 64
epsilon = 1e-06
masked_fill = -1e30
bf16 = jnp.bfloat16
f32 = jnp.float32
ANY = pl.BlockSpec(memory_space=pl.ANY)
SMEM = pl.BlockSpec(memory_space=pltpu.SMEM)
VMEM = pl.BlockSpec(memory_space=pltpu.VMEM)
HBM = pl.BlockSpec(memory_space=pltpu.HBM)
SLOTS = 2
PACE = 1.0


def dot_nn(left, right):
    return lax.dot_general(left, right, (((1,), (0,)), ((), ())), preferred_element_type=f32)


def dot_nt(left, right):
    return lax.dot_general(left, right, (((1,), (1,)), ((), ())), preferred_element_type=f32)


def dot_tn(left, right):
    return lax.dot_general(left, right, (((0,), (0,)), ((), ())), preferred_element_type=f32)


def norm_forward(summed, gain, shift):
    center = summed - jnp.mean(summed, -1, keepdims=True)
    recip = lax.rsqrt(jnp.mean(center * center, -1, keepdims=True) + epsilon)
    normed = center * recip
    return normed * gain + shift, normed, recip


def norm_backward(grad_rows, normed, recip, gain):
    scaled = grad_rows * gain
    first_mean = jnp.mean(scaled, -1, keepdims=True)
    second_mean = jnp.mean(scaled * normed, -1, keepdims=True)
    return recip * (scaled - first_mean - normed * second_mean)


def shape(dims, dtype):
    return jax.ShapeDtypeStruct(dims, dtype)


def params(mib):
    return pltpu.CompilerParams(vmem_limit_bytes=mib * 1024 * 1024)


def here():
    dp = lax.axis_index("dp")
    return dp & 1, (dp >> 1) & 3, lax.axis_index("tensor")


def cost(us):
    return pl.CostEstimate(flops=int(us * 1.1e9 * PACE), bytes_accessed=int(us * 3.6e6 * PACE), transcendentals=0)


def lane_half(rows, which):
    lane = lax.broadcasted_iota(jnp.int32, (rows, 2 * HEAD_DIM), 1)
    return (lane < HEAD_DIM) if which == 0 else (lane >= HEAD_DIM)


class Moves:
    def __init__(self, sems):
        self.sems, self.count, self.out = sems, 0, []

    def make(self, src, dst):
        self.count += 1
        return pltpu.make_async_copy(src, dst, self.sems.at[self.count - 1])

    def start(self, src, dst):
        copy = self.make(src, dst)
        copy.start()
        return copy

    def send(self, src, dst):
        self.out.append(self.start(src, dst))

    def finish(self):
        for copy in self.out:
            copy.wait()


def wait_all(copies):
    for c in copies:
        c.wait()


MOVES = 80
CHUNK = 256


def fetch_attn(moves, layer, own_qkv, own_out, a_refs, b_refs, w):
    core, place, _ = here()
    cols = own_out.shape[1]
    waits = []
    for j in range(4):
        t = j ^ place
        b = moves.start(b_refs[j].at[pl.ds(0, cols)], w.at[t, pl.ds(cols, cols)])
        dst = w.at[t, pl.ds(0, cols)]
        a = moves.make(a_refs[j].at[pl.ds(0, cols)], dst)
        sem = moves.sems.at[moves.count - 1]
        qkv_copy = pltpu.make_async_copy(own_qkv.at[layer, jnp.minimum(t, 2)], dst, sem)
        out_copy = pltpu.make_async_copy(own_out.at[layer], dst, sem)

        @pl.when(core != 0)
        def _(a=a):
            a.start()

        @pl.when((core == 0) & (t < 3))
        def _(qkv_copy=qkv_copy):
            qkv_copy.start()

        @pl.when((core == 0) & (t == 3))
        def _(out_copy=out_copy):
            out_copy.start()

        waits += [b, a]
    return waits


def fetch_ff(moves, layer, own_up, own_down, moved, wu, wd):
    core, place, _ = here()
    width, half = wu.shape[0], own_up.shape[2] // 2
    n_t = wu.shape[1] // half
    part, rows = width // 4, half // 4
    own, x, y, diag_up, diag_down = moved
    ups = [own.at[0], x.at[0], y.at[0], diag_up]
    downs = [own.at[1], x.at[1], y.at[1], diag_down]
    mine = pl.ds(pl.multiple_of(core * half, half), half)

    def up(k):
        if k == 0:
            return [moves.start(own_up.at[layer, :, mine], wu.at[:, pl.ds(0, half)])]
        got = []
        for j in range(4):
            at = pl.ds(pl.multiple_of((j ^ place) * part, part), part)
            got.append(moves.start(ups[j].at[k - 1], wu.at[at, pl.ds(k * half, half)]))
        return got

    def down(k):
        if k == 0:
            return [moves.start(own_down.at[layer, mine], wd.at[pl.ds(0, half)])]
        got = []
        for j in range(4):
            at = pl.ds(pl.multiple_of(k * half + (j ^ place) * rows, rows), rows)
            for n in range(2):
                src = downs[j].at[k - 1, pl.ds(n * rows, rows)]
                got.append(moves.start(src, wd.at[at, pl.ds(n * half, half)]))
        return got

    return up, down, n_t


def chunk_waits(waits, chunk, half):
    start, end = chunk * CHUNK, (chunk + 1) * CHUNK
    for k, copies in enumerate(waits):
        if start <= k * half < end:
            wait_all(copies)


BIAS_ROWS = 16


def split_rows(v):
    parts = []
    for _ in range(3):
        low = v.astype(bf16)
        parts.append(low)
        v = v - low.astype(f32)
    n = sum(p.shape[0] for p in parts)
    return jnp.concatenate(parts + [jnp.zeros((BIAS_ROWS - n, v.shape[1]), bf16)], 0)


def prepare_kernel(own_qkv, own_out, own_up, own_down, up_bias, qv_bias, segments, counts, *refs):
    layers = own_out.shape[0]
    attn, ff, packed, sems = refs[:layers], refs[layers : 2 * layers], refs[2 * layers], refs[2 * layers + 1]
    core, place, _ = here()
    cols, half = own_out.shape[1], up_bias.shape[1] // 2
    part, rows = own_up.shape[1] // 4, half // 4
    copies = []
    for l in range(layers):
        weights = attn[l].at[pl.ds(0, cols)]

        @pl.when(place < 3)
        def _(l=l, weights=weights):
            pltpu.make_async_copy(own_qkv.at[l, jnp.minimum(place, 2)], weights, sems.at[4 * l]).start()

        @pl.when(place == 3)
        def _(l=l, weights=weights):
            pltpu.make_async_copy(own_out.at[l], weights, sems.at[4 * l]).start()

        copies.append(pltpu.make_async_copy(own_out.at[l], weights, sems.at[4 * l]))
        up = own_up.at[l, pl.ds(pl.multiple_of(place * part, part), part), pl.ds(pl.multiple_of(core * half, half), half)]
        copies.append(pltpu.make_async_copy(up, ff[l].at[pl.ds(0, part)], sems.at[4 * l + 1]))
        copies[-1].start()
        at = pl.ds(pl.multiple_of(core * half + place * rows, rows), rows)
        for n in range(2):
            down = own_down.at[l, at, pl.ds(n * half, half)]
            copies.append(pltpu.make_async_copy(down, ff[l].at[pl.ds(part + n * rows, rows)], sems.at[4 * l + 2 + n]))
            copies[-1].start()
    for l in range(layers):
        row = jnp.where(core == 0, up_bias[l : l + 1, :half], up_bias[l : l + 1, half:])
        ff[l][2 * part :] = split_rows(row)
    attn[0][cols:] = split_rows(qv_bias[...])
    n, seq = segments.shape
    packed[:, :seq] = segments[...]
    for i in range(n):
        packed[i : i + 1, seq:] = jnp.full((1, packed.shape[1] - seq), counts[i], jnp.int32)
    for c in copies:
        c.wait()


def prepare(own_qkv, own_out, own_up, own_down, up_bias, qv_bias, segments, counts):
    layers, cols, width = own_out.shape
    half = up_bias.shape[1] // 2
    outs = [shape((cols + (0 if l else BIAS_ROWS), width), bf16) for l in range(layers)]
    outs += [shape((width // 2 + BIAS_ROWS, half), bf16)] * layers
    outs += [shape((segments.shape[0], segments.shape[1] + 128), jnp.int32)]
    got = pl.pallas_call(
        prepare_kernel,
        out_shape=outs,
        in_specs=[HBM] * 4 + [VMEM] * 3 + [SMEM],
        out_specs=[VMEM] * len(outs),
        scratch_shapes=[pltpu.SemaphoreType.DMA((4 * layers,))],
        compiler_params=params(56),
        cost_estimate=cost(2),
        name="prepare",
    )(own_qkv, own_out, own_up, own_down, up_bias, qv_bias, segments, counts)
    return got[:layers], got[layers : 2 * layers], got[2 * layers]


def mask_kernel(mine, theirs, out, out_t):
    core, _, z = here()
    row = pl.ds(z >> 1, 1)
    packed = jnp.where(core == (z & 1), mine[row], theirs[row])
    seq = out.shape[0]
    segments, slots = packed[:, :seq].astype(f32), packed[:, seq : seq + 1]
    column = jnp.transpose(jnp.broadcast_to(segments, (128, seq)))[:, 0:1]
    same = column == segments
    down = lax.broadcasted_iota(jnp.int32, (seq, seq), 0)
    along = lax.broadcasted_iota(jnp.int32, (seq, seq), 1)
    out[...] = jnp.where(same & ((along < slots) | (down >= slots)), 0.0, masked_fill)
    out_t[...] = jnp.where(same & ((down < slots) | (along >= slots)), 0.0, masked_fill)


def masks(mine, theirs):
    seq = mine.shape[1] - 128
    return pl.pallas_call(
        mask_kernel,
        out_shape=[shape((seq, seq), f32)] * 2,
        in_specs=[VMEM, VMEM],
        out_specs=[VMEM] * 2,
        compiler_params=params(12),
        cost_estimate=cost(2),
        name="masks",
    )(mine, theirs)


def attn_fwd_kernel(layer, *refs):
    refs = list(refs)
    first = layer == 0
    rows_in = refs[: 2 if first else 3]
    refs = refs[len(rows_in) :]
    if not first:
        ob, gain, shift = refs[:3]
        refs = refs[3:]
    own_bias, mask_in, a_bias, b_bias, own_qkv, own_out = refs[:6]
    a_refs, b_refs = refs[6:10], refs[10:14]
    refs = refs[14:]
    n_out = 5 if first else 7
    outs, refs = refs[:n_out], refs[n_out:]
    bufs, refs = refs[: len(rows_in)], refs[len(rows_in) :]
    vals, refs = refs[:n_out], refs[n_out:]
    mask, w, lse, packed, sems = refs
    xr = vals[0]
    qkv, lse_t, o, a_low = vals[-4:]
    core, _, _ = here()
    seq, width = xr.shape
    half, cols = seq // 2, own_out.shape[1]
    moves = Moves(sems)
    if first:
        at = [pl.ds(pl.multiple_of(c * half, half), half) for c in (core, 1 - core)]
        row_waits = [moves.start(src, xr.at[a]) for src, a in zip(rows_in, at)]
    else:
        row_waits = [
            [moves.start(src.at[pl.ds(i * half, half)], buf.at[pl.ds(i * half, half)]) for src, buf in zip(rows_in, bufs)]
            for i in range(2)
        ]
    bias_waits = [moves.start(ref.at[pl.ds(cols, BIAS_ROWS)], packed.at[n]) for n, ref in enumerate((a_bias, b_bias))]
    weight_waits = fetch_attn(moves, layer, own_qkv, own_out, a_refs, b_refs, w)
    mask_wait = moves.start(mask_in, mask)

    if first:
        wait_all(row_waits)
        moves.send(xr, outs[0])
    else:
        normed, recip = vals[1:3]
        h_in, f_mine, f_theirs = bufs
        for i in range(seq // 128):
            if i * 128 % half == 0:
                wait_all(row_waits[i * 128 // half])
            at = pl.ds(i * 128, 128)
            h = h_in[at] * gain[layer - 1, 0:1] + shift[layer - 1, 0:1]
            z = h + (f_mine[at].astype(f32) + f_theirs[at].astype(f32)) + ob[layer - 1, 1:2]
            new, n, r = norm_forward(z, gain[layer - 1, 1:2], shift[layer - 1, 1:2])
            xr[at] = new.astype(bf16)
            normed[at] = n
            recip[at] = r
        for n in range(3):
            moves.send(vals[n], outs[n])

    wait_all(bias_waits)
    a_row, b_row = (jnp.sum(packed[n, 0:3].astype(f32), 0, keepdims=True) for n in range(2))
    a_row = jnp.where(core == 0, own_bias[...], a_row)
    qb = []
    for i in range(2):
        base = (2 * layer + i) * cols
        qb.append(jnp.concatenate([a_row[:, base : base + cols], b_row[:, base : base + cols]], 1))
    wait_all(weight_waits)
    rows = 256
    for t in range(3):
        for i in range(seq // rows):
            at = pl.ds(i * rows, rows)
            acc = dot_nt(xr[at], w[t])
            if t != 1:
                acc = acc + qb[t // 2]
            qkv[t, at] = acc.astype(bf16)
    moves.send(qkv, outs[-4])
    mask_wait.wait()
    pairs = qkv.shape[2] // 128
    tile = 128
    lane = lax.broadcasted_iota(jnp.int32, (tile, 128), 1)

    @pl.loop(0, seq // tile)
    def _(i):
        at = pl.ds(pl.multiple_of(i * tile, tile), tile)
        bias = mask[at]
        keep = jnp.zeros((tile, 128), f32)
        for g in range(pairs):
            cs = pl.ds(g * 128, 128)
            q2 = qkv[0, at, cs] * jnp.asarray(1.0 / math.sqrt(HEAD_DIM), bf16)
            k2 = qkv[1, :, cs]
            v2 = qkv[2, :, cs]
            acc = None
            for hh in range(2):
                qm = jnp.where(lane_half(tile, hh), q2, jnp.zeros_like(q2))
                s = dot_nt(qm, k2) + bias
                top = jnp.max(s, -1, keepdims=True)
                e = jnp.exp(s - top)
                d = jnp.sum(e, -1, keepdims=True)
                pr = (e * (1.0 / d)).astype(bf16)
                keep = jnp.where(lane == 2 * g + hh, top + jnp.log(d), keep)
                vm = jnp.where(lane_half(seq, hh), v2, jnp.zeros_like(v2))
                got = dot_nn(pr, vm)
                acc = got if acc is None else acc + got
            o[at, cs] = acc.astype(bf16)
        lse[at] = keep

    moves.send(o, outs[-2])
    for i in range(seq // rows):
        at = pl.ds(i * rows, rows)
        a_low[at] = dot_nn(o[at], w[3]).astype(bf16)
        moves.send(a_low.at[at], outs[-1].at[at])
    lse_t[...] = jnp.transpose(lse[...])[0:8]
    moves.send(lse_t, outs[-3])
    moves.finish()


def attn_fwd(layer, rows_in, mask, bias, own_qkv, own_out, a_refs, b_refs):
    first = layer == 0
    seq, width, cols = mask.shape[0], own_out.shape[2], own_out.shape[1]
    wide = SLOTS * cols
    outs = [shape((seq, width), bf16)]
    if not first:
        outs += [shape((seq, width), f32), shape((seq, 1), f32)]
    outs += [
        shape((3, seq, wide), bf16),
        shape((8, seq), f32),
        shape((seq, wide), bf16),
        shape((seq, width), bf16),
    ]
    moving = 2 if first else 3
    small = rows_in[moving:]
    got = pl.pallas_call(
        functools.partial(attn_fwd_kernel, layer),
        out_shape=outs,
        in_specs=[ANY] * moving + [VMEM] * (len(small) + 1) + [ANY] * 13,
        out_specs=[HBM] * len(outs),
        scratch_shapes=[pltpu.VMEM(v.shape, v.dtype) for v in rows_in[:moving]]
        + [pltpu.VMEM(v.shape, v.dtype) for v in outs]
        + [
            pltpu.VMEM((seq, seq), f32),
            pltpu.VMEM((4, wide, width), bf16),
            pltpu.VMEM((seq, 128), f32),
            pltpu.VMEM((2, BIAS_ROWS, width), bf16),
            pltpu.SemaphoreType.DMA((MOVES,)),
        ],
        compiler_params=params(56),
        cost_estimate=cost(10),
        name="attn_fwd",
    )(*rows_in, bias[0], mask, *bias[1:], own_qkv, own_out, *a_refs, *b_refs)
    if first:
        xr, qkv, lse_t, o, a_low = got
        return xr, None, None, qkv, lse_t, o, a_low
    return got


def ff_fwd_kernel(layer, state_in, a_mine, a_theirs, ob, gain, shift, ub, own_up, own_down, *refs):
    moved, outs = refs[:5], refs[5:11]
    state, am, at_, hr, normed, recip, g, gp, f_low, wu, wd, sems = refs[11:]
    seq = state.shape[0]
    moves = Moves(sems)
    rows = 256
    tiles = [pl.ds(i * rows, rows) for i in range(seq // rows)]
    ins = ((state_in, state), (a_mine, am), (a_theirs, at_))
    row_waits = [[moves.start(src.at[at], dst.at[at]) for src, dst in ins] for at in tiles]
    up, down, n_t = fetch_ff(moves, layer, own_up, own_down, moved, wu, wd)
    up_waits = [up(k) for k in range(n_t)]
    down_waits = [down(k) for k in range(n_t)]
    half = wu.shape[1] // n_t
    for i, at in enumerate(tiles):
        wait_all(row_waits[i])
        entered = state[at].astype(f32)
        if layer:
            entered = entered * gain[layer - 1, 1:2] + shift[layer - 1, 1:2]
        z = entered + (am[at].astype(f32) + at_[at].astype(f32)) + ob[layer, 0:1]
        new, n, r = norm_forward(z, gain[layer, 0:1], shift[layer, 0:1])
        hr[at] = new.astype(bf16)
        normed[at] = n
        recip[at] = r
        for val, out in zip((hr, normed, recip), outs):
            moves.send(val.at[at], out.at[at])
    bias = jnp.concatenate([ub[k : k + 1] for k in range(ub.shape[0])], 1)
    for c in range(wu.shape[1] // CHUNK):
        cs = pl.ds(c * CHUNK, CHUNK)
        chunk_waits(up_waits, c, half)
        u = dot_nn(hr[...], wu[:, cs]) + bias[:, c * CHUNK : (c + 1) * CHUNK]
        phi = 0.5 * (1.0 + lax.erf(u * math.sqrt(0.5)))
        g[:, cs] = (u * phi).astype(bf16)
        gp[:, cs] = (phi + u * (jnp.exp(-0.5 * u * u) * (1.0 / math.sqrt(2 * math.pi)))).astype(bf16)
        moves.send(gp.at[:, cs], outs[4].at[:, cs])
    moves.send(g, outs[3])
    for copies in down_waits:
        wait_all(copies)
    for c in range(wd.shape[1] // CHUNK):
        cs = pl.ds(c * CHUNK, CHUNK)
        f_low[:, cs] = dot_nn(g[...], wd[:, cs]).astype(bf16)
        moves.send(f_low.at[:, cs], outs[5].at[:, cs])
    moves.finish()


def ff_fwd(layer, state, a_mine, a_theirs, norms, ub, own_up, own_down, moved):
    seq, width = state.shape
    n_t, half = ub.shape
    outs = [
        shape((seq, width), bf16),
        shape((seq, width), f32),
        shape((seq, 1), f32),
        shape((seq, n_t * half), bf16),
        shape((seq, n_t * half), bf16),
        shape((seq, width), bf16),
    ]
    return pl.pallas_call(
        functools.partial(ff_fwd_kernel, layer),
        out_shape=outs,
        in_specs=[ANY] * 3 + [VMEM] * 4 + [ANY] * 7,
        out_specs=[HBM] * len(outs),
        scratch_shapes=[pltpu.VMEM(v.shape, v.dtype) for v in (state, a_mine, a_theirs)]
        + [pltpu.VMEM(v.shape, v.dtype) for v in outs]
        + [
            pltpu.VMEM((width, n_t * half), bf16),
            pltpu.VMEM((n_t * half, width), bf16),
            pltpu.SemaphoreType.DMA((MOVES,)),
        ],
        compiler_params=params(56),
        cost_estimate=cost(8),
        name="ff_fwd",
    )(state, a_mine, a_theirs, *norms, ub, own_up, own_down, *moved)


def ff_bwd_kernel(last, layer, *refs):
    rows_in, refs = refs[:5], refs[5:]
    ob, gain, shift, gp_in, own_up, own_down = refs[:6]
    moved, refs = refs[6:11], refs[11:]
    n_out = 7 if last else 6
    outs, refs = refs[:n_out], refs[n_out:]
    bufs, gp, refs = refs[:5], refs[5], refs[6:]
    vals, refs = refs[:n_out], refs[n_out:]
    wu, wd, sems = refs
    dz2, dzr2, du, dh_low, small, ub_sum = vals[-6:]
    core, _, _ = here()
    seq = dz2.shape[0]
    moves = Moves(sems)
    rows = 256
    tiles = [pl.ds(i * rows, rows) for i in range(seq // rows)]
    if last:
        row_waits = [[moves.start(src.at[at], dst.at[at]) for src, dst in zip(rows_in[:3], bufs)] for at in tiles]
        cot_waits = [moves.start(src, dst) for src, dst in zip(rows_in[3:], bufs[3:])]
    else:
        row_waits = [[moves.start(src.at[at], dst.at[at]) for src, dst in zip(rows_in, bufs)] for at in tiles]
    up, down, n_t = fetch_ff(moves, layer, own_up, own_down, moved, wu, wd)
    half = wu.shape[1] // n_t
    down_waits, gp_waits = [], []
    for k in range(n_t):
        down_waits.append(down(k))
        for c in range(gp.shape[1] // CHUNK):
            if k * half <= c * CHUNK < (k + 1) * half:
                cs = pl.ds(c * CHUNK, CHUNK)
                gp_waits.append(moves.start(gp_in.at[:, cs], gp.at[:, cs]))
    up_waits = [up(k) for k in range(n_t)]
    small[...] = jnp.zeros_like(small)
    for i, at in enumerate(tiles):
        wait_all(row_waits[i])
        if last:
            h_in, f_mine, f_theirs, c_mine, c_theirs = bufs
            h = h_in[at] * gain[layer, 0:1] + shift[layer, 0:1]
            z = h + (f_mine[at].astype(f32) + f_theirs[at].astype(f32)) + ob[layer, 1:2]
            new, n, r = norm_forward(z, gain[layer, 1:2], shift[layer, 1:2])
            vals[0][at] = new.astype(bf16)
            if i == 0:
                wait_all(cot_waits)
            dy = jnp.where(core == i, c_mine[...], c_theirs[...]).astype(f32)
        else:
            dz_in, x_mine, x_theirs, normed, recip = bufs
            dy = dz_in[at] + (x_mine[at].astype(f32) + x_theirs[at].astype(f32))
            n, r = normed[at], recip[at]
        dz = norm_backward(dy, n, r, gain[layer, 1:2])
        dz2[at] = dz
        low = dz.astype(bf16)
        dzr2[at] = low
        if last:
            moves.send(vals[0].at[at], outs[0].at[at])
        moves.send(dz2.at[at], outs[-6].at[at])
        moves.send(dzr2.at[at], outs[-5].at[at])
        small[0:1] += jnp.sum(dy * n, 0, keepdims=True)
        small[1:2] += jnp.sum(dy, 0, keepdims=True)
        small[2:3] += jnp.sum(dz, 0, keepdims=True)
    for c in range(wd.shape[0] // CHUNK):
        cs = pl.ds(c * CHUNK, CHUNK)
        chunk_waits(down_waits, c, half)
        gp_waits[c].wait()
        back = (dot_nt(dzr2[...], wd[cs]) * gp[:, cs].astype(f32)).astype(bf16)
        du[:, cs] = back
        ub_sum[:, cs] = jnp.sum(back.astype(f32), 0, keepdims=True)
        moves.send(du.at[:, cs], outs[-4].at[:, cs])
    moves.send(small, outs[-2])
    moves.send(ub_sum, outs[-1])
    for copies in up_waits:
        wait_all(copies)
    for c in range(wu.shape[0] // CHUNK):
        cs = pl.ds(c * CHUNK, CHUNK)
        dh_low[:, cs] = dot_nt(du[...], wu[cs]).astype(bf16)
        moves.send(dh_low.at[:, cs], outs[-3].at[:, cs])
    moves.finish()


def ff_bwd(layer, rows_in, norms, gp, own_up, own_down, moved, last):
    width = own_up.shape[1]
    seq, wide = gp.shape
    outs = [
        shape((seq, width), f32),
        shape((seq, width), bf16),
        shape((seq, wide), bf16),
        shape((seq, width), bf16),
        shape((8, width), f32),
        shape((1, wide), f32),
    ]
    if last:
        outs = [shape((seq, width), bf16)] + outs
    return pl.pallas_call(
        functools.partial(ff_bwd_kernel, last, layer),
        out_shape=outs,
        in_specs=[ANY] * 5 + [VMEM] * 3 + [ANY] * 8,
        out_specs=[HBM] * len(outs),
        scratch_shapes=[pltpu.VMEM(v.shape, v.dtype) for v in (*rows_in, gp)]
        + [pltpu.VMEM(v.shape, v.dtype) for v in outs]
        + [
            pltpu.VMEM((width, wide), bf16),
            pltpu.VMEM((wide, width), bf16),
            pltpu.SemaphoreType.DMA((MOVES,)),
        ],
        compiler_params=params(56),
        cost_estimate=cost(9),
        name="ff_bwd",
    )(*rows_in, *norms, gp, own_up, own_down, *moved)


SEND = ((2, 3), (1, 3))
NEXT = (1, 2)


def ff_dw_kernel(z_first, *refs):
    ins, outs = refs[:4], refs[4:-8]
    g, du, hr, dzr2, su, sd, in_sems, sems = refs[-8:]
    _, place, z = here()
    n_t, width, half = su.shape
    part, rows = width // 4, half // 4

    def target(s, j):
        send, nxt, keep = outs[3 * s : 3 * s + 3]
        if j in SEND[s]:
            return send.at[SEND[s].index(j)]
        return nxt if j == NEXT[s] else keep

    def quarter(k):
        return lax.rem(z + n_t - k, n_t)

    copies = []

    def start(src, dst):
        copies.append(pltpu.make_async_copy(src, dst, sems.at[len(copies)]))
        copies[-1].start()

    moves = Moves(in_sems)
    pair = 2 * half
    hr_wait = moves.start(ins[2], hr)
    du_waits = [moves.start(ins[1].at[:, pl.ds(m * pair, pair)], du.at[:, pl.ds(m * pair, pair)]) for m in range(n_t // 2)]
    dzr2_wait = moves.start(ins[3], dzr2)
    g_waits = [moves.start(ins[0].at[:, pl.ds(m * pair, pair)], g.at[:, pl.ds(m * pair, pair)]) for m in range(n_t // 2)]
    hr_wait.wait()
    for m in range(n_t // 2):
        du_waits[m].wait()
        for c in range(width // CHUNK):
            at = pl.ds(c * CHUNK, CHUNK)
            got = dot_tn(hr[:, at], du[:, m * pair : (m + 1) * pair]).astype(bf16)
            for k in (2 * m, 2 * m + 1):
                su[k, at] = got[:, (k - 2 * m) * half : (k - 2 * m + 1) * half]
        if z_first:
            for k in (2 * m, 2 * m + 1):
                for p in range(4):
                    start(su.at[k, pl.ds(p * part, part)], outs[0].at[quarter(k), p, 0])
    if not z_first:
        for j in range(4):
            at = pl.ds(pl.multiple_of((j ^ place) * part, part), part)
            start(su.at[:, at], target(0, j))
    dzr2_wait.wait()
    for m in range(n_t // 2):
        g_waits[m].wait()
        for c in range(pair // CHUNK):
            at = pl.ds(m * pair + c * CHUNK, CHUNK)
            sd[at] = dot_tn(g[:, at], dzr2[...]).astype(bf16)
        if z_first:
            for k in (2 * m, 2 * m + 1):
                for p in range(4):
                    for n in range(2):
                        start(
                            sd.at[pl.ds(k * half + p * rows, rows), pl.ds(n * half, half)],
                            outs[0].at[quarter(k), p, 1, pl.ds(n * rows, rows)],
                        )
    if not z_first:
        for j in range(4):
            for k in range(n_t):
                at = pl.ds(pl.multiple_of(k * half + (j ^ place) * rows, rows), rows)
                for n in range(2):
                    start(sd.at[at, pl.ds(n * half, half)], target(1, j).at[k, pl.ds(n * rows, rows)])
    for c in copies:
        c.wait()


def ff_dw(g, du, hr, dzr2, z_first):
    width = hr.shape[1]
    half = width // 2
    n_t = g.shape[1] // half
    one = (n_t, width // 4, half)
    if z_first:
        outs = [shape((n_t, 4, 2, width // 4, half), bf16)]
    else:
        outs = [shape((2,) + one, bf16), shape(one, bf16), shape(one, bf16)] * 2
    return pl.pallas_call(
        functools.partial(ff_dw_kernel, z_first),
        out_shape=outs,
        in_specs=[ANY] * 4,
        out_specs=[HBM] * len(outs),
        scratch_shapes=[pltpu.VMEM(v.shape, v.dtype) for v in (g, du, hr, dzr2)]
        + [
            pltpu.VMEM((n_t, width, half), bf16),
            pltpu.VMEM((n_t * half, width), bf16),
            pltpu.SemaphoreType.DMA((2 + 2 * n_t,)),
            pltpu.SemaphoreType.DMA((12 * n_t,)),
        ],
        compiler_params=params(56),
        cost_estimate=cost(5),
        name="ff_dw",
    )(g, du, hr, dzr2)


def attn_bwd_kernel(layer, *refs):
    rows_in, refs = refs[:4], refs[4:]
    recip, gain, qkv_in, lse_t, o, mask_in, own_qkv, own_out = refs[:8]
    a_refs, b_refs, refs = refs[8:12], refs[12:16], refs[16:]
    outs, refs = refs[:5], refs[5:]
    bufs, refs = refs[:4], refs[4:]
    dz1, dzr1, d4, dx_low, small, qkv, mask, w, do, sems = refs
    dz2, h_mine, h_theirs, normed = bufs
    seq, width = dz1.shape
    moves = Moves(sems)
    half = seq // 2
    row_waits = []
    for i in range(2):
        at = pl.ds(i * half, half)
        row_waits.append([moves.start(src.at[at], dst.at[at]) for src, dst in zip(rows_in, bufs)])
    weight_waits = fetch_attn(moves, layer, own_qkv, own_out, a_refs, b_refs, w)
    qkv_wait = moves.start(qkv_in, qkv)
    mask_wait = moves.start(mask_in, mask)
    o_wait = moves.start(o, d4.at[3])
    small[...] = jnp.zeros_like(small)
    for i in range(seq // 128):
        if i * 128 % half == 0:
            wait_all(row_waits[i * 128 // half])
        at = pl.ds(i * 128, 128)
        dh = dz2[at] + (h_mine[at].astype(f32) + h_theirs[at].astype(f32))
        n = normed[at]
        dz = norm_backward(dh, n, recip[at], gain[layer, 0:1])
        dz1[at] = dz
        dzr1[at] = dz.astype(bf16)
        small[0:1] += jnp.sum(dh * n, 0, keepdims=True)
        small[1:2] += jnp.sum(dh, 0, keepdims=True)
        small[2:3] += jnp.sum(dz, 0, keepdims=True)
    moves.send(dz1, outs[0])
    moves.send(dzr1, outs[1])
    wait_all(weight_waits)
    rows = 256
    for i in range(seq // rows):
        at = pl.ds(i * rows, rows)
        do[at] = dot_nt(dzr1[at], w[3]).astype(bf16)
    qkv_wait.wait()
    mask_wait.wait()
    pairs = qkv.shape[2] // 128
    tile = 256
    scale = 1.0 / math.sqrt(HEAD_DIM)
    for g in range(pairs):
        cs = pl.ds(g * 128, 128)
        k2 = qkv[1, :, cs] * jnp.asarray(scale, bf16)
        v2 = qkv[2, :, cs]
        dv = dk = None
        for i in range(seq // tile):
            at = pl.ds(i * tile, tile)
            q2 = qkv[0, at, cs]
            do2 = do[at, cs]
            bias = mask[:, at]
            dq = None
            for hh in range(2):
                all_half = lane_half(seq, hh)
                tile_half = lane_half(tile, hh)
                km = jnp.where(all_half, k2, jnp.zeros_like(k2))
                vm = jnp.where(all_half, v2, jnp.zeros_like(v2))
                qm = jnp.where(tile_half, q2, jnp.zeros_like(q2))
                dom = jnp.where(tile_half, do2, jnp.zeros_like(do2))
                head = 2 * g + hh
                s = dot_nt(km, q2) + bias
                pr = jnp.exp(s - lse_t[head : head + 1, at])
                dp = dot_nt(vm, do2)
                delta = jnp.sum(pr * dp, 0, keepdims=True)
                ds = (pr * (dp - delta)).astype(bf16)
                got_v = dot_nn(pr.astype(bf16), dom)
                got_k = dot_nn(ds, qm)
                got_q = dot_nn(jnp.transpose(km), ds)
                dv = got_v if dv is None else dv + got_v
                dk = got_k if dk is None else dk + got_k
                dq = got_q if dq is None else dq + got_q
            dqr = jnp.transpose(dq)
            d4[0, at, cs] = dqr.astype(bf16)
        d4[1, :, cs] = (dk * scale).astype(bf16)
        d4[2, :, cs] = dv.astype(bf16)
    o_wait.wait()
    moves.send(d4, outs[2])
    wide = d4.shape[2]
    small[3:4, 0:wide] = jnp.sum(d4[0].astype(f32), 0, keepdims=True)
    small[3:4, wide : 2 * wide] = jnp.sum(d4[2].astype(f32), 0, keepdims=True)
    for i in range(seq // rows):
        at = pl.ds(i * rows, rows)
        acc = dot_nn(d4[0, at], w[0]) + dot_nn(d4[1, at], w[1]) + dot_nn(d4[2, at], w[2])
        dx_low[at] = acc.astype(bf16)
        moves.send(dx_low.at[at], outs[3].at[at])
    moves.send(small, outs[4])
    moves.finish()


def attn_bwd(layer, dz2, h_mine, h_theirs, normed, recip, gain, qkv, lse_t, o, mask, own_qkv, own_out, a_refs, b_refs):
    seq, width = dz2.shape
    wide = qkv.shape[2]
    outs = [
        shape((seq, width), f32),
        shape((seq, width), bf16),
        shape((4, seq, wide), bf16),
        shape((seq, width), bf16),
        shape((8, width), f32),
    ]
    rows_in = (dz2, h_mine, h_theirs, normed)
    return pl.pallas_call(
        functools.partial(attn_bwd_kernel, layer),
        out_shape=outs,
        in_specs=[ANY] * 4 + [VMEM] * 2 + [ANY, VMEM] + [ANY] * 12,
        out_specs=[HBM] * 5,
        scratch_shapes=[pltpu.VMEM(v.shape, v.dtype) for v in (*rows_in, *outs, qkv, mask)]
        + [
            pltpu.VMEM((4, wide, width), bf16),
            pltpu.VMEM((seq, wide), bf16),
            pltpu.SemaphoreType.DMA((MOVES,)),
        ],
        compiler_params=params(56),
        cost_estimate=cost(12),
        name="attn_bwd",
    )(*rows_in, recip, gain, qkv, lse_t, o, mask, own_qkv, own_out, *a_refs, *b_refs)


def attn_dw_kernel(*refs):
    ins, outs = refs[:3], refs[3:5]
    d4, right, full, sems = refs[5:]
    core, place, _ = here()
    cols = d4.shape[2] // SLOTS
    count, half = outs[0].shape[3:]
    moves = Moves(sems)
    waits = [moves.start(ins[1], right.at[0]), moves.start(ins[2], right.at[1])]
    d4_waits = [moves.start(ins[0].at[j ^ place], d4.at[j ^ place]) for j in range(4)]
    wait_all(waits)
    for j in range(4):
        t = j ^ place
        d4_waits[j].wait()
        full[j] = dot_tn(d4[t], right[t // 3]).astype(bf16)
        for s in range(SLOTS):
            for out, c in zip(outs, (core, 1 - core)):
                at = pl.ds(pl.multiple_of(s * cols + c * count, count), count)
                for n in range(2):
                    moves.send(full.at[j, at, pl.ds(n * half, half)], out.at[s, j, n])
    moves.finish()


def attn_dw(d4, xr, dzr1):
    wide, width = d4.shape[2], xr.shape[1]
    out = shape((SLOTS, 4, 2, wide // 4, width // 2), bf16)
    return pl.pallas_call(
        attn_dw_kernel,
        out_shape=[out, out],
        in_specs=[ANY] * 3,
        out_specs=[HBM] * 2,
        scratch_shapes=[
            pltpu.VMEM(d4.shape, bf16),
            pltpu.VMEM((2,) + xr.shape, bf16),
            pltpu.VMEM((4, wide, width), bf16),
            pltpu.SemaphoreType.DMA((MOVES,)),
        ],
        compiler_params=params(56),
        cost_estimate=cost(3.5),
        name="attn_dw",
    )(d4, xr, dzr1)


def arrange_kernel(mine, theirs, *outs):
    first = here()[0] == 0
    for ref, same in ((mine, first), (theirs, jnp.logical_not(first))):
        for s in range(SLOTS):
            k = jnp.where(same, s, 3 - s)
            for n in range(2):
                send, nxt, keep = outs[3 * n : 3 * n + 3]
                for j in range(4):
                    val = ref[s, j, n]
                    if j in SEND[n]:
                        send[SEND[n].index(j), k] = val
                    elif j == NEXT[n]:
                        nxt[k] = val
                    else:
                        keep[k] = val


def low_sum(*parts):
    total = parts[0].astype(f32)
    for v in parts[1:]:
        total = total + v.astype(f32)
    return total.astype(bf16)


def small_call(kernel, outs, us, name, *ins):
    n, m = len(ins), len(outs)

    def body(*refs):
        bufs, sems = refs[n + m : -1], refs[-1]
        copies = [pltpu.make_async_copy(src, dst, sems.at[i]) for i, (src, dst) in enumerate(zip(refs[:n], bufs))]
        for c in copies:
            c.start()
        for c in copies:
            c.wait()
        kernel(*bufs, *refs[n : n + m])

    return pl.pallas_call(
        body,
        out_shape=outs,
        in_specs=[ANY] * n,
        out_specs=[VMEM] * m,
        scratch_shapes=[pltpu.VMEM(v.shape, v.dtype) for v in ins] + [pltpu.SemaphoreType.DMA((n,))],
        compiler_params=params(16),
        cost_estimate=cost(us * 0.01),
        name=name,
    )(*ins)


def second_kernel(nxt_a, got_a, nxt_b, got_b, out_a, out_b):
    out_a[...] = low_sum(nxt_a[...], got_a[1])
    out_b[...] = low_sum(nxt_b[...], got_b[1])


def third_kernel(*refs):
    out = refs[-1]
    n_t = out.shape[0]
    z = here()[2]
    row = 0
    for c in range(len(refs) // 6):
        ins = refs[6 * c : 6 * c + 6]
        rows = ins[0].shape[1]
        for n in range(2):
            keep, got, more = ins[3 * n : 3 * n + 3]
            for k in range(n_t):
                q = lax.rem(z + n_t - k, n_t)
                out[q, n, row : row + rows] = low_sum(keep[k], got[0, k], more[k])
        row += rows


def merge_kernel(keep_a, got_a, more_a, keep_b, got_b, more_b, attn, out):
    rows = keep_a.shape[1]
    out[0, :rows] = low_sum(keep_a[0], got_a[0, 0], more_a[0])
    out[1, :rows] = low_sum(keep_b[0], got_b[0, 0], more_b[0])
    out[:, rows:] = attn[...]


def split_kernel(every, *outs):
    _, place, _ = here()
    for s in range(SLOTS):
        send, nxt, keep = outs[3 * s : 3 * s + 3]
        for j in range(4):
            val = every[j ^ place, s]
            if j in SEND[s]:
                send[SEND[s].index(j), 0] = val
            elif j == NEXT[s]:
                nxt[0] = val
            else:
                keep[0] = val


def pick_kernel(every, out, ub):
    n_t, rows = every.shape[0], out.shape[2]
    z = here()[2]
    for k in range(n_t):
        q = lax.rem(z + n_t - k, n_t)
        ub[k : k + 1] = jnp.sum(every[q, 2 * rows : 2 * rows + 3].astype(f32), 0, keepdims=True)
        if k:
            for n in range(2):
                out[n, k - 1] = every[q, n * rows : (n + 1) * rows]


def pack_kernel(*refs):
    out = refs[-1]
    layers = (len(refs) - 1) // 3
    small1, small2, ub = refs[:layers], refs[layers : 2 * layers], refs[2 * layers : 3 * layers]
    core, _, z = here()
    half = out.shape[1] // 2
    n_t = ub[0].shape[1] // half
    cols = half // 2
    once = jnp.where(core == 0, 1.0, 0.0).astype(f32)
    for l in range(layers):
        out[6 * l : 6 * l + 3] = small1[l][0:3] * once
        out[6 * l + 3 : 6 * l + 6] = small2[l][0:3] * once
    none = jnp.zeros((1, half), f32)
    for l in range(layers):
        for q in range(n_t):
            row = none
            for k in range(n_t):
                row = jnp.where(lax.rem(z + n_t - k, n_t) == q, ub[l][:, k * half : (k + 1) * half], row)
            left = jnp.where(core == 0, row, none)
            out[6 * layers + n_t * l + q : 6 * layers + n_t * l + q + 1] = jnp.concatenate([left, row - left], 1)
    slot_k = (jnp.where(core == 0, 0, 3), jnp.where(core == 0, 1, 2))
    none = jnp.zeros((1, cols), f32)
    for q in range(n_t):
        parts = []
        for l in range(layers):
            for i in range(2):
                row = none
                for s in range(SLOTS):
                    at = i * half + s * cols
                    here_q = lax.rem(z + n_t - slot_k[s], n_t) == q
                    row = jnp.where(here_q, small1[l][3:4, at : at + cols], row)
                parts.append(row)
        at = (6 + n_t) * layers + q
        out[at : at + 1] = jnp.concatenate(parts, 1)


def unpack_kernel(flat, gain, shift, bias, up, qv):
    layers, _, cols = qv.shape
    n_t = (flat.shape[0] - 6 * layers) // (layers + 1)
    z = here()[2]

    def own(first):
        row = flat[first : first + 1]
        for q in range(1, n_t):
            row = jnp.where(z == q, flat[first + q : first + q + 1], row)
        return row

    row = own((6 + n_t) * layers)
    for l in range(layers):
        for n in range(2):
            at = 6 * l + 3 * n
            gain[l, n : n + 1] = flat[at : at + 1]
            shift[l, n : n + 1] = flat[at + 1 : at + 2]
            bias[l, n : n + 1] = flat[at + 2 : at + 3]
            qv[l, n : n + 1] = row[:, (2 * l + n) * cols : (2 * l + n + 1) * cols]
        up[l : l + 1] = own(6 * layers + n_t * l)


def out_kernel(layer, n_alias, *refs):
    mine, theirs = refs[:4], refs[4:8]
    up, down, qkv, out, wide, sems = refs[8 + n_alias :]
    core, place, _ = here()
    part, half, cols = up.shape[1] // 4, up.shape[2] // 2, out.shape[1]
    rows, count = half // 4, cols // 2
    copies = []

    def start(src, dst):
        copies.append(pltpu.make_async_copy(src, dst, sems.at[len(copies)]))
        copies[-1].start()

    for n, (pieces, c) in enumerate(((mine, core), (theirs, 1 - core))):
        off = pl.multiple_of(c * half, half)
        for j, ref in enumerate(pieces):
            p = j ^ place
            buf = wide.at[n, j]
            buf[...] = ref[...].astype(f32)
            start(buf.at[0, pl.ds(0, part)], up.at[layer, pl.ds(pl.multiple_of(p * part, part), part), pl.ds(off, half)])
            for m in range(2):
                lanes = pl.ds(m * half, half)
                at = pl.ds(pl.multiple_of(c * half + p * rows, rows), rows)
                start(buf.at[1, pl.ds(m * rows, rows)], down.at[layer, at, lanes])
                src, sem = buf.at[m, pl.ds(part, count)], sems.at[len(copies)]
                at = pl.ds(pl.multiple_of(c * count, count), count)
                to_qkv = pltpu.make_async_copy(src, qkv.at[layer, jnp.minimum(p, 2), at, lanes], sem)
                to_out = pltpu.make_async_copy(src, out.at[layer, at, lanes], sem)

                @pl.when(p < 3)
                def _(to_qkv=to_qkv):
                    to_qkv.start()

                @pl.when(p == 3)
                def _(to_out=to_out):
                    to_out.start()

                copies.append(to_out)
    for c in copies:
        c.wait()


def outputs(layer, dims, mine, theirs, before):
    before = list(before or [])
    n = len(mine) + len(theirs)
    return pl.pallas_call(
        functools.partial(out_kernel, layer, len(before)),
        out_shape=[shape(d, f32) for d in dims],
        in_specs=[VMEM] * n + [HBM] * len(before),
        out_specs=[HBM] * len(dims),
        scratch_shapes=[
            pltpu.VMEM((2, 4) + mine[0].shape, f32),
            pltpu.SemaphoreType.DMA((5 * n,)),
        ],
        input_output_aliases={n + i: i for i in range(len(before))},
        compiler_params=params(24),
        cost_estimate=cost(4),
        name="gradients_out",
    )(*mine, *theirs, *before)


def after(v, *others):
    return lax.optimization_barrier((v, *others))[0]


def local(
    block_input,
    w_qkv,
    qv_bias,
    w_out,
    out_bias,
    w_up,
    up_bias,
    w_down,
    norm_gain,
    norm_shift,
    segment_ids,
    slot_counts,
    cotangent,
):
    layers, width, _, cols = w_qkv.shape
    hidden = w_up.shape[2]
    seq = segment_ids.shape[1]
    n_dp, n_t = lax.axis_size("dp"), lax.axis_size("tensor")
    dp, z = lax.axis_index("dp"), lax.axis_index("tensor")
    core, place = dp & 1, (dp >> 1) & 3
    first = core == 0
    part, half = hidden // 4, hidden // 2
    norms_in = (out_bias, norm_gain, norm_shift)

    def send(v, axis, pairs, name):
        with jax.named_scope(name):
            return lax.ppermute(v, axis, pairs)

    def flip(v, bits, name, odd=False):
        return send(v, "dp", [(i, i ^ bits) for i in range(n_dp) if not odd or i & 1], name)

    def across(v, name):
        return flip(v, 1, name)

    def shift(v, by, name):
        pairs = []
        for i in range(n_dp):
            move = by[i & 1]
            if move:
                pairs += [(i * n_t + k, i * n_t + (k + move) % n_t) for k in range(n_t)]
        return send(v, ("dp", "tensor"), pairs, name)

    def swap(v, name):
        pairs = []
        for i in range(n_dp):
            for k in range(n_t):
                if (i & 1) != (k & 1):
                    pairs.append((i * n_t + k, (i ^ 1) * n_t + (k ^ 1)))
        moved = send(v, ("dp", "tensor"), pairs, name)
        return jnp.where(core == (z & 1), v, moved)

    own_qkv = jnp.transpose(w_qkv, (0, 2, 3, 1))
    own_bias = qv_bias.reshape(1, -1)

    def attn_over_z(piece, l):
        return shift(piece, (1, 2), f"attn{l}_z_b"), shift(piece, (0, 3), f"attn{l}_z_a")

    def attn_over_xy(b, a, l, *late):
        name = f"attn{l}_"
        bx = flip(b, 2, name + "b_x")
        by = flip(b, 4, name + "b_y")
        ay = flip(a, 4, name + "a_y", True)
        ax = flip(a, 2, name + "a_x", True)
        bd = flip(after(bx, *late), 4, name + "b_xy")
        ad = flip(after(ay, *late), 2, name + "a_yx", True)
        return (a, ax, ay, ad), (b, bx, by, bd)

    def ff_over_xy(own, l):
        x, y = flip(own, 2, f"ff{l}_x"), flip(own, 4, f"ff{l}_y")
        return own, x, y, flip(x[0], 4, f"ff{l}_xy"), flip(y[1], 2, f"ff{l}_yx")

    x_mine = swap(block_input, "x_swap")
    attn_piece, ff_piece, packed = prepare(own_qkv, w_out, w_up, w_down, up_bias, own_bias, segment_ids, slot_counts)
    mask, mask_t = masks(packed, across(packed, "seg"))
    x_theirs = across(x_mine, "x_across")

    def ff_over_z(l, *late):
        with jax.named_scope(f"ff{l}_z"):
            return lax.all_gather(after(ff_piece[l], *late), "tensor", axis=0)

    def take(every, l, *late):
        outs = [shape((2, n_t - 1, part, half), bf16), shape((n_t, half), f32)]
        own, ub = small_call(pick_kernel, outs, 1.5, "pick_quarters", after(every, *late))
        return ff_over_xy(own, l), ub

    attn0_z = attn_over_z(attn_piece[0], 0)
    ff0_z = ff_over_z(0, *attn0_z)
    attn0 = attn_over_xy(after(attn0_z[0], mask, x_mine), after(attn0_z[1], mask, x_mine), 0, x_theirs)
    attn1_z = attn_over_z(after(attn_piece[1], *attn0[0][:3], *attn0[1][:3]), 1)
    ff1_z = ff_over_z(1, *attn1_z)
    bias = (own_bias,) + attn0_z[::-1]

    rows_in = (x_mine, x_theirs)
    saved = []
    attn_w, ff_w, ubs = [attn0], [], []
    for l in range(layers):
        xr, n2, r2, qkv, lse_t, o, a_low = attn_fwd(l, rows_in, mask, bias, own_qkv, w_out, *attn_w[l])
        state = n2 if l else xr
        if l:
            saved[l - 1] += (n2, r2)
        else:
            ff0, ub = take(ff0_z, 0, xr)
            ff_w.append(ff0)
            ubs.append(ub)
            attn_w.append(attn_over_xy(after(attn1_z[0], ff0[1], ff0[2]), after(attn1_z[1], ff0[1], ff0[2]), 1))
        hr, n1, r1, g, gp, f_low = ff_fwd(
            l, state, a_low, across(a_low, f"a{l}"), norms_in, ubs[l], w_up, w_down, ff_w[l]
        )
        if l == 0:
            ff1, ub = take(ff1_z, 1, hr)
            ff_w.append(ff1)
            ubs.append(ub)
        saved.append((xr, qkv, lse_t, o, hr, n1, r1, g, gp))
        rows_in = (n1, f_low, across(f_low, f"f{l}")) + norms_in

    class Sums:
        def __init__(self, name):
            self.name = name

        def first(self, pieces):
            self.pieces = pieces
            self.got = (flip(pieces[0], 4, self.name + "_1a"), flip(pieces[3], 2, self.name + "_1b"))
            return self

        def second(self, *late):
            p, got = self.pieces, self.got
            nxt = after(p[1], *late)
            outs = [shape(nxt.shape, bf16)] * 2
            self.sec = small_call(second_kernel, outs, 1.2, "add_second", nxt, got[0], p[4], got[1])
            self.more = (flip(self.sec[0], 2, self.name + "_2a"), flip(self.sec[1], 4, self.name + "_2b"))
            return self

        def parts(self):
            p, got, more = self.pieces, self.got, self.more
            return [p[2], got[0], more[0], p[5], got[1], more[1]]

    def over_z(every):
        with jax.named_scope("sums_z"):
            return lax.psum_scatter(every, "tensor", scatter_dimension=0)

    def third(chunks, *late):
        ins = [v for c in chunks for v in c.parts()]
        rows = sum(c.pieces[2].shape[1] for c in chunks)
        outs = [shape((n_t, 2, rows, half), bf16)]
        (every,) = small_call(third_kernel, outs, 1.5, "add_third", after(ins[0], *late), *ins[1:])
        return every, over_z(every)

    def attn_first(name, mine, theirs):
        one = (n_t, cols // 2, half)
        outs = [shape((2,) + one, bf16), shape(one, bf16), shape(one, bf16)] * 2
        return Sums(name).first(small_call(arrange_kernel, outs, 1.5, "arrange", mine, theirs))

    def split(total, *late):
        one = (1, part, half)
        outs = [shape((2,) + one, bf16), shape(one, bf16), shape(one, bf16)] * 2
        return Sums("gf1").first(small_call(split_kernel, outs, 1.5, "split_pieces", after(total, *late)))

    def spread(total, name):
        bits = 8
        while bits < n_dp:
            total = low_sum(total, flip(total, bits, name + "_rest"))
            bits *= 2
        mine = [total] + [flip(total, bits, f"{name}_c{bits}") for bits in (2, 4, 6)]
        return mine, [across(v, f"{name}_cc{n}") for n, v in enumerate(mine)]

    def finish(l, mine, theirs, before, *late):
        dims = [(layers, width, hidden), (layers, hidden, width), (layers, 3, cols, width), (layers, cols, width)]
        return outputs(l, dims, [after(mine[0], *late)] + mine[1:], theirs, before)

    a1 = None
    smalls = []
    for l in reversed(range(layers)):
        last = l == layers - 1
        xr, qkv, lse_t, o, hr, n1, r1, g, gp = saved[l][:9]
        if last:
            c_mine = swap(cotangent, "cot_swap")
            ff_rows = rows_in[:3] + (c_mine, across(c_mine, "cot_across"))
        else:
            ff_rows = (dz1, dx_low, across(dx_low, f"dx{l}")) + saved[l][9:]
        got = ff_bwd(l, ff_rows, norms_in, gp, w_up, w_down, ff_w[l], last)
        if last:
            out_half = lax.dynamic_slice_in_dim(got[0], core * (seq // 2), seq // 2, 0)
            got = got[1:]
        dz2, dzr2, du, dh_low, small2, ub_sum = got
        if a1:
            a1.second(dzr2)
            dzr2 = after(dzr2, *a1.sec)
        ff_pieces = ff_dw(g, du, hr, dzr2, last)
        if last:
            f1_total = over_z(ff_pieces[0])
        else:
            first_out = [after(ff_pieces[0], *a1.more), *ff_pieces[1:3], after(ff_pieces[3], *a1.more), *ff_pieces[4:]]
            f0 = Sums("gf0").first(first_out)
        dh_theirs = across(dh_low, f"dh{l}")
        dz2 = after(dz2, ff_pieces[0])
        if a1:
            a1_every, a1_total = third([a1])
            dz2 = after(dz2, a1_every)
        dz1, dzr1, d4, dx_low, small1 = attn_bwd(
            l, dz2, dh_low, dh_theirs, n1, r1, norm_gain, qkv, lse_t, o, mask_t, own_qkv, w_out, *attn_w[l]
        )
        at_pieces = attn_dw(d4, xr, dzr1)
        at_theirs = across(at_pieces[1], f"ga{l}_core")
        if last:
            a1 = attn_first("ga1", at_pieces[0], at_theirs)
            dz1 = after(dz1, a1.pieces[0])
        smalls.append((small1, small2, ub_sum))
    smalls = smalls[::-1]

    def more_flat(flat, axis, bits, *late):
        n = lax.axis_size(axis)
        return flat + send(after(flat, *late), axis, [(i, i ^ bits) for i in range(n)], f"flat_{axis}{bits}")

    n_rows = (6 + n_t) * layers + n_t
    (flat,) = small_call(
        pack_kernel,
        [shape((n_rows, width), f32)],
        1.5,
        "pack_small",
        *[g[0] for g in smalls],
        *[g[1] for g in smalls],
        *[g[2] for g in smalls],
    )
    f0.second(at_pieces[0])
    a0 = attn_first("ga0", after(at_pieces[0], *f0.sec), at_theirs)
    flat = more_flat(flat, "dp", 1, a0.pieces[0])
    flat = more_flat(flat, "tensor", 1)
    a0.second(flat)
    flat = more_flat(flat, "tensor", 2, *a0.sec)
    l0_every, l0_total = third([f0, a0], flat)
    f1 = split(f1_total, l0_every)
    flat = more_flat(flat, "dp", 2, f1.pieces[0])
    f1.second(flat)
    flat = more_flat(flat, "dp", 4, *f1.sec)
    bits = 8
    while bits < n_dp:
        flat = more_flat(flat, "dp", bits)
        bits *= 2
    ins = f1.parts()
    ins[0] = after(ins[0], flat)
    (l1_total,) = small_call(merge_kernel, [shape((2, part + cols // 2, half), bf16)], 1.5, "merge", *ins, a1_total)
    l1 = spread(l1_total, "l1")
    dx = dz1 + (dx_low.astype(f32) + across(after(dx_low, l1_total), "dx_last").astype(f32))
    input_grad = swap(lax.dynamic_slice_in_dim(dx, core * (seq // 2), seq // 2, 0), "grad_swap")
    mixed = swap(after(out_half, l1_total), "mixed_swap")
    l0 = spread(after(l0_total, *l1[0]), "l0")
    grads = finish(1, *l1, None, l0_total, input_grad, mixed)
    grads = finish(0, *l0, grads)
    grad_gain, grad_shift, grad_out_bias, grad_up_bias, grad_qv_bias = small_call(
        unpack_kernel,
        [shape((layers, 2, width), f32)] * 3 + [shape((layers, hidden), f32), shape((layers, 2, cols), f32)],
        1.5,
        "unpack_small",
        flat,
    )
    return (
        mixed,
        input_grad,
        jnp.transpose(grads[2], (0, 3, 1, 2)),
        grad_qv_bias,
        grads[3],
        grad_out_bias,
        grads[0],
        grad_up_bias,
        grads[1],
        grad_gain,
        grad_shift,
    )


def solution(mesh):
    placed = (
        P(("dp", "tensor"), None),
        P(None, None, None, "tensor"),
        P(None, None, "tensor"),
        P(None, "tensor", None),
        P(),
        P(None, None, "tensor"),
        P(None, "tensor"),
        P(None, "tensor", None),
        P(),
        P(),
        P("dp", None),
        P("dp"),
        P(("dp", "tensor"), None),
    )
    return jax.shard_map(
        local,
        mesh=mesh,
        in_specs=placed,
        out_specs=(
            P(("dp", "tensor"), None),
            P(("dp", "tensor"), None),
            P(None, None, None, "tensor"),
            P(None, None, "tensor"),
            P(None, "tensor", None),
            P(),
            P(None, None, "tensor"),
            P(None, "tensor"),
            P(None, "tensor", None),
            P(),
            P(),
        ),
        check_vma=False,
    )
```

```python
import functools
import math

import jax
import jax.numpy as jnp
from jax import lax
from jax.experimental import pallas as pl
from jax.experimental.pallas import tpu as pltpu
from jax.sharding import PartitionSpec as P

HEAD_DIM = 64
epsilon = 1e-06
masked_fill = -1e30
bf16 = jnp.bfloat16
f32 = jnp.float32
ANY = pl.BlockSpec(memory_space=pl.ANY)
SMEM = pl.BlockSpec(memory_space=pltpu.SMEM)
VMEM = pl.BlockSpec(memory_space=pltpu.VMEM)
HBM = pl.BlockSpec(memory_space=pltpu.HBM)
SLOTS = 2
PACE = 1.0


def dot_nn(left, right):
    return lax.dot_general(left, right, (((1,), (0,)), ((), ())), preferred_element_type=f32)


def dot_nt(left, right):
    return lax.dot_general(left, right, (((1,), (1,)), ((), ())), preferred_element_type=f32)


def dot_tn(left, right):
    return lax.dot_general(left, right, (((0,), (0,)), ((), ())), preferred_element_type=f32)


def norm_forward(summed, gain, shift):
    center = summed - jnp.mean(summed, -1, keepdims=True)
    recip = lax.rsqrt(jnp.mean(center * center, -1, keepdims=True) + epsilon)
    normed = center * recip
    return normed * gain + shift, normed, recip


def norm_backward(grad_rows, normed, recip, gain):
    scaled = grad_rows * gain
    first_mean = jnp.mean(scaled, -1, keepdims=True)
    second_mean = jnp.mean(scaled * normed, -1, keepdims=True)
    return recip * (scaled - first_mean - normed * second_mean)


def shape(dims, dtype):
    return jax.ShapeDtypeStruct(dims, dtype)


def params(mib):
    return pltpu.CompilerParams(vmem_limit_bytes=mib * 1024 * 1024)


def here():
    dp = lax.axis_index("dp")
    return dp & 1, (dp >> 1) & 3, lax.axis_index("tensor")


def cost(us):
    return pl.CostEstimate(flops=int(us * 1.1e9 * PACE), bytes_accessed=int(us * 3.6e6 * PACE), transcendentals=0)


def lane_half(rows, which):
    lane = lax.broadcasted_iota(jnp.int32, (rows, 2 * HEAD_DIM), 1)
    return (lane < HEAD_DIM) if which == 0 else (lane >= HEAD_DIM)


class Moves:
    def __init__(self, sems):
        self.sems, self.count, self.out = sems, 0, []

    def make(self, src, dst):
        self.count += 1
        return pltpu.make_async_copy(src, dst, self.sems.at[self.count - 1])

    def start(self, src, dst):
        copy = self.make(src, dst)
        copy.start()
        return copy

    def send(self, src, dst):
        self.out.append(self.start(src, dst))

    def finish(self):
        for copy in self.out:
            copy.wait()


def wait_all(copies):
    for c in copies:
        c.wait()


MOVES = 80
CHUNK = 256


def fetch_attn(moves, layer, own_qkv, own_out, a_refs, b_refs, w):
    core, place, _ = here()
    cols = own_out.shape[1]
    waits = []
    for j in range(4):
        t = j ^ place
        b = moves.start(b_refs[j].at[pl.ds(0, cols)], w.at[t, pl.ds(cols, cols)])
        dst = w.at[t, pl.ds(0, cols)]
        a = moves.make(a_refs[j].at[pl.ds(0, cols)], dst)
        sem = moves.sems.at[moves.count - 1]
        qkv_copy = pltpu.make_async_copy(own_qkv.at[layer, jnp.minimum(t, 2)], dst, sem)
        out_copy = pltpu.make_async_copy(own_out.at[layer], dst, sem)

        @pl.when(core != 0)
        def _(a=a):
            a.start()

        @pl.when((core == 0) & (t < 3))
        def _(qkv_copy=qkv_copy):
            qkv_copy.start()

        @pl.when((core == 0) & (t == 3))
        def _(out_copy=out_copy):
            out_copy.start()

        waits += [b, a]
    return waits


def fetch_ff(moves, layer, own_up, own_down, moved, wu, wd):
    core, place, _ = here()
    width, half = wu.shape[0], own_up.shape[2] // 2
    n_t = wu.shape[1] // half
    part, rows = width // 4, half // 4
    own, x, y, diag_up, diag_down = moved
    ups = [own.at[0], x.at[0], y.at[0], diag_up]
    downs = [own.at[1], x.at[1], y.at[1], diag_down]
    mine = pl.ds(pl.multiple_of(core * half, half), half)

    def up(k):
        if k == 0:
            return [moves.start(own_up.at[layer, :, mine], wu.at[:, pl.ds(0, half)])]
        got = []
        for j in range(4):
            at = pl.ds(pl.multiple_of((j ^ place) * part, part), part)
            got.append(moves.start(ups[j].at[k - 1], wu.at[at, pl.ds(k * half, half)]))
        return got

    def down(k):
        if k == 0:
            return [moves.start(own_down.at[layer, mine], wd.at[pl.ds(0, half)])]
        got = []
        for j in range(4):
            at = pl.ds(pl.multiple_of(k * half + (j ^ place) * rows, rows), rows)
            for n in range(2):
                src = downs[j].at[k - 1, pl.ds(n * rows, rows)]
                got.append(moves.start(src, wd.at[at, pl.ds(n * half, half)]))
        return got

    return up, down, n_t


def chunk_waits(waits, chunk, half):
    start, end = chunk * CHUNK, (chunk + 1) * CHUNK
    for k, copies in enumerate(waits):
        if start <= k * half < end:
            wait_all(copies)


BIAS_ROWS = 16


def split_rows(v):
    parts = []
    for _ in range(3):
        low = v.astype(bf16)
        parts.append(low)
        v = v - low.astype(f32)
    n = sum(p.shape[0] for p in parts)
    return jnp.concatenate(parts + [jnp.zeros((BIAS_ROWS - n, v.shape[1]), bf16)], 0)


def prepare_kernel(own_qkv, own_out, own_up, own_down, up_bias, qv_bias, segments, counts, *refs):
    layers = own_out.shape[0]
    attn, ff, packed, sems = refs[:layers], refs[layers : 2 * layers], refs[2 * layers], refs[2 * layers + 1]
    core, place, _ = here()
    cols, half = own_out.shape[1], up_bias.shape[1] // 2
    part, rows = own_up.shape[1] // 4, half // 4
    copies = []
    for l in range(layers):
        weights = attn[l].at[pl.ds(0, cols)]

        @pl.when(place < 3)
        def _(l=l, weights=weights):
            pltpu.make_async_copy(own_qkv.at[l, jnp.minimum(place, 2)], weights, sems.at[4 * l]).start()

        @pl.when(place == 3)
        def _(l=l, weights=weights):
            pltpu.make_async_copy(own_out.at[l], weights, sems.at[4 * l]).start()

        copies.append(pltpu.make_async_copy(own_out.at[l], weights, sems.at[4 * l]))
        up = own_up.at[l, pl.ds(pl.multiple_of(place * part, part), part), pl.ds(pl.multiple_of(core * half, half), half)]
        copies.append(pltpu.make_async_copy(up, ff[l].at[pl.ds(0, part)], sems.at[4 * l + 1]))
        copies[-1].start()
        at = pl.ds(pl.multiple_of(core * half + place * rows, rows), rows)
        for n in range(2):
            down = own_down.at[l, at, pl.ds(n * half, half)]
            copies.append(pltpu.make_async_copy(down, ff[l].at[pl.ds(part + n * rows, rows)], sems.at[4 * l + 2 + n]))
            copies[-1].start()
    for l in range(layers):
        row = jnp.where(core == 0, up_bias[l : l + 1, :half], up_bias[l : l + 1, half:])
        ff[l][2 * part :] = split_rows(row)
    attn[0][cols:] = split_rows(qv_bias[...])
    n, seq = segments.shape
    packed[:, :seq] = segments[...]
    for i in range(n):
        packed[i : i + 1, seq:] = jnp.full((1, packed.shape[1] - seq), counts[i], jnp.int32)
    for c in copies:
        c.wait()


def prepare(own_qkv, own_out, own_up, own_down, up_bias, qv_bias, segments, counts):
    layers, cols, width = own_out.shape
    half = up_bias.shape[1] // 2
    outs = [shape((cols + (0 if l else BIAS_ROWS), width), bf16) for l in range(layers)]
    outs += [shape((width // 2 + BIAS_ROWS, half), bf16)] * layers
    outs += [shape((segments.shape[0], segments.shape[1] + 128), jnp.int32)]
    got = pl.pallas_call(
        prepare_kernel,
        out_shape=outs,
        in_specs=[HBM] * 4 + [VMEM] * 3 + [SMEM],
        out_specs=[VMEM] * len(outs),
        scratch_shapes=[pltpu.SemaphoreType.DMA((4 * layers,))],
        compiler_params=params(56),
        cost_estimate=cost(2),
        name="prepare",
    )(own_qkv, own_out, own_up, own_down, up_bias, qv_bias, segments, counts)
    return got[:layers], got[layers : 2 * layers], got[2 * layers]


def mask_kernel(mine, theirs, out, out_t):
    core, _, z = here()
    row = pl.ds(z >> 1, 1)
    packed = jnp.where(core == (z & 1), mine[row], theirs[row])
    seq = out.shape[0]
    segments, slots = packed[:, :seq].astype(f32), packed[:, seq : seq + 1]
    column = jnp.transpose(jnp.broadcast_to(segments, (128, seq)))[:, 0:1]
    same = column == segments
    down = lax.broadcasted_iota(jnp.int32, (seq, seq), 0)
    along = lax.broadcasted_iota(jnp.int32, (seq, seq), 1)
    out[...] = jnp.where(same & ((along < slots) | (down >= slots)), 0.0, masked_fill)
    out_t[...] = jnp.where(same & ((down < slots) | (along >= slots)), 0.0, masked_fill)


def masks(mine, theirs):
    seq = mine.shape[1] - 128
    return pl.pallas_call(
        mask_kernel,
        out_shape=[shape((seq, seq), f32)] * 2,
        in_specs=[VMEM, VMEM],
        out_specs=[VMEM] * 2,
        compiler_params=params(12),
        cost_estimate=cost(2),
        name="masks",
    )(mine, theirs)


def attn_fwd_kernel(layer, *refs):
    refs = list(refs)
    first = layer == 0
    rows_in = refs[: 2 if first else 3]
    refs = refs[len(rows_in) :]
    if not first:
        ob, gain, shift = refs[:3]
        refs = refs[3:]
    own_bias, mask_in, a_bias, b_bias, own_qkv, own_out = refs[:6]
    a_refs, b_refs = refs[6:10], refs[10:14]
    refs = refs[14:]
    n_out = 5 if first else 7
    outs, refs = refs[:n_out], refs[n_out:]
    bufs, refs = refs[: len(rows_in)], refs[len(rows_in) :]
    vals, refs = refs[:n_out], refs[n_out:]
    mask, w, lse, packed, sems = refs
    xr = vals[0]
    qkv, lse_t, o, a_low = vals[-4:]
    core, _, _ = here()
    seq, width = xr.shape
    half, cols = seq // 2, own_out.shape[1]
    moves = Moves(sems)
    if first:
        at = [pl.ds(pl.multiple_of(c * half, half), half) for c in (core, 1 - core)]
        row_waits = [moves.start(src, xr.at[a]) for src, a in zip(rows_in, at)]
    else:
        row_waits = [
            [moves.start(src.at[pl.ds(i * half, half)], buf.at[pl.ds(i * half, half)]) for src, buf in zip(rows_in, bufs)]
            for i in range(2)
        ]
    bias_waits = [moves.start(ref.at[pl.ds(cols, BIAS_ROWS)], packed.at[n]) for n, ref in enumerate((a_bias, b_bias))]
    weight_waits = fetch_attn(moves, layer, own_qkv, own_out, a_refs, b_refs, w)
    mask_wait = moves.start(mask_in, mask)

    if first:
        wait_all(row_waits)
        moves.send(xr, outs[0])
    else:
        normed, recip = vals[1:3]
        h_in, f_mine, f_theirs = bufs
        for i in range(seq // 128):
            if i * 128 % half == 0:
                wait_all(row_waits[i * 128 // half])
            at = pl.ds(i * 128, 128)
            h = h_in[at] * gain[layer - 1, 0:1] + shift[layer - 1, 0:1]
            z = h + (f_mine[at].astype(f32) + f_theirs[at].astype(f32)) + ob[layer - 1, 1:2]
            new, n, r = norm_forward(z, gain[layer - 1, 1:2], shift[layer - 1, 1:2])
            xr[at] = new.astype(bf16)
            normed[at] = n
            recip[at] = r
        for n in range(3):
            moves.send(vals[n], outs[n])

    wait_all(bias_waits)
    a_row, b_row = (jnp.sum(packed[n, 0:3].astype(f32), 0, keepdims=True) for n in range(2))
    a_row = jnp.where(core == 0, own_bias[...], a_row)
    qb = []
    for i in range(2):
        base = (2 * layer + i) * cols
        qb.append(jnp.concatenate([a_row[:, base : base + cols], b_row[:, base : base + cols]], 1))
    wait_all(weight_waits)
    rows = 256
    for t in range(3):
        for i in range(seq // rows):
            at = pl.ds(i * rows, rows)
            acc = dot_nt(xr[at], w[t])
            if t != 1:
                acc = acc + qb[t // 2]
            qkv[t, at] = acc.astype(bf16)
    moves.send(qkv, outs[-4])
    mask_wait.wait()
    pairs = qkv.shape[2] // 128
    tile = 256
    lane = lax.broadcasted_iota(jnp.int32, (tile, 128), 1)

    @pl.loop(0, seq // tile)
    def _(i):
        at = pl.ds(pl.multiple_of(i * tile, tile), tile)
        bias = mask[at]
        keep = jnp.zeros((tile, 128), f32)
        for g in range(pairs):
            cs = pl.ds(g * 128, 128)
            q2 = qkv[0, at, cs] * jnp.asarray(1.0 / math.sqrt(HEAD_DIM), bf16)
            k2 = qkv[1, :, cs]
            v2 = qkv[2, :, cs]
            acc = None
            for hh in range(2):
                qm = jnp.where(lane_half(tile, hh), q2, jnp.zeros_like(q2))
                s = dot_nt(qm, k2) + bias
                top = jnp.max(s, -1, keepdims=True)
                e = jnp.exp(s - top)
                d = jnp.sum(e, -1, keepdims=True)
                pr = (e * (1.0 / d)).astype(bf16)
                keep = jnp.where(lane == 2 * g + hh, top + jnp.log(d), keep)
                vm = jnp.where(lane_half(seq, hh), v2, jnp.zeros_like(v2))
                got = dot_nn(pr, vm)
                acc = got if acc is None else acc + got
            o[at, cs] = acc.astype(bf16)
        lse[at] = keep

    moves.send(o, outs[-2])
    for i in range(seq // rows):
        at = pl.ds(i * rows, rows)
        a_low[at] = dot_nn(o[at], w[3]).astype(bf16)
        moves.send(a_low.at[at], outs[-1].at[at])
    lse_t[...] = jnp.transpose(lse[...])[0:8]
    moves.send(lse_t, outs[-3])
    moves.finish()


def attn_fwd(layer, rows_in, mask, bias, own_qkv, own_out, a_refs, b_refs):
    first = layer == 0
    seq, width, cols = mask.shape[0], own_out.shape[2], own_out.shape[1]
    wide = SLOTS * cols
    outs = [shape((seq, width), bf16)]
    if not first:
        outs += [shape((seq, width), f32), shape((seq, 1), f32)]
    outs += [
        shape((3, seq, wide), bf16),
        shape((8, seq), f32),
        shape((seq, wide), bf16),
        shape((seq, width), bf16),
    ]
    moving = 2 if first else 3
    small = rows_in[moving:]
    got = pl.pallas_call(
        functools.partial(attn_fwd_kernel, layer),
        out_shape=outs,
        in_specs=[ANY] * moving + [VMEM] * (len(small) + 1) + [ANY] * 13,
        out_specs=[HBM] * len(outs),
        scratch_shapes=[pltpu.VMEM(v.shape, v.dtype) for v in rows_in[:moving]]
        + [pltpu.VMEM(v.shape, v.dtype) for v in outs]
        + [
            pltpu.VMEM((seq, seq), f32),
            pltpu.VMEM((4, wide, width), bf16),
            pltpu.VMEM((seq, 128), f32),
            pltpu.VMEM((2, BIAS_ROWS, width), bf16),
            pltpu.SemaphoreType.DMA((MOVES,)),
        ],
        compiler_params=params(56),
        cost_estimate=cost(10),
        name="attn_fwd",
    )(*rows_in, bias[0], mask, *bias[1:], own_qkv, own_out, *a_refs, *b_refs)
    if first:
        xr, qkv, lse_t, o, a_low = got
        return xr, None, None, qkv, lse_t, o, a_low
    return got


def ff_fwd_kernel(layer, state_in, a_mine, a_theirs, ob, gain, shift, ub, own_up, own_down, *refs):
    moved, outs = refs[:5], refs[5:11]
    state, am, at_, hr, normed, recip, g, gp, f_low, wu, wd, sems = refs[11:]
    seq = state.shape[0]
    moves = Moves(sems)
    rows = 256
    tiles = [pl.ds(i * rows, rows) for i in range(seq // rows)]
    ins = ((state_in, state), (a_mine, am), (a_theirs, at_))
    row_waits = [[moves.start(src.at[at], dst.at[at]) for src, dst in ins] for at in tiles]
    up, down, n_t = fetch_ff(moves, layer, own_up, own_down, moved, wu, wd)
    up_waits = [up(k) for k in range(n_t)]
    down_waits = [down(k) for k in range(n_t)]
    half = wu.shape[1] // n_t
    for i, at in enumerate(tiles):
        wait_all(row_waits[i])
        entered = state[at].astype(f32)
        if layer:
            entered = entered * gain[layer - 1, 1:2] + shift[layer - 1, 1:2]
        z = entered + (am[at].astype(f32) + at_[at].astype(f32)) + ob[layer, 0:1]
        new, n, r = norm_forward(z, gain[layer, 0:1], shift[layer, 0:1])
        hr[at] = new.astype(bf16)
        normed[at] = n
        recip[at] = r
        for val, out in zip((hr, normed, recip), outs):
            moves.send(val.at[at], out.at[at])
    bias = jnp.concatenate([ub[k : k + 1] for k in range(ub.shape[0])], 1)
    for c in range(wu.shape[1] // CHUNK):
        cs = pl.ds(c * CHUNK, CHUNK)
        chunk_waits(up_waits, c, half)
        u = dot_nn(hr[...], wu[:, cs]) + bias[:, c * CHUNK : (c + 1) * CHUNK]
        phi = 0.5 * (1.0 + lax.erf(u * math.sqrt(0.5)))
        g[:, cs] = (u * phi).astype(bf16)
        gp[:, cs] = (phi + u * (jnp.exp(-0.5 * u * u) * (1.0 / math.sqrt(2 * math.pi)))).astype(bf16)
        moves.send(gp.at[:, cs], outs[4].at[:, cs])
    moves.send(g, outs[3])
    for copies in down_waits:
        wait_all(copies)
    for c in range(wd.shape[1] // CHUNK):
        cs = pl.ds(c * CHUNK, CHUNK)
        f_low[:, cs] = dot_nn(g[...], wd[:, cs]).astype(bf16)
        moves.send(f_low.at[:, cs], outs[5].at[:, cs])
    moves.finish()


def ff_fwd(layer, state, a_mine, a_theirs, norms, ub, own_up, own_down, moved):
    seq, width = state.shape
    n_t, half = ub.shape
    outs = [
        shape((seq, width), bf16),
        shape((seq, width), f32),
        shape((seq, 1), f32),
        shape((seq, n_t * half), bf16),
        shape((seq, n_t * half), bf16),
        shape((seq, width), bf16),
    ]
    return pl.pallas_call(
        functools.partial(ff_fwd_kernel, layer),
        out_shape=outs,
        in_specs=[ANY] * 3 + [VMEM] * 4 + [ANY] * 7,
        out_specs=[HBM] * len(outs),
        scratch_shapes=[pltpu.VMEM(v.shape, v.dtype) for v in (state, a_mine, a_theirs)]
        + [pltpu.VMEM(v.shape, v.dtype) for v in outs]
        + [
            pltpu.VMEM((width, n_t * half), bf16),
            pltpu.VMEM((n_t * half, width), bf16),
            pltpu.SemaphoreType.DMA((MOVES,)),
        ],
        compiler_params=params(56),
        cost_estimate=cost(8),
        name="ff_fwd",
    )(state, a_mine, a_theirs, *norms, ub, own_up, own_down, *moved)


def ff_bwd_kernel(last, layer, *refs):
    rows_in, refs = refs[:5], refs[5:]
    ob, gain, shift, gp_in, own_up, own_down = refs[:6]
    moved, refs = refs[6:11], refs[11:]
    n_out = 7 if last else 6
    outs, refs = refs[:n_out], refs[n_out:]
    bufs, gp, refs = refs[:5], refs[5], refs[6:]
    vals, refs = refs[:n_out], refs[n_out:]
    wu, wd, sems = refs
    dz2, dzr2, du, dh_low, small, ub_sum = vals[-6:]
    core, _, _ = here()
    seq = dz2.shape[0]
    moves = Moves(sems)
    rows = 256
    tiles = [pl.ds(i * rows, rows) for i in range(seq // rows)]
    if last:
        row_waits = [[moves.start(src.at[at], dst.at[at]) for src, dst in zip(rows_in[:3], bufs)] for at in tiles]
        cot_waits = [moves.start(src, dst) for src, dst in zip(rows_in[3:], bufs[3:])]
    else:
        row_waits = [[moves.start(src.at[at], dst.at[at]) for src, dst in zip(rows_in, bufs)] for at in tiles]
    up, down, n_t = fetch_ff(moves, layer, own_up, own_down, moved, wu, wd)
    half = wu.shape[1] // n_t
    down_waits, gp_waits = [], []
    for k in range(n_t):
        down_waits.append(down(k))
        for c in range(gp.shape[1] // CHUNK):
            if k * half <= c * CHUNK < (k + 1) * half:
                cs = pl.ds(c * CHUNK, CHUNK)
                gp_waits.append(moves.start(gp_in.at[:, cs], gp.at[:, cs]))
    up_waits = [up(k) for k in range(n_t)]
    small[...] = jnp.zeros_like(small)
    for i, at in enumerate(tiles):
        wait_all(row_waits[i])
        if last:
            h_in, f_mine, f_theirs, c_mine, c_theirs = bufs
            h = h_in[at] * gain[layer, 0:1] + shift[layer, 0:1]
            z = h + (f_mine[at].astype(f32) + f_theirs[at].astype(f32)) + ob[layer, 1:2]
            new, n, r = norm_forward(z, gain[layer, 1:2], shift[layer, 1:2])
            vals[0][at] = new.astype(bf16)
            if i == 0:
                wait_all(cot_waits)
            dy = jnp.where(core == i, c_mine[...], c_theirs[...]).astype(f32)
        else:
            dz_in, x_mine, x_theirs, normed, recip = bufs
            dy = dz_in[at] + (x_mine[at].astype(f32) + x_theirs[at].astype(f32))
            n, r = normed[at], recip[at]
        dz = norm_backward(dy, n, r, gain[layer, 1:2])
        dz2[at] = dz
        low = dz.astype(bf16)
        dzr2[at] = low
        if last:
            moves.send(vals[0].at[at], outs[0].at[at])
        moves.send(dz2.at[at], outs[-6].at[at])
        moves.send(dzr2.at[at], outs[-5].at[at])
        small[0:1] += jnp.sum(dy * n, 0, keepdims=True)
        small[1:2] += jnp.sum(dy, 0, keepdims=True)
        small[2:3] += jnp.sum(dz, 0, keepdims=True)
    for c in range(wd.shape[0] // CHUNK):
        cs = pl.ds(c * CHUNK, CHUNK)
        chunk_waits(down_waits, c, half)
        gp_waits[c].wait()
        back = (dot_nt(dzr2[...], wd[cs]) * gp[:, cs].astype(f32)).astype(bf16)
        du[:, cs] = back
        ub_sum[:, cs] = jnp.sum(back.astype(f32), 0, keepdims=True)
        moves.send(du.at[:, cs], outs[-4].at[:, cs])
    moves.send(small, outs[-2])
    moves.send(ub_sum, outs[-1])
    for copies in up_waits:
        wait_all(copies)
    for c in range(wu.shape[0] // CHUNK):
        cs = pl.ds(c * CHUNK, CHUNK)
        dh_low[:, cs] = dot_nt(du[...], wu[cs]).astype(bf16)
        moves.send(dh_low.at[:, cs], outs[-3].at[:, cs])
    moves.finish()


def ff_bwd(layer, rows_in, norms, gp, own_up, own_down, moved, last):
    width = own_up.shape[1]
    seq, wide = gp.shape
    outs = [
        shape((seq, width), f32),
        shape((seq, width), bf16),
        shape((seq, wide), bf16),
        shape((seq, width), bf16),
        shape((8, width), f32),
        shape((1, wide), f32),
    ]
    if last:
        outs = [shape((seq, width), bf16)] + outs
    return pl.pallas_call(
        functools.partial(ff_bwd_kernel, last, layer),
        out_shape=outs,
        in_specs=[ANY] * 5 + [VMEM] * 3 + [ANY] * 8,
        out_specs=[HBM] * len(outs),
        scratch_shapes=[pltpu.VMEM(v.shape, v.dtype) for v in (*rows_in, gp)]
        + [pltpu.VMEM(v.shape, v.dtype) for v in outs]
        + [
            pltpu.VMEM((width, wide), bf16),
            pltpu.VMEM((wide, width), bf16),
            pltpu.SemaphoreType.DMA((MOVES,)),
        ],
        compiler_params=params(56),
        cost_estimate=cost(9),
        name="ff_bwd",
    )(*rows_in, *norms, gp, own_up, own_down, *moved)


SEND = ((2, 3), (1, 3))
NEXT = (1, 2)


def ff_dw_kernel(z_first, *refs):
    ins, outs = refs[:4], refs[4:-8]
    g, du, hr, dzr2, su, sd, in_sems, sems = refs[-8:]
    _, place, z = here()
    n_t, width, half = su.shape
    part, rows = width // 4, half // 4

    def target(s, j):
        send, nxt, keep = outs[3 * s : 3 * s + 3]
        if j in SEND[s]:
            return send.at[SEND[s].index(j)]
        return nxt if j == NEXT[s] else keep

    def quarter(k):
        return lax.rem(z + n_t - k, n_t)

    copies = []

    def start(src, dst):
        copies.append(pltpu.make_async_copy(src, dst, sems.at[len(copies)]))
        copies[-1].start()

    moves = Moves(in_sems)
    pair = 2 * half
    hr_wait = moves.start(ins[2], hr)
    du_waits = [moves.start(ins[1].at[:, pl.ds(m * pair, pair)], du.at[:, pl.ds(m * pair, pair)]) for m in range(n_t // 2)]
    dzr2_wait = moves.start(ins[3], dzr2)
    g_waits = [moves.start(ins[0].at[:, pl.ds(m * pair, pair)], g.at[:, pl.ds(m * pair, pair)]) for m in range(n_t // 2)]
    hr_wait.wait()
    for m in range(n_t // 2):
        du_waits[m].wait()
        for c in range(width // CHUNK):
            at = pl.ds(c * CHUNK, CHUNK)
            got = dot_tn(hr[:, at], du[:, m * pair : (m + 1) * pair]).astype(bf16)
            for k in (2 * m, 2 * m + 1):
                su[k, at] = got[:, (k - 2 * m) * half : (k - 2 * m + 1) * half]
        if z_first:
            for k in (2 * m, 2 * m + 1):
                for p in range(4):
                    start(su.at[k, pl.ds(p * part, part)], outs[0].at[quarter(k), p, 0])
    if not z_first:
        for j in range(4):
            at = pl.ds(pl.multiple_of((j ^ place) * part, part), part)
            start(su.at[:, at], target(0, j))
    dzr2_wait.wait()
    for m in range(n_t // 2):
        g_waits[m].wait()
        for c in range(pair // CHUNK):
            at = pl.ds(m * pair + c * CHUNK, CHUNK)
            sd[at] = dot_tn(g[:, at], dzr2[...]).astype(bf16)
        if z_first:
            for k in (2 * m, 2 * m + 1):
                for p in range(4):
                    for n in range(2):
                        start(
                            sd.at[pl.ds(k * half + p * rows, rows), pl.ds(n * half, half)],
                            outs[0].at[quarter(k), p, 1, pl.ds(n * rows, rows)],
                        )
    if not z_first:
        for j in range(4):
            for k in range(n_t):
                at = pl.ds(pl.multiple_of(k * half + (j ^ place) * rows, rows), rows)
                for n in range(2):
                    start(sd.at[at, pl.ds(n * half, half)], target(1, j).at[k, pl.ds(n * rows, rows)])
    for c in copies:
        c.wait()


def ff_dw(g, du, hr, dzr2, z_first):
    width = hr.shape[1]
    half = width // 2
    n_t = g.shape[1] // half
    one = (n_t, width // 4, half)
    if z_first:
        outs = [shape((n_t, 4, 2, width // 4, half), bf16)]
    else:
        outs = [shape((2,) + one, bf16), shape(one, bf16), shape(one, bf16)] * 2
    return pl.pallas_call(
        functools.partial(ff_dw_kernel, z_first),
        out_shape=outs,
        in_specs=[ANY] * 4,
        out_specs=[HBM] * len(outs),
        scratch_shapes=[pltpu.VMEM(v.shape, v.dtype) for v in (g, du, hr, dzr2)]
        + [
            pltpu.VMEM((n_t, width, half), bf16),
            pltpu.VMEM((n_t * half, width), bf16),
            pltpu.SemaphoreType.DMA((2 + 2 * n_t,)),
            pltpu.SemaphoreType.DMA((12 * n_t,)),
        ],
        compiler_params=params(56),
        cost_estimate=cost(5),
        name="ff_dw",
    )(g, du, hr, dzr2)


def attn_bwd_kernel(layer, *refs):
    rows_in, refs = refs[:4], refs[4:]
    recip, gain, qkv_in, lse_t, o, mask_in, own_qkv, own_out = refs[:8]
    a_refs, b_refs, refs = refs[8:12], refs[12:16], refs[16:]
    outs, refs = refs[:5], refs[5:]
    bufs, refs = refs[:4], refs[4:]
    dz1, dzr1, d4, dx_low, small, qkv, mask, w, do, sems = refs
    dz2, h_mine, h_theirs, normed = bufs
    seq, width = dz1.shape
    moves = Moves(sems)
    half = seq // 2
    row_waits = []
    for i in range(2):
        at = pl.ds(i * half, half)
        row_waits.append([moves.start(src.at[at], dst.at[at]) for src, dst in zip(rows_in, bufs)])
    weight_waits = fetch_attn(moves, layer, own_qkv, own_out, a_refs, b_refs, w)
    qkv_wait = moves.start(qkv_in, qkv)
    mask_wait = moves.start(mask_in, mask)
    o_wait = moves.start(o, d4.at[3])
    small[...] = jnp.zeros_like(small)
    for i in range(seq // 128):
        if i * 128 % half == 0:
            wait_all(row_waits[i * 128 // half])
        at = pl.ds(i * 128, 128)
        dh = dz2[at] + (h_mine[at].astype(f32) + h_theirs[at].astype(f32))
        n = normed[at]
        dz = norm_backward(dh, n, recip[at], gain[layer, 0:1])
        dz1[at] = dz
        dzr1[at] = dz.astype(bf16)
        small[0:1] += jnp.sum(dh * n, 0, keepdims=True)
        small[1:2] += jnp.sum(dh, 0, keepdims=True)
        small[2:3] += jnp.sum(dz, 0, keepdims=True)
    moves.send(dz1, outs[0])
    moves.send(dzr1, outs[1])
    wait_all(weight_waits)
    rows = 256
    for i in range(seq // rows):
        at = pl.ds(i * rows, rows)
        do[at] = dot_nt(dzr1[at], w[3]).astype(bf16)
    qkv_wait.wait()
    mask_wait.wait()
    pairs = qkv.shape[2] // 128
    tile = 256
    scale = 1.0 / math.sqrt(HEAD_DIM)
    for g in range(pairs):
        cs = pl.ds(g * 128, 128)
        k2 = qkv[1, :, cs] * jnp.asarray(scale, bf16)
        v2 = qkv[2, :, cs]
        dv = dk = None
        for i in range(seq // tile):
            at = pl.ds(i * tile, tile)
            q2 = qkv[0, at, cs]
            do2 = do[at, cs]
            bias = mask[:, at]
            dq = None
            for hh in range(2):
                all_half = lane_half(seq, hh)
                tile_half = lane_half(tile, hh)
                km = jnp.where(all_half, k2, jnp.zeros_like(k2))
                vm = jnp.where(all_half, v2, jnp.zeros_like(v2))
                qm = jnp.where(tile_half, q2, jnp.zeros_like(q2))
                dom = jnp.where(tile_half, do2, jnp.zeros_like(do2))
                head = 2 * g + hh
                s = dot_nt(km, q2) + bias
                pr = jnp.exp(s - lse_t[head : head + 1, at])
                dp = dot_nt(vm, do2)
                delta = jnp.sum(pr * dp, 0, keepdims=True)
                ds = (pr * (dp - delta)).astype(bf16)
                got_v = dot_nn(pr.astype(bf16), dom)
                got_k = dot_nn(ds, qm)
                got_q = dot_nn(jnp.transpose(km), ds)
                dv = got_v if dv is None else dv + got_v
                dk = got_k if dk is None else dk + got_k
                dq = got_q if dq is None else dq + got_q
            dqr = jnp.transpose(dq)
            d4[0, at, cs] = dqr.astype(bf16)
        d4[1, :, cs] = (dk * scale).astype(bf16)
        d4[2, :, cs] = dv.astype(bf16)
    o_wait.wait()
    moves.send(d4, outs[2])
    wide = d4.shape[2]
    small[3:4, 0:wide] = jnp.sum(d4[0].astype(f32), 0, keepdims=True)
    small[3:4, wide : 2 * wide] = jnp.sum(d4[2].astype(f32), 0, keepdims=True)
    for i in range(seq // rows):
        at = pl.ds(i * rows, rows)
        acc = dot_nn(d4[0, at], w[0]) + dot_nn(d4[1, at], w[1]) + dot_nn(d4[2, at], w[2])
        dx_low[at] = acc.astype(bf16)
        moves.send(dx_low.at[at], outs[3].at[at])
    moves.send(small, outs[4])
    moves.finish()


def attn_bwd(layer, dz2, h_mine, h_theirs, normed, recip, gain, qkv, lse_t, o, mask, own_qkv, own_out, a_refs, b_refs):
    seq, width = dz2.shape
    wide = qkv.shape[2]
    outs = [
        shape((seq, width), f32),
        shape((seq, width), bf16),
        shape((4, seq, wide), bf16),
        shape((seq, width), bf16),
        shape((8, width), f32),
    ]
    rows_in = (dz2, h_mine, h_theirs, normed)
    return pl.pallas_call(
        functools.partial(attn_bwd_kernel, layer),
        out_shape=outs,
        in_specs=[ANY] * 4 + [VMEM] * 2 + [ANY, VMEM] + [ANY] * 12,
        out_specs=[HBM] * 5,
        scratch_shapes=[pltpu.VMEM(v.shape, v.dtype) for v in (*rows_in, *outs, qkv, mask)]
        + [
            pltpu.VMEM((4, wide, width), bf16),
            pltpu.VMEM((seq, wide), bf16),
            pltpu.SemaphoreType.DMA((MOVES,)),
        ],
        compiler_params=params(56),
        cost_estimate=cost(12),
        name="attn_bwd",
    )(*rows_in, recip, gain, qkv, lse_t, o, mask, own_qkv, own_out, *a_refs, *b_refs)


def attn_dw_kernel(*refs):
    ins, outs = refs[:3], refs[3:5]
    d4, right, full, sems = refs[5:]
    core, place, _ = here()
    cols = d4.shape[2] // SLOTS
    count, half = outs[0].shape[3:]
    moves = Moves(sems)
    waits = [moves.start(ins[1], right.at[0]), moves.start(ins[2], right.at[1])]
    d4_waits = [moves.start(ins[0].at[j ^ place], d4.at[j ^ place]) for j in range(4)]
    wait_all(waits)
    for j in range(4):
        t = j ^ place
        d4_waits[j].wait()
        full[j] = dot_tn(d4[t], right[t // 3]).astype(bf16)
        for s in range(SLOTS):
            for out, c in zip(outs, (core, 1 - core)):
                at = pl.ds(pl.multiple_of(s * cols + c * count, count), count)
                for n in range(2):
                    moves.send(full.at[j, at, pl.ds(n * half, half)], out.at[s, j, n])
    moves.finish()


def attn_dw(d4, xr, dzr1):
    wide, width = d4.shape[2], xr.shape[1]
    out = shape((SLOTS, 4, 2, wide // 4, width // 2), bf16)
    return pl.pallas_call(
        attn_dw_kernel,
        out_shape=[out, out],
        in_specs=[ANY] * 3,
        out_specs=[HBM] * 2,
        scratch_shapes=[
            pltpu.VMEM(d4.shape, bf16),
            pltpu.VMEM((2,) + xr.shape, bf16),
            pltpu.VMEM((4, wide, width), bf16),
            pltpu.SemaphoreType.DMA((MOVES,)),
        ],
        compiler_params=params(56),
        cost_estimate=cost(3.5),
        name="attn_dw",
    )(d4, xr, dzr1)


def arrange_kernel(mine, theirs, *outs):
    first = here()[0] == 0
    for ref, same in ((mine, first), (theirs, jnp.logical_not(first))):
        for s in range(SLOTS):
            k = jnp.where(same, s, 3 - s)
            for n in range(2):
                send, nxt, keep = outs[3 * n : 3 * n + 3]
                for j in range(4):
                    val = ref[s, j, n]
                    if j in SEND[n]:
                        send[SEND[n].index(j), k] = val
                    elif j == NEXT[n]:
                        nxt[k] = val
                    else:
                        keep[k] = val


def low_sum(*parts):
    total = parts[0].astype(f32)
    for v in parts[1:]:
        total = total + v.astype(f32)
    return total.astype(bf16)


def small_call(kernel, outs, us, name, *ins):
    n, m = len(ins), len(outs)

    def body(*refs):
        bufs, sems = refs[n + m : -1], refs[-1]
        copies = [pltpu.make_async_copy(src, dst, sems.at[i]) for i, (src, dst) in enumerate(zip(refs[:n], bufs))]
        for c in copies:
            c.start()
        for c in copies:
            c.wait()
        kernel(*bufs, *refs[n : n + m])

    return pl.pallas_call(
        body,
        out_shape=outs,
        in_specs=[ANY] * n,
        out_specs=[VMEM] * m,
        scratch_shapes=[pltpu.VMEM(v.shape, v.dtype) for v in ins] + [pltpu.SemaphoreType.DMA((n,))],
        compiler_params=params(16),
        cost_estimate=cost(us * 0.01),
        name=name,
    )(*ins)


def second_kernel(nxt_a, got_a, nxt_b, got_b, out_a, out_b):
    out_a[...] = low_sum(nxt_a[...], got_a[1])
    out_b[...] = low_sum(nxt_b[...], got_b[1])


def third_kernel(*refs):
    out = refs[-1]
    n_t = out.shape[0]
    z = here()[2]
    row = 0
    for c in range(len(refs) // 6):
        ins = refs[6 * c : 6 * c + 6]
        rows = ins[0].shape[1]
        for n in range(2):
            keep, got, more = ins[3 * n : 3 * n + 3]
            for k in range(n_t):
                q = lax.rem(z + n_t - k, n_t)
                out[q, n, row : row + rows] = low_sum(keep[k], got[0, k], more[k])
        row += rows


def merge_kernel(keep_a, got_a, more_a, keep_b, got_b, more_b, attn, out):
    rows = keep_a.shape[1]
    out[0, :rows] = low_sum(keep_a[0], got_a[0, 0], more_a[0])
    out[1, :rows] = low_sum(keep_b[0], got_b[0, 0], more_b[0])
    out[:, rows:] = attn[...]


def split_kernel(every, *outs):
    _, place, _ = here()
    for s in range(SLOTS):
        send, nxt, keep = outs[3 * s : 3 * s + 3]
        for j in range(4):
            val = every[j ^ place, s]
            if j in SEND[s]:
                send[SEND[s].index(j), 0] = val
            elif j == NEXT[s]:
                nxt[0] = val
            else:
                keep[0] = val


def pick_kernel(every, out, ub):
    n_t, rows = every.shape[0], out.shape[2]
    z = here()[2]
    for k in range(n_t):
        q = lax.rem(z + n_t - k, n_t)
        ub[k : k + 1] = jnp.sum(every[q, 2 * rows : 2 * rows + 3].astype(f32), 0, keepdims=True)
        if k:
            for n in range(2):
                out[n, k - 1] = every[q, n * rows : (n + 1) * rows]


def pack_kernel(*refs):
    out = refs[-1]
    layers = (len(refs) - 1) // 3
    small1, small2, ub = refs[:layers], refs[layers : 2 * layers], refs[2 * layers : 3 * layers]
    core, _, z = here()
    half = out.shape[1] // 2
    n_t = ub[0].shape[1] // half
    cols = half // 2
    once = jnp.where(core == 0, 1.0, 0.0).astype(f32)
    for l in range(layers):
        out[6 * l : 6 * l + 3] = small1[l][0:3] * once
        out[6 * l + 3 : 6 * l + 6] = small2[l][0:3] * once
    none = jnp.zeros((1, half), f32)
    for l in range(layers):
        for q in range(n_t):
            row = none
            for k in range(n_t):
                row = jnp.where(lax.rem(z + n_t - k, n_t) == q, ub[l][:, k * half : (k + 1) * half], row)
            left = jnp.where(core == 0, row, none)
            out[6 * layers + n_t * l + q : 6 * layers + n_t * l + q + 1] = jnp.concatenate([left, row - left], 1)
    slot_k = (jnp.where(core == 0, 0, 3), jnp.where(core == 0, 1, 2))
    none = jnp.zeros((1, cols), f32)
    for q in range(n_t):
        parts = []
        for l in range(layers):
            for i in range(2):
                row = none
                for s in range(SLOTS):
                    at = i * half + s * cols
                    here_q = lax.rem(z + n_t - slot_k[s], n_t) == q
                    row = jnp.where(here_q, small1[l][3:4, at : at + cols], row)
                parts.append(row)
        at = (6 + n_t) * layers + q
        out[at : at + 1] = jnp.concatenate(parts, 1)


def unpack_kernel(flat, gain, shift, bias, up, qv):
    layers, _, cols = qv.shape
    n_t = (flat.shape[0] - 6 * layers) // (layers + 1)
    z = here()[2]

    def own(first):
        row = flat[first : first + 1]
        for q in range(1, n_t):
            row = jnp.where(z == q, flat[first + q : first + q + 1], row)
        return row

    row = own((6 + n_t) * layers)
    for l in range(layers):
        for n in range(2):
            at = 6 * l + 3 * n
            gain[l, n : n + 1] = flat[at : at + 1]
            shift[l, n : n + 1] = flat[at + 1 : at + 2]
            bias[l, n : n + 1] = flat[at + 2 : at + 3]
            qv[l, n : n + 1] = row[:, (2 * l + n) * cols : (2 * l + n + 1) * cols]
        up[l : l + 1] = own(6 * layers + n_t * l)


def out_kernel(layer, n_alias, *refs):
    mine, theirs = refs[:4], refs[4:8]
    up, down, qkv, out, wide, sems = refs[8 + n_alias :]
    core, place, _ = here()
    part, half, cols = up.shape[1] // 4, up.shape[2] // 2, out.shape[1]
    rows, count = half // 4, cols // 2
    copies = []

    def start(src, dst):
        copies.append(pltpu.make_async_copy(src, dst, sems.at[len(copies)]))
        copies[-1].start()

    for n, (pieces, c) in enumerate(((mine, core), (theirs, 1 - core))):
        off = pl.multiple_of(c * half, half)
        for j, ref in enumerate(pieces):
            p = j ^ place
            buf = wide.at[n, j]
            buf[...] = ref[...].astype(f32)
            start(buf.at[0, pl.ds(0, part)], up.at[layer, pl.ds(pl.multiple_of(p * part, part), part), pl.ds(off, half)])
            for m in range(2):
                lanes = pl.ds(m * half, half)
                at = pl.ds(pl.multiple_of(c * half + p * rows, rows), rows)
                start(buf.at[1, pl.ds(m * rows, rows)], down.at[layer, at, lanes])
                src, sem = buf.at[m, pl.ds(part, count)], sems.at[len(copies)]
                at = pl.ds(pl.multiple_of(c * count, count), count)
                to_qkv = pltpu.make_async_copy(src, qkv.at[layer, jnp.minimum(p, 2), at, lanes], sem)
                to_out = pltpu.make_async_copy(src, out.at[layer, at, lanes], sem)

                @pl.when(p < 3)
                def _(to_qkv=to_qkv):
                    to_qkv.start()

                @pl.when(p == 3)
                def _(to_out=to_out):
                    to_out.start()

                copies.append(to_out)
    for c in copies:
        c.wait()


def outputs(layer, dims, mine, theirs, before):
    before = list(before or [])
    n = len(mine) + len(theirs)
    return pl.pallas_call(
        functools.partial(out_kernel, layer, len(before)),
        out_shape=[shape(d, f32) for d in dims],
        in_specs=[VMEM] * n + [HBM] * len(before),
        out_specs=[HBM] * len(dims),
        scratch_shapes=[
            pltpu.VMEM((2, 4) + mine[0].shape, f32),
            pltpu.SemaphoreType.DMA((5 * n,)),
        ],
        input_output_aliases={n + i: i for i in range(len(before))},
        compiler_params=params(24),
        cost_estimate=cost(4),
        name="gradients_out",
    )(*mine, *theirs, *before)


def after(v, *others):
    return lax.optimization_barrier((v, *others))[0]


def local(
    block_input,
    w_qkv,
    qv_bias,
    w_out,
    out_bias,
    w_up,
    up_bias,
    w_down,
    norm_gain,
    norm_shift,
    segment_ids,
    slot_counts,
    cotangent,
):
    layers, width, _, cols = w_qkv.shape
    hidden = w_up.shape[2]
    seq = segment_ids.shape[1]
    n_dp, n_t = lax.axis_size("dp"), lax.axis_size("tensor")
    dp, z = lax.axis_index("dp"), lax.axis_index("tensor")
    core, place = dp & 1, (dp >> 1) & 3
    first = core == 0
    part, half = hidden // 4, hidden // 2
    norms_in = (out_bias, norm_gain, norm_shift)

    def send(v, axis, pairs, name):
        with jax.named_scope(name):
            return lax.ppermute(v, axis, pairs)

    def flip(v, bits, name, odd=False):
        return send(v, "dp", [(i, i ^ bits) for i in range(n_dp) if not odd or i & 1], name)

    def across(v, name):
        return flip(v, 1, name)

    def shift(v, by, name):
        pairs = []
        for i in range(n_dp):
            move = by[i & 1]
            if move:
                pairs += [(i * n_t + k, i * n_t + (k + move) % n_t) for k in range(n_t)]
        return send(v, ("dp", "tensor"), pairs, name)

    def swap(v, name):
        pairs = []
        for i in range(n_dp):
            for k in range(n_t):
                if (i & 1) != (k & 1):
                    pairs.append((i * n_t + k, (i ^ 1) * n_t + (k ^ 1)))
        moved = send(v, ("dp", "tensor"), pairs, name)
        return jnp.where(core == (z & 1), v, moved)

    own_qkv = jnp.transpose(w_qkv, (0, 2, 3, 1))
    own_bias = qv_bias.reshape(1, -1)

    def attn_over_z(piece, l):
        return shift(piece, (1, 2), f"attn{l}_z_b"), shift(piece, (0, 3), f"attn{l}_z_a")

    def attn_over_xy(b, a, l, *late):
        name = f"attn{l}_"
        bx = flip(b, 2, name + "b_x")
        by = flip(b, 4, name + "b_y")
        ay = flip(a, 4, name + "a_y", True)
        ax = flip(a, 2, name + "a_x", True)
        bd = flip(after(bx, *late), 4, name + "b_xy")
        ad = flip(after(ay, *late), 2, name + "a_yx", True)
        return (a, ax, ay, ad), (b, bx, by, bd)

    def ff_over_xy(own, l):
        x, y = flip(own, 2, f"ff{l}_x"), flip(own, 4, f"ff{l}_y")
        return own, x, y, flip(x[0], 4, f"ff{l}_xy"), flip(y[1], 2, f"ff{l}_yx")

    x_mine = swap(block_input, "x_swap")
    attn_piece, ff_piece, packed = prepare(own_qkv, w_out, w_up, w_down, up_bias, own_bias, segment_ids, slot_counts)
    mask, mask_t = masks(packed, across(packed, "seg"))
    x_theirs = across(x_mine, "x_across")

    def ff_over_z(l, *late):
        with jax.named_scope(f"ff{l}_z"):
            return lax.all_gather(after(ff_piece[l], *late), "tensor", axis=0)

    def take(every, l, *late):
        outs = [shape((2, n_t - 1, part, half), bf16), shape((n_t, half), f32)]
        own, ub = small_call(pick_kernel, outs, 1.5, "pick_quarters", after(every, *late))
        return ff_over_xy(own, l), ub

    attn0_z = attn_over_z(attn_piece[0], 0)
    ff0_z = ff_over_z(0, *attn0_z)
    attn0 = attn_over_xy(after(attn0_z[0], mask, x_mine), after(attn0_z[1], mask, x_mine), 0, x_theirs)
    attn1_z = attn_over_z(after(attn_piece[1], *attn0[0][:3], *attn0[1][:3]), 1)
    ff1_z = ff_over_z(1, *attn1_z)
    bias = (own_bias,) + attn0_z[::-1]

    rows_in = (x_mine, x_theirs)
    saved = []
    attn_w, ff_w, ubs = [attn0], [], []
    for l in range(layers):
        xr, n2, r2, qkv, lse_t, o, a_low = attn_fwd(l, rows_in, mask, bias, own_qkv, w_out, *attn_w[l])
        state = n2 if l else xr
        if l:
            saved[l - 1] += (n2, r2)
        else:
            ff0, ub = take(ff0_z, 0, xr)
            ff_w.append(ff0)
            ubs.append(ub)
            attn_w.append(attn_over_xy(after(attn1_z[0], ff0[1], ff0[2]), after(attn1_z[1], ff0[1], ff0[2]), 1))
        hr, n1, r1, g, gp, f_low = ff_fwd(
            l, state, a_low, across(a_low, f"a{l}"), norms_in, ubs[l], w_up, w_down, ff_w[l]
        )
        if l == 0:
            ff1, ub = take(ff1_z, 1, hr)
            ff_w.append(ff1)
            ubs.append(ub)
        saved.append((xr, qkv, lse_t, o, hr, n1, r1, g, gp))
        rows_in = (n1, f_low, across(f_low, f"f{l}")) + norms_in

    class Sums:
        def __init__(self, name):
            self.name = name

        def first(self, pieces):
            self.pieces = pieces
            self.got = (flip(pieces[0], 4, self.name + "_1a"), flip(pieces[3], 2, self.name + "_1b"))
            return self

        def second(self, *late):
            p, got = self.pieces, self.got
            nxt = after(p[1], *late)
            outs = [shape(nxt.shape, bf16)] * 2
            self.sec = small_call(second_kernel, outs, 1.2, "add_second", nxt, got[0], p[4], got[1])
            self.more = (flip(self.sec[0], 2, self.name + "_2a"), flip(self.sec[1], 4, self.name + "_2b"))
            return self

        def parts(self):
            p, got, more = self.pieces, self.got, self.more
            return [p[2], got[0], more[0], p[5], got[1], more[1]]

    def over_z(every):
        with jax.named_scope("sums_z"):
            return lax.psum_scatter(every, "tensor", scatter_dimension=0)

    def third(chunks, *late):
        ins = [v for c in chunks for v in c.parts()]
        rows = sum(c.pieces[2].shape[1] for c in chunks)
        outs = [shape((n_t, 2, rows, half), bf16)]
        (every,) = small_call(third_kernel, outs, 1.5, "add_third", after(ins[0], *late), *ins[1:])
        return every, over_z(every)

    def attn_first(name, mine, theirs):
        one = (n_t, cols // 2, half)
        outs = [shape((2,) + one, bf16), shape(one, bf16), shape(one, bf16)] * 2
        return Sums(name).first(small_call(arrange_kernel, outs, 1.5, "arrange", mine, theirs))

    def split(total, *late):
        one = (1, part, half)
        outs = [shape((2,) + one, bf16), shape(one, bf16), shape(one, bf16)] * 2
        return Sums("gf1").first(small_call(split_kernel, outs, 1.5, "split_pieces", after(total, *late)))

    def spread(total, name):
        bits = 8
        while bits < n_dp:
            total = low_sum(total, flip(total, bits, name + "_rest"))
            bits *= 2
        mine = [total] + [flip(total, bits, f"{name}_c{bits}") for bits in (2, 4, 6)]
        return mine, [across(v, f"{name}_cc{n}") for n, v in enumerate(mine)]

    def finish(l, mine, theirs, before, *late):
        dims = [(layers, width, hidden), (layers, hidden, width), (layers, 3, cols, width), (layers, cols, width)]
        return outputs(l, dims, [after(mine[0], *late)] + mine[1:], theirs, before)

    a1 = None
    smalls = []
    for l in reversed(range(layers)):
        last = l == layers - 1
        xr, qkv, lse_t, o, hr, n1, r1, g, gp = saved[l][:9]
        if last:
            c_mine = swap(cotangent, "cot_swap")
            ff_rows = rows_in[:3] + (c_mine, across(c_mine, "cot_across"))
        else:
            ff_rows = (dz1, dx_low, across(dx_low, f"dx{l}")) + saved[l][9:]
        got = ff_bwd(l, ff_rows, norms_in, gp, w_up, w_down, ff_w[l], last)
        if last:
            out_half = lax.dynamic_slice_in_dim(got[0], core * (seq // 2), seq // 2, 0)
            got = got[1:]
        dz2, dzr2, du, dh_low, small2, ub_sum = got
        if a1:
            a1.second(dzr2)
            dzr2 = after(dzr2, *a1.sec)
        ff_pieces = ff_dw(g, du, hr, dzr2, last)
        if last:
            f1_total = over_z(ff_pieces[0])
        else:
            first_out = [after(ff_pieces[0], *a1.more), *ff_pieces[1:3], after(ff_pieces[3], *a1.more), *ff_pieces[4:]]
            f0 = Sums("gf0").first(first_out)
        dh_theirs = across(dh_low, f"dh{l}")
        dz2 = after(dz2, ff_pieces[0])
        if a1:
            a1_every, a1_total = third([a1])
            dz2 = after(dz2, a1_every)
        dz1, dzr1, d4, dx_low, small1 = attn_bwd(
            l, dz2, dh_low, dh_theirs, n1, r1, norm_gain, qkv, lse_t, o, mask_t, own_qkv, w_out, *attn_w[l]
        )
        at_pieces = attn_dw(d4, xr, dzr1)
        at_theirs = across(at_pieces[1], f"ga{l}_core")
        if last:
            a1 = attn_first("ga1", at_pieces[0], at_theirs)
            dz1 = after(dz1, a1.pieces[0])
        smalls.append((small1, small2, ub_sum))
    smalls = smalls[::-1]

    def more_flat(flat, axis, bits, *late):
        n = lax.axis_size(axis)
        return flat + send(after(flat, *late), axis, [(i, i ^ bits) for i in range(n)], f"flat_{axis}{bits}")

    n_rows = (6 + n_t) * layers + n_t
    (flat,) = small_call(
        pack_kernel,
        [shape((n_rows, width), f32)],
        1.5,
        "pack_small",
        *[g[0] for g in smalls],
        *[g[1] for g in smalls],
        *[g[2] for g in smalls],
    )
    f0.second(at_pieces[0])
    a0 = attn_first("ga0", after(at_pieces[0], *f0.sec), at_theirs)
    flat = more_flat(flat, "dp", 1, a0.pieces[0])
    flat = more_flat(flat, "tensor", 1)
    a0.second(flat)
    flat = more_flat(flat, "tensor", 2, *a0.sec)
    l0_every, l0_total = third([f0, a0], flat)
    f1 = split(f1_total, l0_every)
    flat = more_flat(flat, "dp", 2, f1.pieces[0])
    f1.second(flat)
    flat = more_flat(flat, "dp", 4, *f1.sec)
    bits = 8
    while bits < n_dp:
        flat = more_flat(flat, "dp", bits)
        bits *= 2
    ins = f1.parts()
    ins[0] = after(ins[0], flat)
    (l1_total,) = small_call(merge_kernel, [shape((2, part + cols // 2, half), bf16)], 1.5, "merge", *ins, a1_total)
    l1 = spread(l1_total, "l1")
    dx = dz1 + (dx_low.astype(f32) + across(after(dx_low, l1_total), "dx_last").astype(f32))
    input_grad = swap(lax.dynamic_slice_in_dim(dx, core * (seq // 2), seq // 2, 0), "grad_swap")
    mixed = swap(after(out_half, l1_total), "mixed_swap")
    l0 = spread(after(l0_total, *l1[0]), "l0")
    grads = finish(1, *l1, None, l0_total, input_grad, mixed)
    grads = finish(0, *l0, grads)
    grad_gain, grad_shift, grad_out_bias, grad_up_bias, grad_qv_bias = small_call(
        unpack_kernel,
        [shape((layers, 2, width), f32)] * 3 + [shape((layers, hidden), f32), shape((layers, 2, cols), f32)],
        1.5,
        "unpack_small",
        flat,
    )
    return (
        mixed,
        input_grad,
        jnp.transpose(grads[2], (0, 3, 1, 2)),
        grad_qv_bias,
        grads[3],
        grad_out_bias,
        grads[0],
        grad_up_bias,
        grads[1],
        grad_gain,
        grad_shift,
    )


def solution(mesh):
    placed = (
        P(("dp", "tensor"), None),
        P(None, None, None, "tensor"),
        P(None, None, "tensor"),
        P(None, "tensor", None),
        P(),
        P(None, None, "tensor"),
        P(None, "tensor"),
        P(None, "tensor", None),
        P(),
        P(),
        P("dp", None),
        P("dp"),
        P(("dp", "tensor"), None),
    )
    return jax.shard_map(
        local,
        mesh=mesh,
        in_specs=placed,
        out_specs=(
            P(("dp", "tensor"), None),
            P(("dp", "tensor"), None),
            P(None, None, None, "tensor"),
            P(None, None, "tensor"),
            P(None, "tensor", None),
            P(),
            P(None, None, "tensor"),
            P(None, "tensor"),
            P(None, "tensor", None),
            P(),
            P(),
        ),
        check_vma=False,
    )
```
